32 devices in a mesh: dom: 4 (over y, core), band: 8 (over z, x).
Axes of the slice: x: 2, y: 2, z: 4, core: 2. Of those that a mesh axis runs over, the one named last changes fastest.
Arguments:
- psi_in: float32 [4, 8, 20, 1600], P('dom', 'band'), may hold values from -6 to 6
- v_in: float32 [4, 40, 1600], P('dom'), may hold values from -3 to 3
- offsets: int32 [4, 3], replicated, may hold values from 0 to 32, as said below
Outputs:
- psi_out: float32 [4, 8, 20, 1600], P('dom', 'band')
The draws below stay inside these ranges and needn't reach their ends.
Inputs may be any that keep to these rules, and one draw needn't show every extreme that they name: `offsets`: row d is the first corner of domain d's core in the global grid: its first two entries are 0 or 32, its third a multiple of 32 below 32; the 4 rows are distinct, so the cores tile the grid.
All inputs are finite; a program needn't handle non-finite values.
Results may differ from the reference program's by a relative error of at most 0.0003.
Values sent between devices are 32-bit elements; how exact they have to be, the bound alone decides.
No kernel may reach another device: no remote copies, remote signals or barrier semaphores. Data moves between devices by JAX's collectives and lax.ppermute only.
A program may use at most 64 MiB of HBM per device.

```python
import math
import jax
import jax.numpy as jnp
from jax import lax

CORE = 32
BUF = 4
DEG = 8
NDOM = 4
BANDS = 4
SIDE = 40
SLAB = 20


def draw_offsets(key, part):
    order = jax.random.permutation(jax.random.fold_in(key, 17), jnp.arange(NDOM, dtype=jnp.int32))
    corner_x = order % 2 * CORE
    corner_y = order // 2 % 2 * CORE
    corner_z = order // 4 * CORE
    return jnp.stack([corner_x, corner_y, corner_z], 1).astype(jnp.int32)


def block_levels(stream_key, shape, split, smallest, top_value):
    def one(dim, blocks):
        heights = jax.random.uniform(jax.random.fold_in(jax.random.fold_in(stream_key, 6), dim), (blocks,), jnp.float32, smallest / len(split), top_value / len(split))
        return jnp.repeat(jnp.exp(heights), shape[dim] // blocks).reshape((-1,) + (1,) * (len(shape) - dim - 1))

    factor_of = one(*split[0])
    for cut in split[1:]:
        factor_of = factor_of * one(*cut)
    return factor_of


def normal_values(rng, extent, width, limit, split=(), kind=jnp.bfloat16):
    level = block_levels(rng, extent, split, -0.22, 0.18) if split else 1.0
    array = jax.random.normal(rng, extent, jnp.float32) * width * level
    return jnp.minimum(jnp.maximum(array, -limit), limit).astype(kind)


def setup_inputs(seed: int = 0) -> dict:
    keys = jax.random.split(jax.random.key(seed), 4)
    psi_in = normal_values(keys[0], (NDOM, 2 * BANDS, SLAB, SIDE * SIDE), 1.0, 6.0, ((0, 4), (1, 8)), jnp.float32)
    v_in = normal_values(keys[1], (NDOM, SIDE, SIDE * SIDE), 0.5, 3.0, ((0, 4),), jnp.float32)
    offsets = draw_offsets(jax.random.fold_in(keys[3], 71), 0)
    return dict(psi_in=psi_in, v_in=v_in, offsets=offsets)


CENTER = 3.0
HALF_WIDTH = 4.5
FOUR_PI = 4.0 * math.pi
EXCHANGE_COEF = -((3.0 / math.pi) ** (1.0 / 3.0))


def hamiltonian(values, potential):
    padded = jnp.pad(values, 1)
    beside_all = padded[2:, 1:-1, 1:-1] + padded[:-2, 1:-1, 1:-1]
    beside_all = beside_all + padded[1:-1, 2:, 1:-1] + padded[1:-1, :-2, 1:-1]
    beside_all = beside_all + padded[1:-1, 1:-1, 2:] + padded[1:-1, 1:-1, :-2]
    return 0.5 * (6.0 * values - beside_all) + potential * values


def shifted(values, potential):
    return (hamiltonian(values, potential) - CENTER * values) / HALF_WIDTH


def chebyshev(values, potential):
    previous = values
    current = shifted(values, potential)
    for order_idx in range(DEG - 1):
        following = 2.0 * shifted(current, potential) - previous
        previous, current = current, following
    return current


def reference(psi_in, v_in, offsets):
    side_len = CORE + 2 * BUF
    grid_x = 2 * CORE
    grid_z = CORE * NDOM // 4
    wavefunc = psi_in.reshape(NDOM, BANDS, side_len, side_len, side_len)
    potentials = v_in.reshape(NDOM, side_len, side_len, side_len)
    filter_all = jax.vmap(chebyshev, (0, None))

    def first_pass(domain_item):
        return filter_all(domain_item[0], domain_item[1])

    filtered = lax.map(first_pass, (wavefunc, potentials))
    cores = jnp.sum(filtered[:, :, BUF:BUF + CORE, BUF:BUF + CORE, BUF:BUF + CORE] ** 2, axis=1) / BANDS
    density = jnp.zeros((grid_x, grid_x, grid_z), jnp.float32)
    for dom_idx in range(NDOM):
        density = lax.dynamic_update_slice(density, cores[dom_idx], (offsets[dom_idx, 0], offsets[dom_idx, 1], offsets[dom_idx, 2]))
    spectrum = jnp.fft.fftn(density)
    modes_x = jnp.arange(grid_x)
    modes_z = jnp.arange(grid_z)
    eigen_x = 2.0 - 2.0 * jnp.cos(2.0 * math.pi * modes_x.astype(jnp.float32) / grid_x)
    eigen_z = 2.0 - 2.0 * jnp.cos(2.0 * math.pi * modes_z.astype(jnp.float32) / grid_z)
    eigen = eigen_x[:, None, None] + eigen_x[None, :, None] + eigen_z[None, None, :]
    zero_mode = (modes_x[:, None, None] == 0) & (modes_x[None, :, None] == 0) & (modes_z[None, None, :] == 0)
    factor = jnp.where(zero_mode, 0.0, FOUR_PI / jnp.where(zero_mode, 1.0, eigen))
    hartree = jnp.real(jnp.fft.ifftn(spectrum * factor)).astype(jnp.float32)

    def region(values, anchor):
        region_pos = jnp.arange(side_len, dtype=jnp.int32) - BUF
        index_x = ((anchor[0] + region_pos) % grid_x).astype(jnp.int32)
        index_y = ((anchor[1] + region_pos) % grid_x).astype(jnp.int32)
        index_z = ((anchor[2] + region_pos) % grid_z).astype(jnp.int32)
        return jnp.take(jnp.take(jnp.take(values, index_x, 0), index_y, 1), index_z, 2)

    def second_pass(domain_item):
        band_vals, potential, anchor = domain_item
        renewed = potential + region(hartree, anchor) + EXCHANGE_COEF * jnp.cbrt(region(density, anchor))
        return filter_all(band_vals, renewed)

    final = lax.map(second_pass, (filtered, potentials, offsets))
    return final.reshape(NDOM, 2 * BANDS, side_len // 2, side_len * side_len)
```

```python
import functools
import math

import jax
import jax.numpy as jnp
import numpy as np
from jax import lax
from jax.experimental import pallas as pl
from jax.experimental.pallas import tpu as pltpu
from jax.sharding import PartitionSpec as P

CORE = 32
BUF = 4
DEG = 8

HALF_WIDTH = 4.5
FOUR_PI = 4.0 * math.pi
EXCHANGE_COEF = -((3.0 / math.pi) ** (1.0 / 3.0))
precise = lax.Precision.HIGHEST


def swapped(value, axis, mask):
    pairs = [(source, source ^ mask) for source in range(lax.axis_size(axis))]
    return lax.ppermute(value, axis, pairs)


def wave_basis(length):
    cells = np.arange(length)
    rows, waves = [], []
    for wave in range(length // 2 + 1):
        angle = 2.0 * np.pi * ((wave * cells) % length) / length
        if wave in (0, length // 2):
            rows.append(np.cos(angle) / np.sqrt(length))
            waves.append(wave)
        else:
            rows.append(np.cos(angle) * np.sqrt(2.0 / length))
            rows.append(np.sin(angle) * np.sqrt(2.0 / length))
            waves += [wave, wave]
    return np.array(rows), np.array(waves)


def parity_basis():
    rows, waves = wave_basis(2 * CORE)
    return np.stack([rows[waves % 2 == 0], rows[waves % 2 == 1]]), np.stack(
        [waves[waves % 2 == 0], waves[waves % 2 == 1]]
    )


def eigenvalue(waves, length):
    return 2.0 - 2.0 * np.cos(2.0 * np.pi * waves / length)


def padded(length, unit):
    return -(-length // unit) * unit


def place(is_lower, own, halo, field_ref, half, side):
    cells = side * side
    field_ref[...] = jnp.zeros(field_ref.shape, jnp.float32)

    @pl.when(is_lower)
    def _():
        field_ref[0:half, 0:cells] = own
        field_ref[half : half + DEG, 0:cells] = halo

    @pl.when(jnp.logical_not(is_lower))
    def _():
        field_ref[0:DEG, 0:cells] = halo
        field_ref[DEG : DEG + half, 0:cells] = own


def filtered_field(field, scaled_potential, half, side):
    rows, lanes = field.shape
    row_id = lax.broadcasted_iota(jnp.int32, (rows, lanes), 0)
    lane_id = lax.broadcasted_iota(jnp.int32, (rows, lanes), 1)
    inside = (row_id < half + DEG) & (lane_id < side * side)
    weight = jnp.where(inside, 1.0 / HALF_WIDTH, 0.0)
    column = lane_id % side
    not_first = column != 0
    not_last = column != side - 1

    def beside(values):
        total = pltpu.roll(values, 1, 0) + pltpu.roll(values, rows - 1, 0)
        total = total + pltpu.roll(values, side, 1) + pltpu.roll(values, lanes - side, 1)
        total = total + jnp.where(not_first, pltpu.roll(values, 1, 1), 0.0)
        return total + jnp.where(not_last, pltpu.roll(values, lanes - 1, 1), 0.0)

    previous = field
    current = 0.5 * (scaled_potential * field - weight * beside(field))
    for _ in range(DEG - 1):
        following = scaled_potential * current - weight * beside(current) - previous
        previous, current = current, following
    return current


def own_rows(is_lower, values, half):
    return jnp.where(is_lower, values[0:half], values[DEG : DEG + half])


def first_kernel(bands, slab_ref, psi_ref, halo_ref, pot_ref, filt_ref, dens_ref, field_ref, coef_ref):
    half, cells = psi_ref.shape
    side = 2 * half
    is_lower = slab_ref[0] == 0
    place(is_lower, psi_ref[...], halo_ref[...], field_ref, half, side)
    coef_ref[...] = jnp.zeros(coef_ref.shape, jnp.float32)

    @pl.when(is_lower)
    def _():
        coef_ref[0 : half + DEG, 0:cells] = pot_ref[0 : half + DEG] * (2.0 / HALF_WIDTH)

    @pl.when(jnp.logical_not(is_lower))
    def _():
        coef_ref[0 : half + DEG, 0:cells] = pot_ref[half - DEG : side] * (2.0 / HALF_WIDTH)

    result = filtered_field(field_ref[...], coef_ref[...], half, side)
    filt_ref[...] = own_rows(is_lower, result, half)[:, 0:cells]
    slab = CORE // 2
    core_rows = jnp.where(is_lower, result[BUF : BUF + slab], result[DEG : DEG + slab])
    squares = core_rows * core_rows * (1.0 / bands)
    per_tile = 128 // CORE
    for tile in range(CORE // per_tile):
        pieces = []
        for line in range(tile * per_tile, (tile + 1) * per_tile):
            start = (line + BUF) * side + BUF
            pieces.append(squares[:, start : start + CORE])
        dens_ref[:, tile * 128 : (tile + 1) * 128] = jnp.concatenate(pieces, 1)


def second_kernel(slab_ref, filt_ref, halo_ref, pot_ref, out_ref, field_ref, coef_ref):
    half, cells = filt_ref.shape
    side = 2 * half
    is_lower = slab_ref[0] == 0
    place(is_lower, filt_ref[...], halo_ref[...], field_ref, half, side)
    coef_ref[...] = jnp.zeros(coef_ref.shape, jnp.float32)

    @pl.when(is_lower)
    def _():
        coef_ref[0 : half + DEG, 0:cells] = pot_ref[0 : half + DEG] * (2.0 / HALF_WIDTH)

    @pl.when(jnp.logical_not(is_lower))
    def _():
        coef_ref[0 : half + DEG, 0:cells] = pot_ref[half - DEG : side] * (2.0 / HALF_WIDTH)

    result = filtered_field(field_ref[...], coef_ref[...], half, side)
    out_ref[...] = own_rows(is_lower, result, half)[:, 0:cells]


def field_scratch(half):
    shape = (padded(half + DEG, 8), padded(4 * half * half, 128))
    return [pltpu.VMEM(shape, jnp.float32)] * 2


SMEM = pl.BlockSpec(memory_space=pltpu.SMEM)
VMEM = pl.BlockSpec(memory_space=pltpu.VMEM)
params = pltpu.CompilerParams(vmem_limit_bytes=40 * 1024 * 1024)


def local(psi_in, v_in, offsets):
    band_count = lax.axis_size("band")
    dom_count = lax.axis_size("dom")
    dom_idx = lax.axis_index("dom")
    slab_idx = lax.axis_index("band") % 2
    is_lower = slab_idx == 0
    slab_scalar = slab_idx.astype(jnp.int32).reshape(1)
    side = v_in.shape[1]
    half = side // 2
    cells = side * side
    bands = band_count // 2
    grid_z = CORE * dom_count // 4

    wavefunc = psi_in[0, 0]
    potential = v_in[0]

    def halo_of(rows):
        edge = jnp.where(is_lower, rows[half - DEG : half], rows[0:DEG])
        return swapped(edge, "band", 1)

    filt, dens = pl.pallas_call(
        functools.partial(first_kernel, bands),
        out_shape=(
            jax.ShapeDtypeStruct((half, cells), jnp.float32),
            jax.ShapeDtypeStruct((CORE // 2, CORE * CORE), jnp.float32),
        ),
        in_specs=[SMEM, VMEM, VMEM, VMEM],
        out_specs=(VMEM, VMEM),
        scratch_shapes=field_scratch(half),
        compiler_params=params,
    )(slab_scalar, wavefunc, halo_of(wavefunc), potential)

    mask = 2
    while mask < band_count:
        dens = dens + swapped(dens, "band", mask)
        mask *= 2
    filt_edge, dens = lax.optimization_barrier((filt, dens))
    halo = halo_of(filt_edge)
    beside = swapped(dens, "band", 1)
    cube = jnp.concatenate([jnp.where(is_lower, dens, beside), jnp.where(is_lower, beside, dens)], 0)
    cubes = cube[None]
    masks = [0]
    bit = dom_count // 2
    while bit:
        cubes = jnp.concatenate([cubes, swapped(cubes, "dom", bit)], 0)
        masks = masks + [one | bit for one in masks]
        bit //= 2

    anchor = lax.dynamic_slice_in_dim(offsets, dom_idx, 1, 0)[0]
    others = jnp.take(offsets, dom_idx ^ jnp.array(masks, jnp.int32), axis=0)
    shift = (others - anchor) // CORE
    shift = jnp.stack([shift[:, 0] % 2, shift[:, 1] % 2, shift[:, 2] % (grid_z // CORE)], 1)
    basis, waves = parity_basis()
    z_basis, z_waves = wave_basis(grid_z)
    parity = jnp.arange(2)
    sign_x = 1.0 - 2.0 * ((shift[:, 0:1] * parity) % 2).astype(jnp.float32)
    sign_y = 1.0 - 2.0 * ((shift[:, 1:2] * parity) % 2).astype(jnp.float32)
    z_tables = z_basis.T.reshape(grid_z // CORE, CORE, grid_z).astype(np.float32)
    into_z = jnp.take(jnp.asarray(z_tables), shift[:, 2], axis=0)
    into_z = sign_x[:, :, None, None, None] * sign_y[:, None, :, None, None] * into_z[:, None, None]
    region = np.arange(side) - BUF
    inner = basis[:, :, :CORE].astype(np.float32)
    outer = basis[:, :, region % (2 * CORE)].astype(np.float32)
    outer_z = z_basis[:, region % grid_z].astype(np.float32)
    eigen = eigenvalue(waves, 2 * CORE)
    lam = (
        eigen[:, None, :, None, None]
        + eigen[None, :, None, :, None]
        + eigenvalue(z_waves, grid_z)[None, None, None, None, :]
    )
    lam[0, 0, 0, 0, 0] = np.inf
    factor = (FOUR_PI / lam).astype(np.float32)
    grid_cubes = cubes.reshape(dom_count, CORE, CORE, CORE)
    spec = jnp.einsum("jxyz,jpqzk->pqxyk", grid_cubes, into_z, precision=precise)
    spec = jnp.einsum("pqxyk,pax->pqayk", spec, inner, precision=precise)
    spec = jnp.einsum("pqayk,qby->pqabk", spec, inner, precision=precise)
    spec = spec * factor
    field = jnp.einsum("pqabk,pax->qxbk", spec, outer, precision=precise)
    field = jnp.einsum("qxbk,qby->xyk", field, outer, precision=precise)
    hartree = jnp.einsum("xyk,kz->xyz", field, outer_z, precision=precise)
    place_of = (shift[:, 2] * 2 + shift[:, 1]) * 2 + shift[:, 0]
    by_place = jnp.zeros_like(grid_cubes).at[place_of].set(grid_cubes)
    by_place = by_place.reshape(grid_z // CORE, 2, 2, CORE, CORE, CORE)
    density = jnp.transpose(by_place, (2, 3, 1, 4, 0, 5)).reshape(2 * CORE, 2 * CORE, grid_z)
    density = jnp.concatenate([density[-BUF:], density[: CORE + BUF]], 0)
    density = jnp.concatenate([density[:, -BUF:], density[:, : CORE + BUF]], 1)
    z_index = region % grid_z
    density = jnp.take(density, jnp.asarray(z_index), axis=2)
    renewed = potential + hartree.reshape(side, cells) + EXCHANGE_COEF * jnp.cbrt(density.reshape(side, cells))

    result = pl.pallas_call(
        second_kernel,
        out_shape=jax.ShapeDtypeStruct((half, cells), jnp.float32),
        in_specs=[SMEM, VMEM, VMEM, VMEM],
        out_specs=VMEM,
        scratch_shapes=field_scratch(half),
        compiler_params=params,
    )(slab_scalar, filt, halo, renewed)
    return result[None, None]


def solution(mesh):
    in_specs = (P("dom", "band", None, None), P("dom", None, None), P())
    out_specs = P("dom", "band", None, None)
    return jax.shard_map(local, mesh=mesh, in_specs=in_specs, out_specs=out_specs, check_vma=False)
```

```python
import functools
import math

import jax
import jax.numpy as jnp
import ml_dtypes
import numpy as np
from jax import lax
from jax.experimental import pallas as pl
from jax.experimental.pallas import tpu as pltpu
from jax.sharding import PartitionSpec as P

CORE = 32
BUF = 4
DEG = 8

HALF_WIDTH = 4.5
FOUR_PI = 4.0 * math.pi
EXCHANGE_COEF = -((3.0 / math.pi) ** (1.0 / 3.0))


def swapped(value, axis, mask):
    pairs = [(source, source ^ mask) for source in range(lax.axis_size(axis))]
    return lax.ppermute(value, axis, pairs)


def wave_basis(length):
    cells = np.arange(length)
    rows, waves = [], []
    for wave in range(length // 2 + 1):
        angle = 2.0 * np.pi * ((wave * cells) % length) / length
        if wave in (0, length // 2):
            rows.append(np.cos(angle) / np.sqrt(length))
            waves.append(wave)
        else:
            rows.append(np.cos(angle) * np.sqrt(2.0 / length))
            rows.append(np.sin(angle) * np.sqrt(2.0 / length))
            waves += [wave, wave]
    return np.array(rows), np.array(waves)


def parity_basis():
    rows, waves = wave_basis(2 * CORE)
    return np.stack([rows[waves % 2 == 0], rows[waves % 2 == 1]]), np.stack(
        [waves[waves % 2 == 0], waves[waves % 2 == 1]]
    )


def eigenvalue(waves, length):
    return 2.0 - 2.0 * np.cos(2.0 * np.pi * waves / length)


def padded(length, unit):
    return -(-length // unit) * unit


def place(is_lower, own, halo, field_ref, half, side):
    cells = side * side
    field_ref[...] = jnp.zeros(field_ref.shape, jnp.float32)

    @pl.when(is_lower)
    def _():
        field_ref[0:half, 0:cells] = own
        field_ref[half : half + DEG, 0:cells] = halo

    @pl.when(jnp.logical_not(is_lower))
    def _():
        field_ref[0:DEG, 0:cells] = halo
        field_ref[DEG : DEG + half, 0:cells] = own


def filtered_field(field, scaled_potential, half, side):
    rows, lanes = field.shape
    row_id = lax.broadcasted_iota(jnp.int32, (rows, lanes), 0)
    lane_id = lax.broadcasted_iota(jnp.int32, (rows, lanes), 1)
    inside = (row_id < half + DEG) & (lane_id < side * side)
    weight = jnp.where(inside, 1.0 / HALF_WIDTH, 0.0)
    column = lane_id % side
    not_first = column != 0
    not_last = column != side - 1

    def beside(values):
        total = pltpu.roll(values, 1, 0) + pltpu.roll(values, rows - 1, 0)
        total = total + pltpu.roll(values, side, 1) + pltpu.roll(values, lanes - side, 1)
        total = total + jnp.where(not_first, pltpu.roll(values, 1, 1), 0.0)
        return total + jnp.where(not_last, pltpu.roll(values, lanes - 1, 1), 0.0)

    previous = field
    current = 0.5 * (scaled_potential * field - weight * beside(field))
    for _ in range(DEG - 1):
        following = scaled_potential * current - weight * beside(current) - previous
        previous, current = current, following
    return current


def own_rows(is_lower, values, half):
    return jnp.where(is_lower, values[0:half], values[DEG : DEG + half])


def first_kernel(bands, slab_ref, psi_ref, halo_ref, pot_ref, filt_ref, dens_ref, field_ref, coef_ref):
    half, cells = psi_ref.shape
    side = 2 * half
    is_lower = slab_ref[0] == 0
    place(is_lower, psi_ref[...], halo_ref[...], field_ref, half, side)
    coef_ref[...] = jnp.zeros(coef_ref.shape, jnp.float32)

    @pl.when(is_lower)
    def _():
        coef_ref[0 : half + DEG, 0:cells] = pot_ref[0 : half + DEG] * (2.0 / HALF_WIDTH)

    @pl.when(jnp.logical_not(is_lower))
    def _():
        coef_ref[0 : half + DEG, 0:cells] = pot_ref[half - DEG : side] * (2.0 / HALF_WIDTH)

    result = filtered_field(field_ref[...], coef_ref[...], half, side)
    filt_ref[...] = own_rows(is_lower, result, half)[:, 0:cells]
    slab = CORE // 2
    core_rows = jnp.where(is_lower, result[BUF : BUF + slab], result[DEG : DEG + slab])
    squares = core_rows * core_rows * (1.0 / bands)
    per_tile = 128 // CORE
    for tile in range(CORE // per_tile):
        pieces = []
        for line in range(tile * per_tile, (tile + 1) * per_tile):
            start = (line + BUF) * side + BUF
            pieces.append(squares[:, start : start + CORE])
        dens_ref[:, tile * 128 : (tile + 1) * 128] = jnp.concatenate(pieces, 1)


def split2(values):
    high = values.astype(jnp.bfloat16)
    return high, (values - high.astype(jnp.float32)).astype(jnp.bfloat16)


def split3(values):
    high = values.astype(jnp.bfloat16)
    rest = values - high.astype(jnp.float32)
    middle = rest.astype(jnp.bfloat16)
    return high, middle, (rest - middle.astype(jnp.float32)).astype(jnp.bfloat16)


def dot(left, right):
    return jnp.dot(left, right, preferred_element_type=jnp.float32)


def table_parts(table):
    high = table.astype(ml_dtypes.bfloat16)
    return high, (table - high.astype(np.float64)).astype(ml_dtypes.bfloat16)


def left_table(table):
    high, low = table_parts(table)
    return np.concatenate([high, low, high], -1)


def stacked(values):
    high, low = split2(values)
    return jnp.concatenate([high, high, low], 0)


@functools.lru_cache(maxsize=None)
def solver_tables(side, grid_z):
    half = side // 2
    blocks_z = grid_z // CORE
    basis, waves = parity_basis()
    z_basis, z_waves = wave_basis(grid_z)
    lines = 128 // CORE
    into = []
    for place_z in range(blocks_z):
        along_z = z_basis[:, place_z * CORE : (place_z + 1) * CORE].T
        for place_y in range(2):
            for place_x in range(2):
                signs = [(-1.0) ** (px * place_x + py * place_y) for px in range(2) for py in range(2)]
                table = np.kron(np.eye(lines), np.concatenate([sign * along_z for sign in signs], 1))
                high, low = table_parts(table)
                into += [high, high, low]
    into = np.concatenate(into, 0)
    forward = left_table(np.concatenate([basis[0, :, :CORE], basis[1, :, :CORE]], 0))
    region = np.arange(side) - BUF
    outer = basis[:, :, region % (2 * CORE)]
    back_y = left_table(np.concatenate([outer[0].T, outer[1].T], 0))
    back_x = []
    for first_row in (0, half - DEG):
        rows = outer[:, :, first_row : first_row + half + DEG]
        rows = np.pad(rows, ((0, 0), (0, 0), (0, padded(half + DEG, 8) - half - DEG)))
        back_x.append(left_table(np.concatenate([rows[0].T, rows[1].T], 0)))
    back_x = np.stack(back_x)
    outer_z = np.zeros((4, grid_z, 128))
    outer_z[:, :, :side] = z_basis[:, region % grid_z]
    high, low = table_parts(outer_z.reshape(4 * grid_z, 128))
    back_z = np.block([[high, low], [high, np.zeros_like(low)]])
    eigen = eigenvalue(waves, 2 * CORE)
    lam = (
        eigen.T[:, None, :, None, None]
        + eigen.T[None, :, None, :, None]
        + eigenvalue(z_waves, grid_z)[None, None, None, None, :]
    )
    lam[0, 0, 0, 0, 0] = np.inf
    factor = (FOUR_PI / lam).reshape(CORE * CORE, 4 * grid_z).astype(np.float32)
    spread = np.zeros((blocks_z, 3, CORE, side))
    for cell, pos in enumerate(region % grid_z):
        spread[pos // CORE, :, pos % CORE, cell] = 1.0
    spread = np.concatenate(
        [np.kron(np.eye(lines), spread[block, part]) for block in range(blocks_z) for part in range(3)], 0
    ).astype(ml_dtypes.bfloat16)
    return dict(
        into=into, forward=forward, back_y=back_y, back_x=back_x, back_z=back_z, factor=factor, spread=spread
    )


def cube_root(values):
    positive = values > 0.0
    safe = jnp.where(positive, values, 1.0)
    root = jnp.exp(jnp.log(safe) * (1.0 / 3.0))
    root = root - (root - safe / (root * root)) * (1.0 / 3.0)
    return jnp.where(positive, root, 0.0)


def second_kernel(
    masks, index_ref, offsets_ref, cubes_ref, filt_ref, halo_ref, pot_ref,
    into_ref, forward_ref, back_y_ref, back_x_ref, back_z_ref, factor_ref, spread_ref,
    out_ref, field_ref, coef_ref, dens_ref, left_ref, rows_ref, waves_ref, mixed_ref, flat_ref,
):
    half, cells = filt_ref.shape
    side = 2 * half
    slab, dom = index_ref[0], index_ref[1]
    is_lower = slab == 0
    dom_count = len(masks)
    blocks_z = dom_count // 4
    grid_z = CORE * blocks_z
    lanes = 4 * grid_z
    columns = lanes // 128
    tiles = CORE * CORE // 128
    lines = 128 // CORE
    field_rows = field_ref.shape[0]

    place_of = []
    for mask in masks:
        other = dom ^ mask
        at_x = (offsets_ref[other, 0] != offsets_ref[dom, 0]).astype(jnp.int32)
        at_y = (offsets_ref[other, 1] != offsets_ref[dom, 1]).astype(jnp.int32)
        at_z = (offsets_ref[other, 2] - offsets_ref[dom, 2]) // CORE
        at_z = jnp.where(at_z < 0, at_z + blocks_z, at_z)
        place_of.append((at_z * 2 + at_y) * 2 + at_x)
    cube_at = []
    for where in range(dom_count):
        found = jnp.int32(0)
        for idx in range(dom_count):
            found = found + jnp.where(place_of[idx] == where, idx, 0)
        cube_at.append(found)

    mean = jnp.sum(cubes_ref[...]) * (1.0 / (dom_count * CORE * CORE * CORE))

    for where in range(dom_count):
        for tile in range(tiles):
            part = cubes_ref[cube_at[where], :, tile * 128 : (tile + 1) * 128] - mean
            high, low = split2(part)
            rows = slice(tile * CORE, (tile + 1) * CORE)
            for idx, piece in enumerate((high, low, high)):
                left_ref[rows, (where * 3 + idx) * 128 : (where * 3 + idx + 1) * 128] = piece
    product = dot(left_ref[...], into_ref[...])
    for tile in range(tiles):
        for line in range(lines):
            y = tile * lines + line
            for col in range(columns):
                start = line * lanes + col * 128
                rows_ref[col, y * CORE : (y + 1) * CORE, :] = product[
                    tile * CORE : (tile + 1) * CORE, start : start + 128
                ]

    group = max(1, 256 // lanes)
    lane_id = lax.broadcasted_iota(jnp.int32, (1, group * lanes), 1) % lanes
    even_x = lane_id < 2 * grid_z
    even_y = (lane_id // grid_z) % 2 == 0

    def side_by_side(ref, starts, stride, count):
        pieces = []
        for start in starts:
            for col in range(columns):
                if stride == 1:
                    pieces.append(ref[col, pl.ds(start, count), :])
                else:
                    pieces.append(ref[col, pl.ds(start, count, stride=stride), :])
        return jnp.concatenate(pieces, 1)

    def scatter(ref, starts, values, count):
        for idx, start in enumerate(starts):
            for col in range(columns):
                at = (idx * columns + col) * 128
                ref[col, start : start + count, :] = values[:, at : at + 128]

    forward = forward_ref[...]
    for first in range(0, CORE, group):
        starts = [y * CORE for y in range(first, first + group)]
        both = dot(forward, stacked(side_by_side(rows_ref, starts, 1, CORE)))
        scatter(waves_ref, starts, jnp.where(even_x, both[:CORE], both[CORE:]), CORE)

    back_y = back_y_ref[...]
    for first in range(0, CORE, group):
        waves_x = list(range(first, first + group))
        both = dot(forward, stacked(side_by_side(waves_ref, waves_x, CORE, CORE)))
        modes = jnp.where(even_y, both[:CORE], both[CORE:])
        scale = jnp.concatenate([factor_ref[wave * CORE : (wave + 1) * CORE] for wave in waves_x], 1)
        both = dot(back_y, stacked(modes * scale))
        scatter(mixed_ref, [wave * side for wave in waves_x], jnp.where(even_y, both[:side], both[side:]), side)

    back_x = back_x_ref[slab]
    for first in range(0, side, group):
        both = dot(back_x, stacked(side_by_side(mixed_ref, list(range(first, first + group)), side, CORE)))
        high, low = split2(jnp.where(even_x, both[:field_rows], both[field_rows:]))
        for idx in range(group):
            rows = slice((first + idx) * field_rows, (first + idx + 1) * field_rows)
            flat_ref[rows, 0:lanes] = high[:, idx * lanes : (idx + 1) * lanes]
            flat_ref[rows, lanes : 2 * lanes] = low[:, idx * lanes : (idx + 1) * lanes]

    product = dot(flat_ref[...], back_z_ref[...])
    hartree = product[:, 0:128] + product[:, 128:256]
    coef_ref[...] = jnp.zeros(coef_ref.shape, jnp.float32)
    for y in range(side):
        coef_ref[:, y * side : (y + 1) * side] = hartree[y * field_rows : (y + 1) * field_rows, 0:side]

    dens_ref[...] = jnp.zeros(dens_ref.shape, jnp.float32)
    ahead = half + DEG - BUF
    width = lines * side
    for tile in range(-1, tiles + 1):
        at_y = 0 if 0 <= tile < tiles else 1
        src = tile % tiles
        pieces = []
        for at_z in range(blocks_z):
            cols = slice(src * 128, (src + 1) * 128)
            own = cubes_ref[cube_at[(at_z * 2 + at_y) * 2], :, cols]
            beside = cubes_ref[cube_at[(at_z * 2 + at_y) * 2 + 1], :, cols]
            lower = jnp.concatenate([beside[CORE - BUF :], own[:ahead]], 0)
            upper = jnp.concatenate([own[CORE - ahead :], beside[:BUF]], 0)
            rows = jnp.where(is_lower, lower, upper)
            rows = jnp.concatenate([rows, jnp.zeros((field_rows - half - DEG, 128), jnp.float32)], 0)
            pieces += split3(rows)
        spread = dot(jnp.concatenate(pieces, 1), spread_ref[...])
        start = (tile + 1) * width
        dens_ref[:, start : start + width] = spread
    hartree_exchange = coef_ref[...] + EXCHANGE_COEF * cube_root(dens_ref[...])

    field_ref[...] = jnp.zeros(field_ref.shape, jnp.float32)

    @pl.when(is_lower)
    def _():
        field_ref[0 : half + DEG, 0:cells] = pot_ref[0 : half + DEG]

    @pl.when(jnp.logical_not(is_lower))
    def _():
        field_ref[0 : half + DEG, 0:cells] = pot_ref[half - DEG : side]

    coef_ref[...] = (field_ref[...] + hartree_exchange) * (2.0 / HALF_WIDTH)
    place(is_lower, filt_ref[...], halo_ref[...], field_ref, half, side)
    result = filtered_field(field_ref[...], coef_ref[...], half, side)
    out_ref[...] = own_rows(is_lower, result, half)[:, 0:cells]


def field_scratch(half, count):
    shape = (padded(half + DEG, 8), padded(4 * half * half, 128))
    return [pltpu.VMEM(shape, jnp.float32)] * count


SMEM = pl.BlockSpec(memory_space=pltpu.SMEM)
VMEM = pl.BlockSpec(memory_space=pltpu.VMEM)
params = pltpu.CompilerParams(vmem_limit_bytes=40 * 1024 * 1024)


def local(psi_in, v_in, offsets):
    band_count = lax.axis_size("band")
    dom_count = lax.axis_size("dom")
    dom_idx = lax.axis_index("dom")
    slab_idx = lax.axis_index("band") % 2
    is_lower = slab_idx == 0
    slab_scalar = slab_idx.astype(jnp.int32).reshape(1)
    side = v_in.shape[1]
    half = side // 2
    cells = side * side
    bands = band_count // 2
    grid_z = CORE * dom_count // 4

    wavefunc = psi_in[0, 0]
    potential = v_in[0]

    def halo_of(rows):
        edge = jnp.where(is_lower, rows[half - DEG : half], rows[0:DEG])
        return swapped(edge, "band", 1)

    filt, dens = pl.pallas_call(
        functools.partial(first_kernel, bands),
        out_shape=(
            jax.ShapeDtypeStruct((half, cells), jnp.float32),
            jax.ShapeDtypeStruct((CORE // 2, CORE * CORE), jnp.float32),
        ),
        in_specs=[SMEM, VMEM, VMEM, VMEM],
        out_specs=(VMEM, VMEM),
        scratch_shapes=field_scratch(half, 2),
        compiler_params=params,
    )(slab_scalar, wavefunc, halo_of(wavefunc), potential)

    mask = 2
    while mask < band_count:
        dens = dens + swapped(dens, "band", mask)
        mask *= 2
    filt_edge, dens = lax.optimization_barrier((filt, dens))
    halo = halo_of(filt_edge)
    beside = swapped(dens, "band", 1)
    cube = jnp.concatenate([jnp.where(is_lower, dens, beside), jnp.where(is_lower, beside, dens)], 0)
    cubes = cube[None]
    masks = [0]
    bit = dom_count // 2
    while bit:
        cubes = jnp.concatenate([cubes, swapped(cubes, "dom", bit)], 0)
        masks = masks + [one | bit for one in masks]
        bit //= 2

    tables = solver_tables(side, grid_z)
    names = ("into", "forward", "back_y", "back_x", "back_z", "factor", "spread")
    index = jnp.stack([slab_idx, dom_idx]).astype(jnp.int32)
    lanes = 4 * grid_z
    field_rows = padded(half + DEG, 8)
    f32, bf16 = jnp.float32, jnp.bfloat16
    result = pl.pallas_call(
        functools.partial(second_kernel, masks),
        out_shape=jax.ShapeDtypeStruct((half, cells), f32),
        in_specs=[SMEM, SMEM] + [VMEM] * (4 + len(names)),
        out_specs=VMEM,
        scratch_shapes=field_scratch(half, 3)
        + [
            pltpu.VMEM((CORE * CORE * CORE // 128, dom_count * 3 * 128), bf16),
            pltpu.VMEM((lanes // 128, CORE * CORE, 128), f32),
            pltpu.VMEM((lanes // 128, CORE * CORE, 128), f32),
            pltpu.VMEM((lanes // 128, CORE * side, 128), f32),
            pltpu.VMEM((side * field_rows, 2 * lanes), bf16),
        ],
        compiler_params=params,
    )(index, offsets, cubes, filt, halo, potential, *[jnp.asarray(tables[name]) for name in names])
    return result[None, None]


def solution(mesh):
    in_specs = (P("dom", "band", None, None), P("dom", None, None), P())
    out_specs = P("dom", "band", None, None)
    return jax.shard_map(local, mesh=mesh, in_specs=in_specs, out_specs=out_specs, check_vma=False)
```

```python
import functools
import math

import jax
import jax.numpy as jnp
import ml_dtypes
import numpy as np
from jax import lax
from jax.experimental import pallas as pl
from jax.experimental.pallas import tpu as pltpu
from jax.sharding import PartitionSpec as P

CORE = 32
BUF = 4
DEG = 8

HALF_WIDTH = 4.5
FOUR_PI = 4.0 * math.pi
EXCHANGE_COEF = -((3.0 / math.pi) ** (1.0 / 3.0))


def swapped(value, axis, mask):
    pairs = [(source, source ^ mask) for source in range(lax.axis_size(axis))]
    return lax.ppermute(value, axis, pairs)


def wave_basis(length):
    cells = np.arange(length)
    rows, waves = [], []
    for wave in range(length // 2 + 1):
        angle = 2.0 * np.pi * ((wave * cells) % length) / length
        if wave in (0, length // 2):
            rows.append(np.cos(angle) / np.sqrt(length))
            waves.append(wave)
        else:
            rows.append(np.cos(angle) * np.sqrt(2.0 / length))
            rows.append(np.sin(angle) * np.sqrt(2.0 / length))
            waves += [wave, wave]
    return np.array(rows), np.array(waves)


def parity_basis():
    rows, waves = wave_basis(2 * CORE)
    return np.stack([rows[waves % 2 == 0], rows[waves % 2 == 1]]), np.stack(
        [waves[waves % 2 == 0], waves[waves % 2 == 1]]
    )


def eigenvalue(waves, length):
    return 2.0 - 2.0 * np.cos(2.0 * np.pi * waves / length)


def padded(length, unit):
    return -(-length // unit) * unit


def set_halo(is_lower, halo, field_ref, half):
    cells = halo.shape[1]

    @pl.when(is_lower)
    def _():
        field_ref[half : half + DEG, 0:cells] = halo

    @pl.when(jnp.logical_not(is_lower))
    def _():
        field_ref[0:DEG, 0:cells] = halo


def edge_rows(is_lower, own, half):
    return jnp.where(is_lower, own[half - DEG : half], own[0:DEG])


def start_kernel(slab_ref, psi_ref, pot_ref, edge_ref, field_ref, coef_ref, own_ref, all_ref, sems):
    half, _, cells = psi_ref.shape
    side = 2 * half
    is_lower = slab_ref[0] == 0
    rows_copy = pltpu.make_async_copy(psi_ref, own_ref, sems.at[0])
    pot_copy = pltpu.make_async_copy(pot_ref, all_ref, sems.at[1])
    rows_copy.start()
    pot_copy.start()
    field_ref[...] = jnp.zeros(field_ref.shape, jnp.float32)
    coef_ref[...] = jnp.zeros(coef_ref.shape, jnp.float32)
    rows_copy.wait()
    own = own_ref[:, 0, :]
    edge_ref[...] = edge_rows(is_lower, own, half)

    @pl.when(is_lower)
    def _():
        field_ref[0:half, 0:cells] = own

    @pl.when(jnp.logical_not(is_lower))
    def _():
        field_ref[DEG : DEG + half, 0:cells] = own

    pot_copy.wait()

    @pl.when(is_lower)
    def _():
        coef_ref[0 : half + DEG, 0:cells] = all_ref[0 : half + DEG] * (2.0 / HALF_WIDTH)

    @pl.when(jnp.logical_not(is_lower))
    def _():
        coef_ref[0 : half + DEG, 0:cells] = all_ref[half - DEG : side] * (2.0 / HALF_WIDTH)


def filtered_field(field, scaled_potential, half, side):
    rows, lanes = field.shape
    row_id = lax.broadcasted_iota(jnp.int32, (rows, lanes), 0)
    lane_id = lax.broadcasted_iota(jnp.int32, (rows, lanes), 1)
    inside = (row_id < half + DEG) & (lane_id < side * side)
    weight = jnp.where(inside, 1.0 / HALF_WIDTH, 0.0)
    column = lane_id % side
    not_first = column != 0
    not_last = column != side - 1

    def beside(values):
        total = pltpu.roll(values, 1, 0) + pltpu.roll(values, rows - 1, 0)
        total = total + pltpu.roll(values, side, 1) + pltpu.roll(values, lanes - side, 1)
        total = total + jnp.where(not_first, pltpu.roll(values, 1, 1), 0.0)
        return total + jnp.where(not_last, pltpu.roll(values, lanes - 1, 1), 0.0)

    previous = field
    current = 0.5 * (scaled_potential * field - weight * beside(field))
    for _ in range(DEG - 1):
        following = scaled_potential * current - weight * beside(current) - previous
        previous, current = current, following
    return current


def own_rows(is_lower, values, half):
    return jnp.where(is_lower, values[0:half], values[DEG : DEG + half])


def first_kernel(bands, side, slab_ref, start_ref, halo_ref, coef_ref, filt_ref, edge_ref, dens_ref, field_ref):
    half = side // 2
    cells = side * side
    is_lower = slab_ref[0] == 0
    field_ref[...] = start_ref[...]
    set_halo(is_lower, halo_ref[...], field_ref, half)
    result = filtered_field(field_ref[...], coef_ref[...], half, side)
    filt_ref[...] = result
    edge_ref[...] = edge_rows(is_lower, own_rows(is_lower, result, half), half)[:, 0:cells]
    slab = CORE // 2
    core_rows = jnp.where(is_lower, result[BUF : BUF + slab], result[DEG : DEG + slab])
    squares = core_rows * core_rows * (1.0 / bands)
    per_tile = 128 // CORE
    for tile in range(CORE // per_tile):
        pieces = []
        for line in range(tile * per_tile, (tile + 1) * per_tile):
            start = (line + BUF) * side + BUF
            pieces.append(squares[:, start : start + CORE])
        dens_ref[:, tile * 128 : (tile + 1) * 128] = jnp.concatenate(pieces, 1)


def split2(values):
    high = values.astype(jnp.bfloat16)
    return high, (values - high.astype(jnp.float32)).astype(jnp.bfloat16)


def split3(values):
    high = values.astype(jnp.bfloat16)
    rest = values - high.astype(jnp.float32)
    middle = rest.astype(jnp.bfloat16)
    return high, middle, (rest - middle.astype(jnp.float32)).astype(jnp.bfloat16)


def dot(left, right):
    return jnp.dot(left, right, preferred_element_type=jnp.float32)


def table_parts(table):
    high = table.astype(ml_dtypes.bfloat16)
    return high, (table - high.astype(np.float64)).astype(ml_dtypes.bfloat16)


def left_table(table):
    high, low = table_parts(table)
    return np.concatenate([high, low, high], -1)


def stacked(values):
    high, low = split2(values)
    return jnp.concatenate([high, high, low], 0)


@functools.lru_cache(maxsize=None)
def solver_tables(side, grid_z):
    half = side // 2
    blocks_z = grid_z // CORE
    basis, waves = parity_basis()
    z_basis, z_waves = wave_basis(grid_z)
    lines = 128 // CORE
    into = []
    for place_z in range(blocks_z):
        along_z = z_basis[:, place_z * CORE : (place_z + 1) * CORE].T
        for place_y in range(2):
            for place_x in range(2):
                signs = [(-1.0) ** (px * place_x + py * place_y) for px in range(2) for py in range(2)]
                table = np.kron(np.eye(lines), np.concatenate([sign * along_z for sign in signs], 1))
                high, low = table_parts(table)
                into += [high, high, low]
    into = np.concatenate(into, 0)
    forward = left_table(np.concatenate([basis[0, :, :CORE], basis[1, :, :CORE]], 0))
    region = np.arange(side) - BUF
    outer = basis[:, :, region % (2 * CORE)]
    back_y = left_table(np.concatenate([outer[0].T, outer[1].T], 0))
    back_x = []
    for first_row in (0, half - DEG):
        rows = outer[:, :, first_row : first_row + half + DEG]
        rows = np.pad(rows, ((0, 0), (0, 0), (0, padded(half + DEG, 8) - half - DEG)))
        back_x.append(left_table(np.concatenate([rows[0].T, rows[1].T], 0)))
    back_x = np.stack(back_x)
    outer_z = np.zeros((4, grid_z, 128))
    outer_z[:, :, :side] = z_basis[:, region % grid_z]
    high, low = table_parts(outer_z.reshape(4 * grid_z, 128))
    back_z = np.block([[high, low], [high, np.zeros_like(low)]])
    eigen = eigenvalue(waves, 2 * CORE)
    lam = (
        eigen.T[:, None, :, None, None]
        + eigen.T[None, :, None, :, None]
        + eigenvalue(z_waves, grid_z)[None, None, None, None, :]
    )
    lam[0, 0, 0, 0, 0] = np.inf
    factor = (FOUR_PI / lam).reshape(CORE * CORE, 4 * grid_z).astype(np.float32)
    spread = np.zeros((blocks_z, 3, CORE, side))
    for cell, pos in enumerate(region % grid_z):
        spread[pos // CORE, :, pos % CORE, cell] = 1.0
    spread = np.concatenate(
        [np.kron(np.eye(lines), spread[block, part]) for block in range(blocks_z) for part in range(3)], 0
    ).astype(ml_dtypes.bfloat16)
    return dict(
        into=into, forward=forward, back_y=back_y, back_x=back_x, back_z=back_z, factor=factor, spread=spread
    )


def cube_root(values):
    positive = values > 0.0
    safe = jnp.where(positive, values, 1.0)
    root = jnp.exp(jnp.log(safe) * (1.0 / 3.0))
    root = root - (root - safe / (root * root)) * (1.0 / 3.0)
    return jnp.where(positive, root, 0.0)


def second_kernel(
    masks, index_ref, offsets_ref, cubes_ref, filt_ref, halo_ref, start_coef_ref,
    into_ref, forward_ref, back_y_ref, back_x_ref, back_z_ref, factor_ref, spread_ref,
    out_ref, field_ref, coef_ref, dens_ref, left_ref, rows_ref, waves_ref, mixed_ref, flat_ref,
):
    half, _, cells = out_ref.shape
    side = 2 * half
    slab, dom = index_ref[0], index_ref[1]
    is_lower = slab == 0
    dom_count = len(masks)
    blocks_z = dom_count // 4
    grid_z = CORE * blocks_z
    lanes = 4 * grid_z
    columns = lanes // 128
    tiles = CORE * CORE // 128
    lines = 128 // CORE
    field_rows = field_ref.shape[0]

    place_of = []
    for mask in masks:
        other = dom ^ mask
        at_x = (offsets_ref[other, 0] != offsets_ref[dom, 0]).astype(jnp.int32)
        at_y = (offsets_ref[other, 1] != offsets_ref[dom, 1]).astype(jnp.int32)
        at_z = (offsets_ref[other, 2] - offsets_ref[dom, 2]) // CORE
        at_z = jnp.where(at_z < 0, at_z + blocks_z, at_z)
        place_of.append((at_z * 2 + at_y) * 2 + at_x)
    cube_at = []
    for where in range(dom_count):
        found = jnp.int32(0)
        for idx in range(dom_count):
            found = found + jnp.where(place_of[idx] == where, idx, 0)
        cube_at.append(found)

    mean = jnp.sum(cubes_ref[...]) * (1.0 / (dom_count * CORE * CORE * CORE))

    for where in range(dom_count):
        for tile in range(tiles):
            part = cubes_ref[cube_at[where], :, tile * 128 : (tile + 1) * 128] - mean
            high, low = split2(part)
            rows = slice(tile * CORE, (tile + 1) * CORE)
            for idx, piece in enumerate((high, low, high)):
                left_ref[rows, (where * 3 + idx) * 128 : (where * 3 + idx + 1) * 128] = piece
    product = dot(left_ref[...], into_ref[...])
    for tile in range(tiles):
        for line in range(lines):
            y = tile * lines + line
            for col in range(columns):
                start = line * lanes + col * 128
                rows_ref[col, y * CORE : (y + 1) * CORE, :] = product[
                    tile * CORE : (tile + 1) * CORE, start : start + 128
                ]

    group = max(1, 256 // lanes)
    lane_id = lax.broadcasted_iota(jnp.int32, (1, group * lanes), 1) % lanes
    even_x = lane_id < 2 * grid_z
    even_y = (lane_id // grid_z) % 2 == 0

    def side_by_side(ref, starts, stride, count):
        pieces = []
        for start in starts:
            for col in range(columns):
                if stride == 1:
                    pieces.append(ref[col, pl.ds(start, count), :])
                else:
                    pieces.append(ref[col, pl.ds(start, count, stride=stride), :])
        return jnp.concatenate(pieces, 1)

    def scatter(ref, starts, values, count):
        for idx, start in enumerate(starts):
            for col in range(columns):
                at = (idx * columns + col) * 128
                ref[col, start : start + count, :] = values[:, at : at + 128]

    forward = forward_ref[...]
    for first in range(0, CORE, group):
        starts = [y * CORE for y in range(first, first + group)]
        both = dot(forward, stacked(side_by_side(rows_ref, starts, 1, CORE)))
        scatter(waves_ref, starts, jnp.where(even_x, both[:CORE], both[CORE:]), CORE)

    back_y = back_y_ref[...]
    for first in range(0, CORE, group):
        waves_x = list(range(first, first + group))
        both = dot(forward, stacked(side_by_side(waves_ref, waves_x, CORE, CORE)))
        modes = jnp.where(even_y, both[:CORE], both[CORE:])
        scale = jnp.concatenate([factor_ref[wave * CORE : (wave + 1) * CORE] for wave in waves_x], 1)
        both = dot(back_y, stacked(modes * scale))
        scatter(mixed_ref, [wave * side for wave in waves_x], jnp.where(even_y, both[:side], both[side:]), side)

    back_x = back_x_ref[slab]
    for first in range(0, side, group):
        both = dot(back_x, stacked(side_by_side(mixed_ref, list(range(first, first + group)), side, CORE)))
        high, low = split2(jnp.where(even_x, both[:field_rows], both[field_rows:]))
        for idx in range(group):
            rows = slice((first + idx) * field_rows, (first + idx + 1) * field_rows)
            flat_ref[rows, 0:lanes] = high[:, idx * lanes : (idx + 1) * lanes]
            flat_ref[rows, lanes : 2 * lanes] = low[:, idx * lanes : (idx + 1) * lanes]

    product = dot(flat_ref[...], back_z_ref[...])
    hartree = product[:, 0:128] + product[:, 128:256]
    coef_ref[...] = jnp.zeros(coef_ref.shape, jnp.float32)
    for y in range(side):
        coef_ref[:, y * side : (y + 1) * side] = hartree[y * field_rows : (y + 1) * field_rows, 0:side]

    dens_ref[...] = jnp.zeros(dens_ref.shape, jnp.float32)
    ahead = half + DEG - BUF
    width = lines * side
    for tile in range(-1, tiles + 1):
        at_y = 0 if 0 <= tile < tiles else 1
        src = tile % tiles
        pieces = []
        for at_z in range(blocks_z):
            cols = slice(src * 128, (src + 1) * 128)
            own = cubes_ref[cube_at[(at_z * 2 + at_y) * 2], :, cols]
            beside = cubes_ref[cube_at[(at_z * 2 + at_y) * 2 + 1], :, cols]
            lower = jnp.concatenate([beside[CORE - BUF :], own[:ahead]], 0)
            upper = jnp.concatenate([own[CORE - ahead :], beside[:BUF]], 0)
            rows = jnp.where(is_lower, lower, upper)
            rows = jnp.concatenate([rows, jnp.zeros((field_rows - half - DEG, 128), jnp.float32)], 0)
            pieces += split3(rows)
        spread = dot(jnp.concatenate(pieces, 1), spread_ref[...])
        start = (tile + 1) * width
        dens_ref[:, start : start + width] = spread
    hartree_exchange = coef_ref[...] + EXCHANGE_COEF * cube_root(dens_ref[...])

    coef_ref[...] = start_coef_ref[...] + hartree_exchange * (2.0 / HALF_WIDTH)
    field_ref[...] = filt_ref[...]
    set_halo(is_lower, halo_ref[...], field_ref, half)
    result = filtered_field(field_ref[...], coef_ref[...], half, side)
    out_ref[:, 0, :] = own_rows(is_lower, result, half)[:, 0:cells]


SMEM = pl.BlockSpec(memory_space=pltpu.SMEM)
VMEM = pl.BlockSpec(memory_space=pltpu.VMEM)
HBM = pl.BlockSpec(memory_space=pltpu.HBM)
params = pltpu.CompilerParams(vmem_limit_bytes=40 * 1024 * 1024)


def local(psi_in, v_in, offsets):
    band_count = lax.axis_size("band")
    dom_count = lax.axis_size("dom")
    dom_idx = lax.axis_index("dom")
    slab_idx = lax.axis_index("band") % 2
    is_lower = slab_idx == 0
    slab_scalar = slab_idx.astype(jnp.int32).reshape(1)
    side = v_in.shape[1]
    half = side // 2
    cells = side * side
    bands = band_count // 2
    grid_z = CORE * dom_count // 4

    f32, bf16 = jnp.float32, jnp.bfloat16
    field_rows = padded(half + DEG, 8)
    field_shape = (field_rows, padded(cells, 128))
    field_type = jax.ShapeDtypeStruct(field_shape, f32)
    edge_type = jax.ShapeDtypeStruct((DEG, cells), f32)

    edge, start, coef = pl.pallas_call(
        start_kernel,
        out_shape=(edge_type, field_type, field_type),
        in_specs=[SMEM, HBM, HBM],
        out_specs=(VMEM, VMEM, VMEM),
        scratch_shapes=[
            pltpu.VMEM((half, 1, cells), f32),
            pltpu.VMEM((side, cells), f32),
            pltpu.SemaphoreType.DMA((2,)),
        ],
        compiler_params=params,
    )(slab_scalar, psi_in.reshape(half, 1, cells), v_in[0])

    filt, edge, dens = pl.pallas_call(
        functools.partial(first_kernel, bands, side),
        out_shape=(field_type, edge_type, jax.ShapeDtypeStruct((CORE // 2, CORE * CORE), f32)),
        in_specs=[SMEM, VMEM, VMEM, VMEM],
        out_specs=(VMEM, VMEM, VMEM),
        scratch_shapes=[pltpu.VMEM(field_shape, f32)],
        compiler_params=params,
    )(slab_scalar, start, swapped(edge, "band", 1), coef)

    mask = 2
    while mask < band_count:
        received = swapped(dens, "band", mask)
        mask *= 2
        if mask >= band_count:
            edge, _ = lax.optimization_barrier((edge, dens))
            halo = swapped(edge, "band", 1)
            received, halo = lax.optimization_barrier((received, halo))
        dens = dens + received

    far = dom_count // 2
    both = ("dom", "band")
    count = dom_count * band_count

    def crossed(value, mask):
        return lax.ppermute(value, both, [(source, source ^ mask) for source in range(count)])

    beside = crossed(dens, 1)
    across = crossed(dens, far * band_count)
    diagonal = crossed(dens, far * band_count + 1)

    def cube_of(own, other):
        return jnp.concatenate([jnp.where(is_lower, own, other), jnp.where(is_lower, other, own)], 0)

    cubes = jnp.stack([cube_of(dens, beside), cube_of(across, diagonal)])
    masks = [0, far]
    bit = far // 2
    while bit:
        cubes = jnp.concatenate([cubes, swapped(cubes, "dom", bit)], 0)
        masks = masks + [one | bit for one in masks]
        bit //= 2

    tables = solver_tables(side, grid_z)
    names = ("into", "forward", "back_y", "back_x", "back_z", "factor", "spread")
    index = jnp.stack([slab_idx, dom_idx]).astype(jnp.int32)
    lanes = 4 * grid_z
    result = pl.pallas_call(
        functools.partial(second_kernel, masks),
        out_shape=jax.ShapeDtypeStruct((half, 1, cells), f32),
        in_specs=[SMEM, SMEM] + [VMEM] * (4 + len(names)),
        out_specs=VMEM,
        scratch_shapes=[pltpu.VMEM(field_shape, f32)] * 3
        + [
            pltpu.VMEM((CORE * CORE * CORE // 128, dom_count * 3 * 128), bf16),
            pltpu.VMEM((lanes // 128, CORE * CORE, 128), f32),
            pltpu.VMEM((lanes // 128, CORE * CORE, 128), f32),
            pltpu.VMEM((lanes // 128, CORE * side, 128), f32),
            pltpu.VMEM((side * field_rows, 2 * lanes), bf16),
        ],
        compiler_params=params,
    )(index, offsets, cubes, filt, halo, coef, *[jnp.asarray(tables[name]) for name in names])
    return result.reshape(1, 1, half, cells)


def solution(mesh):
    in_specs = (P("dom", "band", None, None), P("dom", None, None), P())
    out_specs = P("dom", "band", None, None)
    return jax.shard_map(local, mesh=mesh, in_specs=in_specs, out_specs=out_specs, check_vma=False)
```

```python
import functools
import math

import jax
import jax.numpy as jnp
import ml_dtypes
import numpy as np
from jax import lax
from jax.experimental import pallas as pl
from jax.experimental.pallas import tpu as pltpu
from jax.sharding import PartitionSpec as P

CORE = 32
BUF = 4
DEG = 8

HALF_WIDTH = 4.5
FOUR_PI = 4.0 * math.pi
EXCHANGE_COEF = -((3.0 / math.pi) ** (1.0 / 3.0))


def swapped(value, axis, mask):
    pairs = [(source, source ^ mask) for source in range(lax.axis_size(axis))]
    return lax.ppermute(value, axis, pairs)


def wave_basis(length):
    cells = np.arange(length)
    rows, waves = [], []
    for wave in range(length // 2 + 1):
        angle = 2.0 * np.pi * ((wave * cells) % length) / length
        if wave in (0, length // 2):
            rows.append(np.cos(angle) / np.sqrt(length))
            waves.append(wave)
        else:
            rows.append(np.cos(angle) * np.sqrt(2.0 / length))
            rows.append(np.sin(angle) * np.sqrt(2.0 / length))
            waves += [wave, wave]
    return np.array(rows), np.array(waves)


def parity_basis():
    rows, waves = wave_basis(2 * CORE)
    return np.stack([rows[waves % 2 == 0], rows[waves % 2 == 1]]), np.stack(
        [waves[waves % 2 == 0], waves[waves % 2 == 1]]
    )


def eigenvalue(waves, length):
    return 2.0 - 2.0 * np.cos(2.0 * np.pi * waves / length)


def padded(length, unit):
    return -(-length // unit) * unit


def set_halo(is_lower, halo, field_ref, half):
    cells = halo.shape[1]

    @pl.when(is_lower)
    def _():
        field_ref[half : half + DEG, 0:cells] = halo

    @pl.when(jnp.logical_not(is_lower))
    def _():
        field_ref[0:DEG, 0:cells] = halo


def edge_rows(is_lower, own, half):
    return jnp.where(is_lower, own[half - DEG : half], own[0:DEG])


def start_kernel(slab_ref, psi_ref, pot_ref, field_ref, coef_ref):
    half, _, cells = psi_ref.shape
    side = 2 * half
    is_lower = slab_ref[0] == 0
    field_ref[...] = jnp.zeros(field_ref.shape, jnp.float32)
    coef_ref[...] = jnp.zeros(coef_ref.shape, jnp.float32)
    own = psi_ref[:, 0, :]

    @pl.when(is_lower)
    def _():
        field_ref[0:half, 0:cells] = own
        coef_ref[0 : half + DEG, 0:cells] = pot_ref[0 : half + DEG] * (2.0 / HALF_WIDTH)

    @pl.when(jnp.logical_not(is_lower))
    def _():
        field_ref[DEG : DEG + half, 0:cells] = own
        coef_ref[0 : half + DEG, 0:cells] = pot_ref[half - DEG : side] * (2.0 / HALF_WIDTH)


def filtered_field(field, scaled_potential, half, side):
    rows, lanes = field.shape
    row_id = lax.broadcasted_iota(jnp.int32, (rows, lanes), 0)
    lane_id = lax.broadcasted_iota(jnp.int32, (rows, lanes), 1)
    inside = (row_id < half + DEG) & (lane_id < side * side)
    weight = jnp.where(inside, 1.0 / HALF_WIDTH, 0.0)
    column = lane_id % side
    not_first = column != 0
    not_last = column != side - 1

    def beside(values):
        total = pltpu.roll(values, 1, 0) + pltpu.roll(values, rows - 1, 0)
        total = total + pltpu.roll(values, side, 1) + pltpu.roll(values, lanes - side, 1)
        total = total + jnp.where(not_first, pltpu.roll(values, 1, 1), 0.0)
        return total + jnp.where(not_last, pltpu.roll(values, lanes - 1, 1), 0.0)

    previous = field
    current = 0.5 * (scaled_potential * field - weight * beside(field))
    for _ in range(DEG - 1):
        following = scaled_potential * current - weight * beside(current) - previous
        previous, current = current, following
    return current


def own_rows(is_lower, values, half):
    return jnp.where(is_lower, values[0:half], values[DEG : DEG + half])


def first_kernel(bands, side, slab_ref, start_ref, halo_ref, coef_ref, filt_ref, edge_ref, dens_ref, field_ref):
    half = side // 2
    is_lower = slab_ref[0] == 0
    field_ref[...] = start_ref[...]
    set_halo(is_lower, halo_ref[:, 0, :], field_ref, half)
    result = filtered_field(field_ref[...], coef_ref[...], half, side)
    filt_ref[...] = result
    edge = edge_rows(is_lower, own_rows(is_lower, result, half), half)
    width = edge_ref.shape[1]
    edge_ref[0:DEG] = edge[:, 0:width]
    edge_ref[DEG : 2 * DEG] = jnp.zeros((DEG, width), jnp.float32)
    edge_ref[DEG : 2 * DEG, 0 : edge.shape[1] - width] = edge[:, width:]
    slab = CORE // 2
    core_rows = jnp.where(is_lower, result[BUF : BUF + slab], result[DEG : DEG + slab])
    squares = core_rows * core_rows * (1.0 / bands)
    per_tile = 128 // CORE
    for tile in range(CORE // per_tile):
        pieces = []
        for line in range(tile * per_tile, (tile + 1) * per_tile):
            start = (line + BUF) * side + BUF
            pieces.append(squares[:, start : start + CORE])
        dens_ref[:, tile * 128 : (tile + 1) * 128] = jnp.concatenate(pieces, 1)


def split2(values):
    high = values.astype(jnp.bfloat16)
    return high, (values - high.astype(jnp.float32)).astype(jnp.bfloat16)


def split3(values):
    high = values.astype(jnp.bfloat16)
    rest = values - high.astype(jnp.float32)
    middle = rest.astype(jnp.bfloat16)
    return high, middle, (rest - middle.astype(jnp.float32)).astype(jnp.bfloat16)


def dot(left, right):
    return jnp.dot(left, right, preferred_element_type=jnp.float32)


def table_parts(table):
    high = table.astype(ml_dtypes.bfloat16)
    return high, (table - high.astype(np.float64)).astype(ml_dtypes.bfloat16)


def left_table(table):
    high, low = table_parts(table)
    return np.concatenate([high, low, high], -1)


def stacked(values):
    high, low = split2(values)
    return jnp.concatenate([high, high, low], 0)


@functools.lru_cache(maxsize=None)
def solver_tables(side, grid_z):
    half = side // 2
    blocks_z = grid_z // CORE
    basis, waves = parity_basis()
    z_basis, z_waves = wave_basis(grid_z)
    lines = 128 // CORE
    into = []
    for place_z in range(blocks_z):
        along_z = z_basis[:, place_z * CORE : (place_z + 1) * CORE].T
        for place_y in range(2):
            for place_x in range(2):
                signs = [(-1.0) ** (px * place_x + py * place_y) for px in range(2) for py in range(2)]
                table = np.kron(np.eye(lines), np.concatenate([sign * along_z for sign in signs], 1))
                high, low = table_parts(table)
                into += [high, high, low]
    into = np.concatenate(into, 0)
    forward = left_table(np.concatenate([basis[0, :, :CORE], basis[1, :, :CORE]], 0))
    region = np.arange(side) - BUF
    outer = basis[:, :, region % (2 * CORE)]
    back_y = left_table(np.concatenate([outer[0].T, outer[1].T], 0))
    back_x = []
    for first_row in (0, half - DEG):
        rows = outer[:, :, first_row : first_row + half + DEG]
        rows = np.pad(rows, ((0, 0), (0, 0), (0, padded(half + DEG, 8) - half - DEG)))
        back_x.append(left_table(np.concatenate([rows[0].T, rows[1].T], 0)))
    back_x = np.stack(back_x)
    outer_z = np.zeros((4, grid_z, 128))
    outer_z[:, :, :side] = z_basis[:, region % grid_z]
    high, low = table_parts(outer_z.reshape(4 * grid_z, 128))
    back_z = np.block([[high, low], [high, np.zeros_like(low)]])
    eigen = eigenvalue(waves, 2 * CORE)
    lam = (
        eigen.T[:, None, :, None, None]
        + eigen.T[None, :, None, :, None]
        + eigenvalue(z_waves, grid_z)[None, None, None, None, :]
    )
    lam[0, 0, 0, 0, 0] = np.inf
    factor = (FOUR_PI / lam).reshape(CORE * CORE, 4 * grid_z).astype(np.float32)
    spread = np.zeros((blocks_z, 3, CORE, side))
    for cell, pos in enumerate(region % grid_z):
        spread[pos // CORE, :, pos % CORE, cell] = 1.0
    spread = np.concatenate(
        [np.kron(np.eye(lines), spread[block, part]) for block in range(blocks_z) for part in range(3)], 0
    ).astype(ml_dtypes.bfloat16)
    return dict(
        into=into, forward=forward, back_y=back_y, back_x=back_x, back_z=back_z, factor=factor, spread=spread
    )


def cube_root(values):
    positive = values > 0.0
    safe = jnp.where(positive, values, 1.0)
    root = jnp.exp(jnp.log(safe) * (1.0 / 3.0))
    root = root - (root - safe / (root * root)) * (1.0 / 3.0)
    return jnp.where(positive, root, 0.0)


def second_kernel(
    masks, index_ref, offsets_ref, near_ref, across_ref, filt_ref, beside_ref, start_coef_ref,
    into_ref, forward_ref, back_y_ref, back_x_ref, back_z_ref, factor_ref, spread_ref,
    out_ref, cubes_ref, field_ref, coef_ref, dens_ref, left_ref, rows_ref, waves_ref, mixed_ref, flat_ref,
):
    half, _, cells = out_ref.shape
    side = 2 * half
    slab, dom = index_ref[0], index_ref[1]
    is_lower = slab == 0
    dom_count = len(masks)
    blocks_z = dom_count // 4
    grid_z = CORE * blocks_z
    lanes = 4 * grid_z
    columns = lanes // 128
    tiles = CORE * CORE // 128
    lines = 128 // CORE
    field_rows = field_ref.shape[0]

    place_of = []
    for mask in masks:
        other = dom ^ mask
        at_x = (offsets_ref[other, 0] != offsets_ref[dom, 0]).astype(jnp.int32)
        at_y = (offsets_ref[other, 1] != offsets_ref[dom, 1]).astype(jnp.int32)
        at_z = (offsets_ref[other, 2] - offsets_ref[dom, 2]) // CORE
        at_z = jnp.where(at_z < 0, at_z + blocks_z, at_z)
        place_of.append((at_z * 2 + at_y) * 2 + at_x)
    cube_at = []
    for where in range(dom_count):
        found = jnp.int32(0)
        for idx in range(dom_count):
            found = found + jnp.where(place_of[idx] == where, idx, 0)
        cube_at.append(found)

    cubes_ref[0 : dom_count // 2] = near_ref[...]
    cubes_ref[dom_count // 2 : dom_count] = across_ref[...]
    mean = jnp.sum(cubes_ref[...]) * (1.0 / (dom_count * CORE * CORE * CORE))

    for where in range(dom_count):
        for tile in range(tiles):
            part = cubes_ref[cube_at[where], :, tile * 128 : (tile + 1) * 128] - mean
            high, low = split2(part)
            rows = slice(tile * CORE, (tile + 1) * CORE)
            for idx, piece in enumerate((high, low, high)):
                left_ref[rows, (where * 3 + idx) * 128 : (where * 3 + idx + 1) * 128] = piece
    product = dot(left_ref[...], into_ref[...])
    for tile in range(tiles):
        for line in range(lines):
            y = tile * lines + line
            for col in range(columns):
                start = line * lanes + col * 128
                rows_ref[col, y * CORE : (y + 1) * CORE, :] = product[
                    tile * CORE : (tile + 1) * CORE, start : start + 128
                ]

    group = max(1, 256 // lanes)
    lane_id = lax.broadcasted_iota(jnp.int32, (1, group * lanes), 1) % lanes
    even_x = lane_id < 2 * grid_z
    even_y = (lane_id // grid_z) % 2 == 0

    def side_by_side(ref, starts, stride, count):
        pieces = []
        for start in starts:
            for col in range(columns):
                if stride == 1:
                    pieces.append(ref[col, pl.ds(start, count), :])
                else:
                    pieces.append(ref[col, pl.ds(start, count, stride=stride), :])
        return jnp.concatenate(pieces, 1)

    def scatter(ref, starts, values, count):
        for idx, start in enumerate(starts):
            for col in range(columns):
                at = (idx * columns + col) * 128
                ref[col, start : start + count, :] = values[:, at : at + 128]

    forward = forward_ref[...]
    for first in range(0, CORE, group):
        starts = [y * CORE for y in range(first, first + group)]
        both = dot(forward, stacked(side_by_side(rows_ref, starts, 1, CORE)))
        scatter(waves_ref, starts, jnp.where(even_x, both[:CORE], both[CORE:]), CORE)

    back_y = back_y_ref[...]
    for first in range(0, CORE, group):
        waves_x = list(range(first, first + group))
        both = dot(forward, stacked(side_by_side(waves_ref, waves_x, CORE, CORE)))
        modes = jnp.where(even_y, both[:CORE], both[CORE:])
        scale = jnp.concatenate([factor_ref[wave * CORE : (wave + 1) * CORE] for wave in waves_x], 1)
        both = dot(back_y, stacked(modes * scale))
        scatter(mixed_ref, [wave * side for wave in waves_x], jnp.where(even_y, both[:side], both[side:]), side)

    back_x = back_x_ref[slab]
    for first in range(0, side, group):
        both = dot(back_x, stacked(side_by_side(mixed_ref, list(range(first, first + group)), side, CORE)))
        high, low = split2(jnp.where(even_x, both[:field_rows], both[field_rows:]))
        for idx in range(group):
            rows = slice((first + idx) * field_rows, (first + idx + 1) * field_rows)
            flat_ref[rows, 0:lanes] = high[:, idx * lanes : (idx + 1) * lanes]
            flat_ref[rows, lanes : 2 * lanes] = low[:, idx * lanes : (idx + 1) * lanes]

    product = dot(flat_ref[...], back_z_ref[...])
    hartree = product[:, 0:128] + product[:, 128:256]
    coef_ref[...] = jnp.zeros(coef_ref.shape, jnp.float32)
    for y in range(side):
        coef_ref[:, y * side : (y + 1) * side] = hartree[y * field_rows : (y + 1) * field_rows, 0:side]

    dens_ref[...] = jnp.zeros(dens_ref.shape, jnp.float32)
    ahead = half + DEG - BUF
    width = lines * side
    for tile in range(-1, tiles + 1):
        at_y = 0 if 0 <= tile < tiles else 1
        src = tile % tiles
        pieces = []
        for at_z in range(blocks_z):
            cols = slice(src * 128, (src + 1) * 128)
            own = cubes_ref[cube_at[(at_z * 2 + at_y) * 2], :, cols]
            beside = cubes_ref[cube_at[(at_z * 2 + at_y) * 2 + 1], :, cols]
            lower = jnp.concatenate([beside[CORE - BUF :], own[:ahead]], 0)
            upper = jnp.concatenate([own[CORE - ahead :], beside[:BUF]], 0)
            rows = jnp.where(is_lower, lower, upper)
            rows = jnp.concatenate([rows, jnp.zeros((field_rows - half - DEG, 128), jnp.float32)], 0)
            pieces += split3(rows)
        spread = dot(jnp.concatenate(pieces, 1), spread_ref[...])
        start = (tile + 1) * width
        dens_ref[:, start : start + width] = spread
    hartree_exchange = coef_ref[...] + EXCHANGE_COEF * cube_root(dens_ref[...])

    coef_ref[...] = start_coef_ref[...] + hartree_exchange * (2.0 / HALF_WIDTH)
    field_ref[...] = filt_ref[...]
    packed = beside_ref[CORE // 2 :]
    halo = jnp.concatenate([packed[0:DEG], packed[DEG : 2 * DEG]], 1)[:, 0:cells]
    set_halo(is_lower, halo, field_ref, half)
    result = filtered_field(field_ref[...], coef_ref[...], half, side)
    out_ref[:, 0, :] = own_rows(is_lower, result, half)[:, 0:cells]


SMEM = pl.BlockSpec(memory_space=pltpu.SMEM)
VMEM = pl.BlockSpec(memory_space=pltpu.VMEM)
params = pltpu.CompilerParams(vmem_limit_bytes=32 * 1024 * 1024)


def local(psi_in, v_in, offsets):
    band_count = lax.axis_size("band")
    dom_count = lax.axis_size("dom")
    dom_idx = lax.axis_index("dom")
    slab_idx = lax.axis_index("band") % 2
    is_lower = slab_idx == 0
    slab_scalar = slab_idx.astype(jnp.int32).reshape(1)
    side = v_in.shape[1]
    half = side // 2
    cells = side * side
    bands = band_count // 2
    grid_z = CORE * dom_count // 4

    f32, bf16 = jnp.float32, jnp.bfloat16
    field_rows = padded(half + DEG, 8)
    field_shape = (field_rows, padded(cells, 128))
    field_type = jax.ShapeDtypeStruct(field_shape, f32)
    rows = psi_in.reshape(half, 1, cells)
    halo = swapped(lax.dynamic_slice_in_dim(rows, jnp.where(is_lower, half - DEG, 0), DEG, 0), "band", 1)
    start, coef = pl.pallas_call(
        start_kernel,
        out_shape=(field_type, field_type),
        in_specs=[SMEM, VMEM, VMEM],
        out_specs=(VMEM, VMEM),
        compiler_params=params,
    )(slab_scalar, rows, v_in[0])

    filt, edge, dens = pl.pallas_call(
        functools.partial(first_kernel, bands, side),
        out_shape=(
            field_type,
            jax.ShapeDtypeStruct((2 * DEG, CORE * CORE), f32),
            jax.ShapeDtypeStruct((CORE // 2, CORE * CORE), f32),
        ),
        in_specs=[SMEM, VMEM, VMEM, VMEM],
        out_specs=(VMEM, VMEM, VMEM),
        scratch_shapes=[pltpu.VMEM(field_shape, f32)],
        compiler_params=params,
    )(slab_scalar, start, halo, coef)

    mask = 2
    while mask < band_count:
        dens = dens + swapped(dens, "band", mask)
        mask *= 2

    far = dom_count // 2
    both = ("dom", "band")
    count = dom_count * band_count

    def crossed(value, mask):
        return lax.ppermute(value, both, [(source, source ^ mask) for source in range(count)])

    beside_all = crossed(jnp.concatenate([dens, edge], 0), 1)
    beside = beside_all[: CORE // 2]
    across = crossed(dens, far * band_count)
    diagonal = crossed(dens, far * band_count + 1)

    def cube_of(own, other):
        return jnp.concatenate([jnp.where(is_lower, own, other), jnp.where(is_lower, other, own)], 0)

    cubes = jnp.stack([cube_of(dens, beside), cube_of(across, diagonal)])
    masks = [0, far]
    bit = far // 2
    while bit:
        if bit > 1:
            cubes = jnp.concatenate([cubes, swapped(cubes, "dom", bit)], 0)
        masks = masks + [one | bit for one in masks]
        bit //= 2
    cubes_across = swapped(cubes, "dom", 1)

    tables = solver_tables(side, grid_z)
    names = ("into", "forward", "back_y", "back_x", "back_z", "factor", "spread")
    index = jnp.stack([slab_idx, dom_idx]).astype(jnp.int32)
    lanes = 4 * grid_z
    result = pl.pallas_call(
        functools.partial(second_kernel, masks),
        out_shape=jax.ShapeDtypeStruct((half, 1, cells), f32),
        in_specs=[SMEM, SMEM] + [VMEM] * (5 + len(names)),
        out_specs=VMEM,
        scratch_shapes=[pltpu.VMEM((dom_count, CORE, CORE * CORE), f32)]
        + [pltpu.VMEM(field_shape, f32)] * 3
        + [
            pltpu.VMEM((CORE * CORE * CORE // 128, dom_count * 3 * 128), bf16),
            pltpu.VMEM((lanes // 128, CORE * CORE, 128), f32),
            pltpu.VMEM((lanes // 128, CORE * CORE, 128), f32),
            pltpu.VMEM((lanes // 128, CORE * side, 128), f32),
            pltpu.VMEM((side * field_rows, 2 * lanes), bf16),
        ],
        compiler_params=params,
    )(index, offsets, cubes, cubes_across, filt, beside_all, coef, *[jnp.asarray(tables[name]) for name in names])
    return result.reshape(1, 1, half, cells)


def solution(mesh):
    in_specs = (P("dom", "band", None, None), P("dom", None, None), P())
    out_specs = P("dom", "band", None, None)
    return jax.shard_map(local, mesh=mesh, in_specs=in_specs, out_specs=out_specs, check_vma=False)
```

```python
import functools
import math

import jax
import jax.numpy as jnp
import ml_dtypes
import numpy as np
from jax import lax
from jax.experimental import pallas as pl
from jax.experimental.pallas import tpu as pltpu
from jax.sharding import PartitionSpec as P

CORE = 32
BUF = 4
DEG = 8

HALF_WIDTH = 4.5
FOUR_PI = 4.0 * math.pi
EXCHANGE_COEF = -((3.0 / math.pi) ** (1.0 / 3.0))


def swapped(value, axis, mask):
    pairs = [(source, source ^ mask) for source in range(lax.axis_size(axis))]
    return lax.ppermute(value, axis, pairs)


def wave_basis(length):
    cells = np.arange(length)
    rows, waves = [], []
    for wave in range(length // 2 + 1):
        angle = 2.0 * np.pi * ((wave * cells) % length) / length
        if wave in (0, length // 2):
            rows.append(np.cos(angle) / np.sqrt(length))
            waves.append(wave)
        else:
            rows.append(np.cos(angle) * np.sqrt(2.0 / length))
            rows.append(np.sin(angle) * np.sqrt(2.0 / length))
            waves += [wave, wave]
    return np.array(rows), np.array(waves)


def parity_basis():
    rows, waves = wave_basis(2 * CORE)
    return np.stack([rows[waves % 2 == 0], rows[waves % 2 == 1]]), np.stack(
        [waves[waves % 2 == 0], waves[waves % 2 == 1]]
    )


def eigenvalue(waves, length):
    return 2.0 - 2.0 * np.cos(2.0 * np.pi * waves / length)


def padded(length, unit):
    return -(-length // unit) * unit


class Packing:
    def __init__(self, side):
        self.side = side
        self.half = side // 2
        self.rows = self.half + DEG
        self.blocks = 128 // (side + 1)
        self.span = 128 // self.blocks
        self.depth = -(-self.rows // self.blocks)
        self.shape = (self.depth, side, 128)
        self.padded_shape = (self.depth, side + 16, 128)
        self.edge_groups = -(-DEG // self.blocks)
        self.pitch = padded(self.rows, 16) + 8

    def where(self, row):
        return row // self.depth, row % self.depth


def lanes_of(shape):
    return lax.broadcasted_iota(jnp.int32, shape, len(shape) - 1)


def roll(values, shift):
    return values if isinstance(shift, int) and shift % 128 == 0 else pltpu.roll(values, shift % 128, 1)


def pack(pk, flat, pitched_ref, field_ref):
    count = flat.shape[0]
    pitched_ref[...] = jnp.zeros(pitched_ref.shape, jnp.float32)
    for y in range(pk.side):
        pitched_ref[y * pk.pitch : y * pk.pitch + count, 0 : pk.side] = flat[:, y * pk.side : (y + 1) * pk.side]
    for level in range(pk.depth):
        total = None
        for block in range(pk.blocks):
            row = block * pk.depth + level
            if row < pk.rows:
                part = roll(pitched_ref[pl.ds(row, pk.side, stride=pk.pitch), :], block * pk.span)
                total = part if total is None else total + part
        field_ref[level] = total


def start_kernel(pk, slab_ref, psi_ref, pot_ref, field_ref, coef_ref, flat_ref, pitched_ref):
    half, side = pk.half, pk.side
    cells = side * side
    is_lower = slab_ref[0] == 0
    flat_ref[...] = jnp.zeros(flat_ref.shape, jnp.float32)
    own = psi_ref[:, 0, :]

    @pl.when(is_lower)
    def _():
        flat_ref[0:half] = own

    @pl.when(jnp.logical_not(is_lower))
    def _():
        flat_ref[DEG : DEG + half] = own

    pack(pk, flat_ref[...], pitched_ref, field_ref)

    @pl.when(is_lower)
    def _():
        flat_ref[0 : pk.rows] = pot_ref[0 : pk.rows] * (2.0 / HALF_WIDTH)

    @pl.when(jnp.logical_not(is_lower))
    def _():
        flat_ref[0 : pk.rows] = pot_ref[side - pk.rows : side] * (2.0 / HALF_WIDTH)

    pack(pk, flat_ref[...], pitched_ref, coef_ref)


def filtered_field(pk, first_ref, second_ref, coef_ref):
    lane = lanes_of((8, 128))
    is_cell = (lane % pk.span < pk.side) & (lane < pk.blocks * pk.span)
    full_weight = jnp.where(is_cell, 1.0 / HALF_WIDTH, 0.0)
    part_weight = jnp.where(is_cell & (lane < (pk.blocks - 1) * pk.span), 1.0 / HALF_WIDTH, 0.0)
    after_first = lane >= pk.span
    before_last = lane < (pk.blocks - 1) * pk.span
    current_ref, other_ref = first_ref, second_ref
    for order in range(DEG):
        for tile in range(pk.side // 8):
            at = 8 + 8 * tile
            values = [current_ref[level, at : at + 8, :] for level in range(pk.depth)]
            before = jnp.where(after_first, roll(values[-1], pk.span), 0.0)
            after = jnp.where(before_last, roll(values[0], -pk.span), 0.0)
            around = [before] + values + [after]
            for level in range(pk.depth):
                value = values[level]
                total = around[level] + around[level + 2]
                total = total + (
                    current_ref[level, at - 1 : at + 7, :] + current_ref[level, at + 1 : at + 9, :]
                )
                total = total + (roll(value, 1) + roll(value, -1))
                weight = full_weight if (pk.blocks - 1) * pk.depth + level < pk.rows else part_weight
                following = coef_ref[level, at - 8 : at, :] * value - weight * total
                if order == 0:
                    following = 0.5 * following
                else:
                    following = following - other_ref[level, at : at + 8, :]
                other_ref[level, at : at + 8, :] = following
        current_ref, other_ref = other_ref, current_ref
    return current_ref


def clear_margins(pk, ref):
    zeros = jnp.zeros((pk.depth, 8, 128), jnp.float32)
    ref[:, 0:8, :] = zeros
    ref[:, 8 + pk.side : 16 + pk.side, :] = zeros


def first_kernel(
    pk, bands, slab_ref, start_ref, halo_ref, coef_ref, filt_ref, edge_ref, dens_ref, one_ref, two_ref, lines_ref
):
    side, span = pk.side, pk.span
    slab = slab_ref[0]
    is_lower = slab == 0
    clear_margins(pk, one_ref)
    clear_margins(pk, two_ref)
    one_ref[:, 8 : 8 + side, :] = start_ref[...]
    halo = halo_ref[:, 0, :]
    lines_ref[...] = jnp.zeros(lines_ref.shape, jnp.float32)
    for y in range(side):
        lines_ref[y * DEG : (y + 1) * DEG, 0:side] = halo[:, y * side : (y + 1) * side]
    for row in range(DEG):
        line = lines_ref[pl.ds(row, side, stride=DEG), :]
        low_block, low_level = pk.where(pk.half + row)
        high_block, high_level = pk.where(row)
        if low_level == high_level:
            line = jnp.where(is_lower, roll(line, low_block * span), roll(line, high_block * span))
            one_ref[low_level, 8 : 8 + side, :] = one_ref[low_level, 8 : 8 + side, :] + line
        else:
            low_line = jnp.where(is_lower, roll(line, low_block * span), 0.0)
            high_line = jnp.where(is_lower, 0.0, roll(line, high_block * span))
            one_ref[low_level, 8 : 8 + side, :] = one_ref[low_level, 8 : 8 + side, :] + low_line
            one_ref[high_level, 8 : 8 + side, :] = one_ref[high_level, 8 : 8 + side, :] + high_line

    result_ref = filtered_field(pk, one_ref, two_ref, coef_ref)
    filt_ref[...] = result_ref[:, 8 : 8 + side, :]

    lane = lanes_of((side, 128))
    for group in range(pk.edge_groups):
        total = jnp.zeros((side, 128), jnp.float32)
        for slot in range(min(pk.blocks, DEG - group * pk.blocks)):
            row = group * pk.blocks + slot + jnp.where(is_lower, pk.half - DEG, DEG)
            shift = slot * span - row // pk.depth * span + 128 * pk.blocks
            line = pltpu.roll(result_ref[row % pk.depth, 8 : 8 + side, :], shift % 128, 1)
            total = jnp.where((lane >= slot * span) & (lane < slot * span + side), line, total)
        edge_ref[group * side : (group + 1) * side] = total

    lane = lanes_of((8, 128))
    lines = 128 // CORE
    for cell in range(CORE // 2):
        row = cell + jnp.where(is_lower, BUF, DEG)
        block, level = row // pk.depth, row % pk.depth
        total = jnp.zeros((8, 128), jnp.float32)
        for line in range(lines):
            value = result_ref[level, 8 + BUF + 8 * line : 16 + BUF + 8 * line, :]
            shift = line * CORE - BUF - block * span + 128 * pk.blocks
            total = jnp.where(lane // CORE == line, pltpu.roll(value, shift % 128, 1), total)
        dens_ref[cell * 8 : (cell + 1) * 8] = total * total * (1.0 / bands)


def split2(values):
    high = values.astype(jnp.bfloat16)
    return high, (values - high.astype(jnp.float32)).astype(jnp.bfloat16)


def split3(values):
    high = values.astype(jnp.bfloat16)
    rest = values - high.astype(jnp.float32)
    middle = rest.astype(jnp.bfloat16)
    return high, middle, (rest - middle.astype(jnp.float32)).astype(jnp.bfloat16)


def dot(left, right):
    return jnp.dot(left, right, preferred_element_type=jnp.float32)


def table_parts(table):
    high = table.astype(ml_dtypes.bfloat16)
    return high, (table - high.astype(np.float64)).astype(ml_dtypes.bfloat16)


def left_table(table):
    high, low = table_parts(table)
    return np.concatenate([high, low, high], -1)


def stacked(values):
    high, low = split2(values)
    return jnp.concatenate([high, high, low], 0)


@functools.lru_cache(maxsize=None)
def solver_tables(side, grid_z):
    pk = Packing(side)
    blocks_z = grid_z // CORE
    lanes = 4 * grid_z
    basis, waves = parity_basis()
    z_basis, z_waves = wave_basis(grid_z)
    lines = 128 // CORE
    into = []
    for place_z in range(blocks_z):
        along_z = z_basis[:, place_z * CORE : (place_z + 1) * CORE].T
        for place_y in range(2):
            for place_x in range(2):
                signs = [(-1.0) ** (px * place_x + py * place_y) for px in range(2) for py in range(2)]
                table = np.kron(np.eye(lines), np.concatenate([sign * along_z for sign in signs], 1))
                high, low = table_parts(table)
                into += [high, high, low]
    into = np.concatenate(into, 0)
    region = np.arange(side) - BUF
    outer = basis[:, :, region % (2 * CORE)]
    small = [left_table(np.concatenate([basis[0, :, :CORE], basis[1, :, :CORE]], 0))]
    small.append(left_table(np.concatenate([outer[0].T, outer[1].T], 0)))
    for first_row in (0, side - pk.rows):
        rows = outer[:, :, first_row : first_row + pk.rows]
        rows = np.pad(rows, ((0, 0), (0, 0), (0, padded(pk.rows, 8) - pk.rows)))
        small.append(left_table(np.concatenate([rows[0].T, rows[1].T], 0)))
    small = np.concatenate(small, 0)
    back_z = []
    spread = np.zeros((blocks_z, 3, 128, 128))
    for block in range(pk.blocks):
        start = block * pk.span
        table = np.zeros((4, grid_z, 128))
        table[:, :, start : start + side] = z_basis[:, region % grid_z]
        high, low = table_parts(table.reshape(lanes, 128))
        back_z.append(np.block([[high, low], [high, np.zeros_like(low)]]))
        for cell, pos in enumerate(region % grid_z):
            spread[pos // CORE, :, block * CORE + pos % CORE, start + cell] = 1.0
    back_z = np.concatenate(back_z, 0)
    spread = spread.reshape(blocks_z * 3 * 128, 128).astype(ml_dtypes.bfloat16)
    eigen = eigenvalue(waves, 2 * CORE)
    lam = (
        eigen.T[:, None, None, :, None]
        + eigen.T[None, :, :, None, None]
        + eigenvalue(z_waves, grid_z)[None, None, None, None, :]
    )
    lam[0, 0, 0, 0, 0] = np.inf
    factor = (FOUR_PI / lam).reshape(CORE * CORE, lanes).astype(np.float32)
    return dict(into=into, small=small, back_z=back_z, factor=factor, spread=spread)


def cube_root(values):
    positive = values > 0.0
    safe = jnp.where(positive, values, 1.0)
    root = jnp.exp(jnp.log(safe) * (1.0 / 3.0))
    root = root - (root - safe / (root * root)) * (1.0 / 3.0)
    return jnp.where(positive, root, 0.0)


def second_kernel(
    pk, masks, info_ref, near_ref, across_ref, filt_ref, beside_ref, start_coef_ref,
    into_ref, small_ref, back_z_ref, factor_ref, spread_ref,
    out_ref, cubes_ref, one_ref, two_ref, coef_ref, left_ref, rows_ref, waves_ref, mixed_ref, flat_ref,
    near_dens_ref, own_ref, lined_ref,
):
    side, half, span = pk.side, pk.half, pk.span
    slab, dom = info_ref[0], info_ref[1]
    is_lower = slab == 0
    dom_count = len(masks)
    blocks_z = dom_count // 4
    grid_z = CORE * blocks_z
    lanes = 4 * grid_z
    columns = lanes // 128
    lines = 128 // CORE
    pitch = CORE + 8
    kept = padded(pk.rows, 8)

    def offset(which, axis):
        return info_ref[2 + 3 * which + axis]

    place_of = []
    for mask in masks:
        other = dom ^ mask
        at_x = (offset(other, 0) != offset(dom, 0)).astype(jnp.int32)
        at_y = (offset(other, 1) != offset(dom, 1)).astype(jnp.int32)
        at_z = (offset(other, 2) - offset(dom, 2)) // CORE
        at_z = jnp.where(at_z < 0, at_z + blocks_z, at_z)
        place_of.append((at_z * 2 + at_y) * 2 + at_x)
    cube_at = []
    for where in range(dom_count):
        found = jnp.int32(0)
        for idx in range(dom_count):
            found = found + jnp.where(place_of[idx] == where, idx, 0)
        cube_at.append(found)

    cubes_ref[0 : dom_count // 2] = near_ref[...]
    cubes_ref[dom_count // 2 : dom_count] = across_ref[...]
    mean = jnp.sum(cubes_ref[...]) * (1.0 / (dom_count * CORE * CORE * CORE))

    for where in range(dom_count):
        high, low = split2(cubes_ref[cube_at[where]] - mean)
        for idx, piece in enumerate((high, low, high)):
            left_ref[:, (where * 3 + idx) * 128 : (where * 3 + idx + 1) * 128] = piece
    product = dot(left_ref[...], into_ref[...])
    for x in range(CORE):
        for line in range(lines):
            for col in range(columns):
                start = line * lanes + col * 128
                rows_ref[col, x * pitch + line * 8 : x * pitch + line * 8 + 8, :] = product[
                    x * 8 : (x + 1) * 8, start : start + 128
                ]

    lane = lanes_of((8, 128))
    for at_z in range(blocks_z):
        for level in range(pk.depth):
            inner, low_wrap, high_wrap = [], None, None
            for block in range(pk.blocks):
                row = block * pk.depth + level
                if row >= pk.rows:
                    continue
                x = row - BUF + jnp.where(is_lower, 0, side - pk.rows)
                inside = (x >= 0) & (x < CORE)
                cell = pl.multiple_of((x + CORE) % CORE * 8, 8)

                def source(at_y):
                    place = (at_z * 2 + at_y) * 2
                    cube = jnp.where(inside, cube_at[place], cube_at[place + 1])
                    return cubes_ref[cube, pl.ds(cell, 8), :]

                def put(value, line, total):
                    value = roll(value, (block - line) * CORE)
                    return jnp.where((lane >= block * CORE) & (lane < (block + 1) * CORE), value, total)

                own, beside = source(0), source(1)
                zeros = jnp.zeros((8, 128), jnp.float32)
                inner = inner or [zeros] * lines
                inner = [put(own, line, total) for line, total in enumerate(inner)]
                low_wrap = put(beside, lines - 1, zeros if low_wrap is None else low_wrap)
                high_wrap = put(beside, 0, zeros if high_wrap is None else high_wrap)
            base = level * side
            near_dens_ref[at_z, base : base + BUF, :] = low_wrap[8 - BUF :]
            for line in range(lines):
                near_dens_ref[at_z, base + BUF + 8 * line : base + BUF + 8 * line + 8, :] = inner[line]
            near_dens_ref[at_z, base + BUF + CORE : base + side, :] = high_wrap[:BUF]

    group = max(1, 256 // lanes)
    lane_id = lanes_of((1, group * lanes)) % lanes
    even_x = lane_id < 2 * grid_z
    even_y = (lane_id // grid_z) % 2 == 0

    def side_by_side(ref, starts, stride, count):
        pieces = []
        for start in starts:
            for col in range(columns):
                if stride == 1:
                    pieces.append(ref[col, pl.ds(start, count), :])
                else:
                    pieces.append(ref[col, pl.ds(start, count, stride=stride), :])
        return jnp.concatenate(pieces, 1)

    def scatter(ref, starts, values, count):
        for idx, start in enumerate(starts):
            for col in range(columns):
                at = (idx * columns + col) * 128
                ref[col, start : start + count, :] = values[:, at : at + 128]

    forward = small_ref[0 : 2 * CORE]
    back_y = small_ref[2 * CORE : 2 * CORE + 2 * side]
    first = 2 * CORE + 2 * side
    back_x = jnp.where(is_lower, small_ref[first : first + 2 * kept], small_ref[first + 2 * kept : first + 4 * kept])
    for first in range(0, CORE, group):
        starts = [x * pitch for x in range(first, first + group)]
        both = dot(forward, stacked(side_by_side(rows_ref, starts, 1, CORE)))
        scatter(waves_ref, starts, jnp.where(even_y, both[:CORE], both[CORE:]), CORE)

    for first in range(0, CORE, group):
        waves_y = list(range(first, first + group))
        both = dot(forward, stacked(side_by_side(waves_ref, waves_y, pitch, CORE)))
        modes = jnp.where(even_x, both[:CORE], both[CORE:])
        scale = jnp.concatenate([factor_ref[wave * CORE : (wave + 1) * CORE] for wave in waves_y], 1)
        both = dot(back_x, stacked(modes * scale))
        scatter(mixed_ref, [wave * pitch for wave in waves_y], jnp.where(even_x, both[:kept], both[kept:]), kept)

    for level in range(pk.depth):
        rows = [block * pk.depth + level for block in range(pk.blocks)]
        rows = [row for row in rows if row < pk.rows]
        for first in range(0, len(rows), group):
            taken = rows[first : first + group]
            both = dot(back_y, stacked(side_by_side(mixed_ref, taken, pitch, CORE)))
            width = both.shape[1]
            field = jnp.where(even_y[:, :width], both[:side], both[side:])
            for idx in range(len(taken)):
                flat_ref[first + idx, level * side : (level + 1) * side, :] = field[:, idx * lanes : (idx + 1) * lanes]
        for block in range(len(rows), pk.blocks):
            flat_ref[block, level * side : (level + 1) * side, :] = jnp.zeros((side, lanes), jnp.float32)

    pieces = []
    for block in range(pk.blocks):
        pieces += split2(flat_ref[block])
    product = dot(jnp.concatenate(pieces, 1), back_z_ref[...])
    hartree = product[:, 0:128] + product[:, 128:256]
    pieces = []
    for at_z in range(blocks_z):
        pieces += split3(near_dens_ref[at_z])
    density = dot(jnp.concatenate(pieces, 1), spread_ref[...])
    added = (hartree + EXCHANGE_COEF * cube_root(density)) * (2.0 / HALF_WIDTH)
    for level in range(pk.depth):
        coef_ref[level] = start_coef_ref[level] + added[level * side : (level + 1) * side]

    clear_margins(pk, one_ref)
    clear_margins(pk, two_ref)
    one_ref[:, 8 : 8 + side, :] = filt_ref[...]
    lane = lanes_of((side, 128))
    base = CORE // 2 * 8
    for row in range(DEG):
        group_at, slot = row // pk.blocks, row % pk.blocks
        line = beside_ref[base + group_at * side : base + (group_at + 1) * side, :]
        for wanted, (block, level) in ((True, pk.where(half + row)), (False, pk.where(row))):
            here = (lane >= block * span) & (lane < block * span + side) & (is_lower == wanted)
            old = one_ref[level, 8 : 8 + side, :]
            one_ref[level, 8 : 8 + side, :] = jnp.where(here, roll(line, (block - slot) * span), old)
    result_ref = filtered_field(pk, one_ref, two_ref, coef_ref)

    for row in range(half):
        at = row + jnp.where(is_lower, 0, DEG)
        shift = 128 * pk.blocks - at // pk.depth * span
        own_ref[row * side : (row + 1) * side, :] = pltpu.roll(
            result_ref[at % pk.depth, 8 : 8 + side, :], shift % 128, 1
        )
    for y in range(side):
        lined_ref[:, y * side : (y + 1) * side] = own_ref[pl.ds(y, half, stride=side), :][:, 0:side]
    out_ref[:, 0, :] = lined_ref[...]


SMEM = pl.BlockSpec(memory_space=pltpu.SMEM)
VMEM = pl.BlockSpec(memory_space=pltpu.VMEM)
params = pltpu.CompilerParams(vmem_limit_bytes=32 * 1024 * 1024)


def local(psi_in, v_in, offsets):
    band_count = lax.axis_size("band")
    dom_count = lax.axis_size("dom")
    dom_idx = lax.axis_index("dom")
    slab_idx = lax.axis_index("band") % 2
    is_lower = slab_idx == 0
    slab_scalar = slab_idx.astype(jnp.int32).reshape(1)
    side = v_in.shape[1]
    pk = Packing(side)
    half = side // 2
    cells = side * side
    bands = band_count // 2
    grid_z = CORE * dom_count // 4
    lanes = 4 * grid_z
    slab_rows = CORE // 2 * 8

    f32, bf16 = jnp.float32, jnp.bfloat16
    field_type = jax.ShapeDtypeStruct(pk.shape, f32)
    padded_field = pltpu.VMEM(pk.padded_shape, f32)

    rows = psi_in.reshape(half, 1, cells)
    halo = swapped(lax.dynamic_slice_in_dim(rows, jnp.where(is_lower, half - DEG, 0), DEG, 0), "band", 1)
    start, coef = pl.pallas_call(
        functools.partial(start_kernel, pk),
        out_shape=(field_type, field_type),
        in_specs=[SMEM, VMEM, VMEM],
        out_specs=(VMEM, VMEM),
        scratch_shapes=[pltpu.VMEM((pk.rows, cells), f32), pltpu.VMEM((side * pk.pitch, 128), f32)],
        compiler_params=params,
    )(slab_scalar, rows, v_in[0])

    filt, edge, dens = pl.pallas_call(
        functools.partial(first_kernel, pk, bands),
        out_shape=(
            field_type,
            jax.ShapeDtypeStruct((pk.edge_groups * side, 128), f32),
            jax.ShapeDtypeStruct((slab_rows, 128), f32),
        ),
        in_specs=[SMEM, VMEM, VMEM, VMEM],
        out_specs=(VMEM, VMEM, VMEM),
        scratch_shapes=[padded_field, padded_field, pltpu.VMEM((side * DEG, 128), f32)],
        compiler_params=params,
    )(slab_scalar, start, halo, coef)

    mask = 2
    while mask < band_count:
        dens = dens + swapped(dens, "band", mask)
        mask *= 2

    far = dom_count // 2
    both = ("dom", "band")
    count = dom_count * band_count

    def crossed(value, mask):
        return lax.ppermute(value, both, [(source, source ^ mask) for source in range(count)])

    beside_all = crossed(jnp.concatenate([dens, edge], 0), 1)
    beside = beside_all[:slab_rows]
    across = crossed(dens, far * band_count)
    diagonal = crossed(dens, far * band_count + 1)

    def cube_of(own, other):
        return jnp.concatenate([jnp.where(is_lower, own, other), jnp.where(is_lower, other, own)], 0)

    cubes = jnp.stack([cube_of(dens, beside), cube_of(across, diagonal)])
    masks = [0, far]
    bit = far // 2
    while bit:
        if bit > 1:
            cubes = jnp.concatenate([cubes, swapped(cubes, "dom", bit)], 0)
        masks = masks + [one | bit for one in masks]
        bit //= 2
    cubes_across = swapped(cubes, "dom", 1)

    tables = solver_tables(side, grid_z)
    names = ("into", "small", "back_z", "factor", "spread")
    info = jnp.concatenate([slab_scalar, dom_idx.astype(jnp.int32).reshape(1), offsets.reshape(-1)])
    pitch = CORE + 8
    result = pl.pallas_call(
        functools.partial(second_kernel, pk, masks),
        out_shape=jax.ShapeDtypeStruct((half, 1, cells), f32),
        in_specs=[SMEM] + [VMEM] * (5 + len(names)),
        out_specs=VMEM,
        scratch_shapes=[
            pltpu.VMEM((dom_count, CORE * 8, 128), f32),
            padded_field,
            padded_field,
            pltpu.VMEM(pk.shape, f32),
            pltpu.VMEM((CORE * 8, dom_count * 3 * 128), bf16),
            pltpu.VMEM((lanes // 128, CORE * pitch, 128), f32),
            pltpu.VMEM((lanes // 128, CORE * pitch, 128), f32),
            pltpu.VMEM((lanes // 128, CORE * pitch, 128), f32),
            pltpu.VMEM((pk.blocks, pk.depth * side, lanes), f32),
            pltpu.VMEM((dom_count // 4, pk.depth * side, 128), f32),
            pltpu.VMEM((half * side, 128), f32),
            pltpu.VMEM((half, cells), f32),
        ],
        compiler_params=params,
    )(info, cubes, cubes_across, filt, beside_all, coef, *[jnp.asarray(tables[name]) for name in names])
    return result.reshape(1, 1, half, cells)


def solution(mesh):
    in_specs = (P("dom", "band", None, None), P("dom", None, None), P())
    out_specs = P("dom", "band", None, None)
    return jax.shard_map(local, mesh=mesh, in_specs=in_specs, out_specs=out_specs, check_vma=False)
```

```python
import functools
import math

import jax
import jax.numpy as jnp
import ml_dtypes
import numpy as np
from jax import lax
from jax.experimental import pallas as pl
from jax.experimental.pallas import tpu as pltpu
from jax.sharding import PartitionSpec as P

CORE = 32
BUF = 4
DEG = 8

HALF_WIDTH = 4.5
FOUR_PI = 4.0 * math.pi
EXCHANGE_COEF = -((3.0 / math.pi) ** (1.0 / 3.0))


def swapped(value, axis, mask):
    pairs = [(source, source ^ mask) for source in range(lax.axis_size(axis))]
    return lax.ppermute(value, axis, pairs)


def wave_basis(length):
    cells = np.arange(length)
    rows, waves = [], []
    for wave in range(length // 2 + 1):
        angle = 2.0 * np.pi * ((wave * cells) % length) / length
        if wave in (0, length // 2):
            rows.append(np.cos(angle) / np.sqrt(length))
            waves.append(wave)
        else:
            rows.append(np.cos(angle) * np.sqrt(2.0 / length))
            rows.append(np.sin(angle) * np.sqrt(2.0 / length))
            waves += [wave, wave]
    return np.array(rows), np.array(waves)


def parity_basis():
    rows, waves = wave_basis(2 * CORE)
    return np.stack([rows[waves % 2 == 0], rows[waves % 2 == 1]]), np.stack(
        [waves[waves % 2 == 0], waves[waves % 2 == 1]]
    )


def eigenvalue(waves, length):
    return 2.0 - 2.0 * np.cos(2.0 * np.pi * waves / length)


def padded(length, unit):
    return -(-length // unit) * unit


class Packing:
    def __init__(self, side):
        self.side = side
        self.half = side // 2
        self.rows = self.half + DEG
        self.blocks = 128 // (side + 1)
        self.span = 128 // self.blocks
        self.depth = -(-self.rows // self.blocks)
        self.shape = (self.depth, side, 128)
        self.padded_shape = (self.depth, side + 16, 128)
        self.edge_groups = -(-DEG // self.blocks)
        self.pitch = padded(self.rows, 16) + 8

    def where(self, row):
        return row // self.depth, row % self.depth


def lanes_of(shape):
    return lax.broadcasted_iota(jnp.int32, shape, len(shape) - 1)


def roll(values, shift):
    return values if isinstance(shift, int) and shift % 128 == 0 else pltpu.roll(values, shift % 128, 1)


def pack(pk, flat, pitched_ref, field_ref):
    count = flat.shape[0]
    for y in range(pk.side):
        pitched_ref[y * pk.pitch : y * pk.pitch + count, 0 : pk.side] = flat[:, y * pk.side : (y + 1) * pk.side]
    for level in range(pk.depth):
        total = None
        for block in range(pk.blocks):
            row = block * pk.depth + level
            if row < pk.rows:
                part = roll(pitched_ref[pl.ds(row, pk.side, stride=pk.pitch), :], block * pk.span)
                total = part if total is None else total + part
        field_ref[level] = total


def edge_kernel(pk, slab_ref, psi_ref, edge_ref):
    first = jnp.where(slab_ref[0] == 0, pk.half - DEG, 0)
    edge_ref[...] = psi_ref[pl.ds(first, DEG)]


def start_kernel(pk, slab_ref, psi_ref, pot_ref, field_ref, coef_ref, flat_ref, pitched_ref):
    half, side = pk.half, pk.side
    cells = side * side
    is_lower = slab_ref[0] == 0
    flat_ref[...] = jnp.zeros(flat_ref.shape, jnp.float32)
    pitched_ref[...] = jnp.zeros(pitched_ref.shape, jnp.float32)
    own = psi_ref[:, 0, :]

    @pl.when(is_lower)
    def _():
        flat_ref[0:half] = own

    @pl.when(jnp.logical_not(is_lower))
    def _():
        flat_ref[DEG : DEG + half] = own

    pack(pk, flat_ref[...], pitched_ref, field_ref)

    @pl.when(is_lower)
    def _():
        flat_ref[0 : pk.rows] = pot_ref[0 : pk.rows] * (2.0 / HALF_WIDTH)

    @pl.when(jnp.logical_not(is_lower))
    def _():
        flat_ref[0 : pk.rows] = pot_ref[side - pk.rows : side] * (2.0 / HALF_WIDTH)

    pack(pk, flat_ref[...], pitched_ref, coef_ref)


def filtered_field(pk, first_ref, second_ref, coef_ref):
    lane = lanes_of((8, 128))
    is_cell = (lane % pk.span < pk.side) & (lane < pk.blocks * pk.span)
    full_weight = jnp.where(is_cell, 1.0 / HALF_WIDTH, 0.0)
    part_weight = jnp.where(is_cell & (lane < (pk.blocks - 1) * pk.span), 1.0 / HALF_WIDTH, 0.0)
    after_first = lane >= pk.span
    before_last = lane < (pk.blocks - 1) * pk.span
    current_ref, other_ref = first_ref, second_ref
    for order in range(DEG):
        for tile in range(pk.side // 8):
            at = 8 + 8 * tile
            values = [current_ref[level, at : at + 8, :] for level in range(pk.depth)]
            before = jnp.where(after_first, roll(values[-1], pk.span), 0.0)
            after = jnp.where(before_last, roll(values[0], -pk.span), 0.0)
            around = [before] + values + [after]
            for level in range(pk.depth):
                value = values[level]
                total = around[level] + around[level + 2]
                total = total + (
                    current_ref[level, at - 1 : at + 7, :] + current_ref[level, at + 1 : at + 9, :]
                )
                total = total + (roll(value, 1) + roll(value, -1))
                weight = full_weight if (pk.blocks - 1) * pk.depth + level < pk.rows else part_weight
                following = coef_ref[level, at - 8 : at, :] * value - weight * total
                if order == 0:
                    following = 0.5 * following
                else:
                    following = following - other_ref[level, at : at + 8, :]
                other_ref[level, at : at + 8, :] = following
        current_ref, other_ref = other_ref, current_ref
    return current_ref


def clear_margins(pk, ref):
    zeros = jnp.zeros((pk.depth, 8, 128), jnp.float32)
    ref[:, 0:8, :] = zeros
    ref[:, 8 + pk.side : 16 + pk.side, :] = zeros


def first_kernel(
    pk, bands, slab_ref, start_ref, halo_ref, coef_ref, filt_ref, edge_ref, dens_ref, one_ref, two_ref, lines_ref
):
    side, span = pk.side, pk.span
    slab = slab_ref[0]
    is_lower = slab == 0
    clear_margins(pk, one_ref)
    clear_margins(pk, two_ref)
    one_ref[:, 8 : 8 + side, :] = start_ref[...]
    halo = halo_ref[:, 0, :]
    lines_ref[...] = jnp.zeros(lines_ref.shape, jnp.float32)
    for y in range(side):
        lines_ref[y * DEG : (y + 1) * DEG, 0:side] = halo[:, y * side : (y + 1) * side]
    for row in range(DEG):
        line = lines_ref[pl.ds(row, side, stride=DEG), :]
        low_block, low_level = pk.where(pk.half + row)
        high_block, high_level = pk.where(row)
        if low_level == high_level:
            line = jnp.where(is_lower, roll(line, low_block * span), roll(line, high_block * span))
            one_ref[low_level, 8 : 8 + side, :] = one_ref[low_level, 8 : 8 + side, :] + line
        else:
            low_line = jnp.where(is_lower, roll(line, low_block * span), 0.0)
            high_line = jnp.where(is_lower, 0.0, roll(line, high_block * span))
            one_ref[low_level, 8 : 8 + side, :] = one_ref[low_level, 8 : 8 + side, :] + low_line
            one_ref[high_level, 8 : 8 + side, :] = one_ref[high_level, 8 : 8 + side, :] + high_line

    result_ref = filtered_field(pk, one_ref, two_ref, coef_ref)
    filt_ref[...] = result_ref[:, 8 : 8 + side, :]

    lane = lanes_of((side, 128))
    for group in range(pk.edge_groups):
        total = jnp.zeros((side, 128), jnp.float32)
        for slot in range(min(pk.blocks, DEG - group * pk.blocks)):
            row = group * pk.blocks + slot + jnp.where(is_lower, pk.half - DEG, DEG)
            shift = slot * span - row // pk.depth * span + 128 * pk.blocks
            line = pltpu.roll(result_ref[row % pk.depth, 8 : 8 + side, :], shift % 128, 1)
            total = jnp.where((lane >= slot * span) & (lane < slot * span + side), line, total)
        edge_ref[group * side : (group + 1) * side] = total

    lane = lanes_of((8, 128))
    lines = 128 // CORE
    for cell in range(CORE // 2):
        row = cell + jnp.where(is_lower, BUF, DEG)
        block, level = row // pk.depth, row % pk.depth
        total = jnp.zeros((8, 128), jnp.float32)
        for line in range(lines):
            value = result_ref[level, 8 + BUF + 8 * line : 16 + BUF + 8 * line, :]
            shift = line * CORE - BUF - block * span + 128 * pk.blocks
            total = jnp.where(lane // CORE == line, pltpu.roll(value, shift % 128, 1), total)
        dens_ref[cell * 8 : (cell + 1) * 8] = total * total * (1.0 / bands)


def split2(values):
    high = values.astype(jnp.bfloat16)
    return high, (values - high.astype(jnp.float32)).astype(jnp.bfloat16)


def split3(values):
    high = values.astype(jnp.bfloat16)
    rest = values - high.astype(jnp.float32)
    middle = rest.astype(jnp.bfloat16)
    return high, middle, (rest - middle.astype(jnp.float32)).astype(jnp.bfloat16)


def dot(left, right):
    return jnp.dot(left, right, preferred_element_type=jnp.float32)


def table_parts(table):
    high = table.astype(ml_dtypes.bfloat16)
    return high, (table - high.astype(np.float64)).astype(ml_dtypes.bfloat16)


def left_table(table):
    high, low = table_parts(table)
    return np.concatenate([high, low, high], -1)


def stacked(values):
    high, low = split2(values)
    return jnp.concatenate([high, high, low], 0)


@functools.lru_cache(maxsize=None)
def solver_tables(side, grid_z):
    pk = Packing(side)
    blocks_z = grid_z // CORE
    lanes = 4 * grid_z
    basis, waves = parity_basis()
    z_basis, z_waves = wave_basis(grid_z)
    lines = 128 // CORE
    into = []
    for place_z in range(blocks_z):
        along_z = z_basis[:, place_z * CORE : (place_z + 1) * CORE].T
        for place_y in range(2):
            for place_x in range(2):
                signs = [(-1.0) ** (px * place_x + py * place_y) for px in range(2) for py in range(2)]
                table = np.kron(np.eye(lines), np.concatenate([sign * along_z for sign in signs], 1))
                high, low = table_parts(table)
                into += [high, high, low]
    into = np.concatenate(into, 0)
    region = np.arange(side) - BUF
    outer = basis[:, :, region % (2 * CORE)]
    small = [left_table(np.concatenate([basis[0, :, :CORE], basis[1, :, :CORE]], 0))]
    small.append(left_table(np.concatenate([outer[0].T, outer[1].T], 0)))
    for first_row in (0, side - pk.rows):
        rows = outer[:, :, first_row : first_row + pk.rows]
        rows = np.pad(rows, ((0, 0), (0, 0), (0, padded(pk.rows, 8) - pk.rows)))
        small.append(left_table(np.concatenate([rows[0].T, rows[1].T], 0)))
    small = np.concatenate(small, 0)
    back_z = []
    spread = np.zeros((blocks_z, 3, 128, 128))
    for block in range(pk.blocks):
        start = block * pk.span
        table = np.zeros((4, grid_z, 128))
        table[:, :, start : start + side] = z_basis[:, region % grid_z]
        high, low = table_parts(table.reshape(lanes, 128))
        back_z.append(np.block([[high, low], [high, np.zeros_like(low)]]))
        for cell, pos in enumerate(region % grid_z):
            spread[pos // CORE, :, block * CORE + pos % CORE, start + cell] = 1.0
    back_z = np.concatenate(back_z, 0)
    spread = spread.reshape(blocks_z * 3 * 128, 128).astype(ml_dtypes.bfloat16)
    eigen = eigenvalue(waves, 2 * CORE)
    lam = (
        eigen.T[:, None, None, :, None]
        + eigen.T[None, :, :, None, None]
        + eigenvalue(z_waves, grid_z)[None, None, None, None, :]
    )
    lam[0, 0, 0, 0, 0] = np.inf
    factor = (FOUR_PI / lam).reshape(CORE * CORE, lanes).astype(np.float32)
    rest = np.zeros((max(len(back_z), len(spread), len(small)), into.shape[1]), ml_dtypes.bfloat16)
    rest[: len(back_z), 0:256] = back_z
    rest[: len(spread), 256:384] = spread
    rest[: len(small), 384 : 384 + small.shape[1]] = small
    return np.concatenate([into, rest], 0), factor


def cube_root(values):
    positive = values > 0.0
    safe = jnp.where(positive, values, 1.0)
    root = jnp.exp(jnp.log(safe) * (1.0 / 3.0))
    root = root - (root - safe / (root * root)) * (1.0 / 3.0)
    return jnp.where(positive, root, 0.0)


def second_kernel(
    pk, masks, slab_ref, dom_ref, info_in_ref, near_ref, across_ref, filt_ref, beside_ref, start_coef_ref,
    table_ref, factor_ref,
    out_ref, cubes_ref, one_ref, two_ref, coef_ref, left_ref, rows_ref, waves_ref, mixed_ref, flat_ref,
    near_dens_ref, own_ref, lined_ref, info_ref, sem,
):
    side, half, span = pk.side, pk.half, pk.span
    slab, dom = slab_ref[0], dom_ref[0]
    is_lower = slab == 0
    dom_count = len(masks)
    blocks_z = dom_count // 4
    grid_z = CORE * blocks_z
    lanes = 4 * grid_z
    columns = lanes // 128
    lines = 128 // CORE
    pitch = CORE + 8
    kept = padded(pk.rows, 8)

    copy = pltpu.make_async_copy(info_in_ref, info_ref, sem)
    copy.start()
    cubes_ref[0 : dom_count // 2] = near_ref[...]
    cubes_ref[dom_count // 2 : dom_count] = across_ref[...]
    mean = jnp.sum(cubes_ref[...]) * (1.0 / (dom_count * CORE * CORE * CORE))

    clear_margins(pk, one_ref)
    clear_margins(pk, two_ref)
    one_ref[:, 8 : 8 + side, :] = filt_ref[...]
    lane = lanes_of((side, 128))
    base = CORE // 2 * 8
    for row in range(DEG):
        group_at, slot = row // pk.blocks, row % pk.blocks
        line = beside_ref[base + group_at * side : base + (group_at + 1) * side, :]
        for wanted, (block, level) in ((True, pk.where(half + row)), (False, pk.where(row))):
            here = (lane >= block * span) & (lane < block * span + side) & (is_lower == wanted)
            old = one_ref[level, 8 : 8 + side, :]
            one_ref[level, 8 : 8 + side, :] = jnp.where(here, roll(line, (block - slot) * span), old)
    copy.wait()

    def offset(which, axis):
        return info_ref[3 * which + axis]

    place_of = []
    for mask in masks:
        other = dom ^ mask
        at_x = (offset(other, 0) != offset(dom, 0)).astype(jnp.int32)
        at_y = (offset(other, 1) != offset(dom, 1)).astype(jnp.int32)
        at_z = (offset(other, 2) - offset(dom, 2)) // CORE
        at_z = jnp.where(at_z < 0, at_z + blocks_z, at_z)
        place_of.append((at_z * 2 + at_y) * 2 + at_x)
    cube_at = []
    for where in range(dom_count):
        found = jnp.int32(0)
        for idx in range(dom_count):
            found = found + jnp.where(place_of[idx] == where, idx, 0)
        cube_at.append(found)

    for where in range(dom_count):
        high, low = split2(cubes_ref[cube_at[where]] - mean)
        for idx, piece in enumerate((high, low, high)):
            left_ref[:, (where * 3 + idx) * 128 : (where * 3 + idx + 1) * 128] = piece
    product = dot(left_ref[...], table_ref[0 : dom_count * 3 * 128])
    for x in range(CORE):
        for line in range(lines):
            for col in range(columns):
                start = line * lanes + col * 128
                rows_ref[col, x * pitch + line * 8 : x * pitch + line * 8 + 8, :] = product[
                    x * 8 : (x + 1) * 8, start : start + 128
                ]

    lane = lanes_of((8, 128))
    for at_z in range(blocks_z):
        for level in range(pk.depth):
            inner, low_wrap, high_wrap = [], None, None
            for block in range(pk.blocks):
                row = block * pk.depth + level
                if row >= pk.rows:
                    continue
                x = row - BUF + jnp.where(is_lower, 0, side - pk.rows)
                inside = (x >= 0) & (x < CORE)
                cell = pl.multiple_of((x + CORE) % CORE * 8, 8)

                def source(at_y):
                    place = (at_z * 2 + at_y) * 2
                    cube = jnp.where(inside, cube_at[place], cube_at[place + 1])
                    return cubes_ref[cube, pl.ds(cell, 8), :]

                def put(value, line, total):
                    value = roll(value, (block - line) * CORE)
                    return jnp.where((lane >= block * CORE) & (lane < (block + 1) * CORE), value, total)

                own, beside = source(0), source(1)
                zeros = jnp.zeros((8, 128), jnp.float32)
                inner = inner or [zeros] * lines
                inner = [put(own, line, total) for line, total in enumerate(inner)]
                low_wrap = put(beside, lines - 1, zeros if low_wrap is None else low_wrap)
                high_wrap = put(beside, 0, zeros if high_wrap is None else high_wrap)
            base = level * side
            near_dens_ref[at_z, base : base + BUF, :] = low_wrap[8 - BUF :]
            for line in range(lines):
                near_dens_ref[at_z, base + BUF + 8 * line : base + BUF + 8 * line + 8, :] = inner[line]
            near_dens_ref[at_z, base + BUF + CORE : base + side, :] = high_wrap[:BUF]

    group = max(1, 256 // lanes)
    lane_id = lanes_of((1, group * lanes)) % lanes
    even_x = lane_id < 2 * grid_z
    even_y = (lane_id // grid_z) % 2 == 0

    def side_by_side(ref, starts, stride, count):
        pieces = []
        for start in starts:
            for col in range(columns):
                if stride == 1:
                    pieces.append(ref[col, pl.ds(start, count), :])
                else:
                    pieces.append(ref[col, pl.ds(start, count, stride=stride), :])
        return jnp.concatenate(pieces, 1)

    def scatter(ref, starts, values, count):
        for idx, start in enumerate(starts):
            for col in range(columns):
                at = (idx * columns + col) * 128
                ref[col, start : start + count, :] = values[:, at : at + 128]

    base = dom_count * 3 * 128

    def small(first, count):
        return table_ref[base + first : base + first + count, 384 : 384 + 3 * CORE]

    forward = small(0, 2 * CORE)
    back_y = small(2 * CORE, 2 * side)
    first = 2 * CORE + 2 * side
    back_x = jnp.where(is_lower, small(first, 2 * kept), small(first + 2 * kept, 2 * kept))
    for first in range(0, CORE, group):
        starts = [x * pitch for x in range(first, first + group)]
        both = dot(forward, stacked(side_by_side(rows_ref, starts, 1, CORE)))
        scatter(waves_ref, starts, jnp.where(even_y, both[:CORE], both[CORE:]), CORE)

    for first in range(0, CORE, group):
        waves_y = list(range(first, first + group))
        both = dot(forward, stacked(side_by_side(waves_ref, waves_y, pitch, CORE)))
        modes = jnp.where(even_x, both[:CORE], both[CORE:])
        scale = jnp.concatenate([factor_ref[wave * CORE : (wave + 1) * CORE] for wave in waves_y], 1)
        both = dot(back_x, stacked(modes * scale))
        scatter(mixed_ref, [wave * pitch for wave in waves_y], jnp.where(even_x, both[:kept], both[kept:]), kept)

    for level in range(pk.depth):
        rows = [block * pk.depth + level for block in range(pk.blocks)]
        rows = [row for row in rows if row < pk.rows]
        for first in range(0, len(rows), group):
            taken = rows[first : first + group]
            both = dot(back_y, stacked(side_by_side(mixed_ref, taken, pitch, CORE)))
            width = both.shape[1]
            field = jnp.where(even_y[:, :width], both[:side], both[side:])
            for idx in range(len(taken)):
                flat_ref[first + idx, level * side : (level + 1) * side, :] = field[:, idx * lanes : (idx + 1) * lanes]
        for block in range(len(rows), pk.blocks):
            flat_ref[block, level * side : (level + 1) * side, :] = jnp.zeros((side, lanes), jnp.float32)

    pieces = []
    for block in range(pk.blocks):
        pieces += split2(flat_ref[block])
    product = dot(jnp.concatenate(pieces, 1), table_ref[base : base + pk.blocks * 2 * lanes, 0:256])
    hartree = product[:, 0:128] + product[:, 128:256]
    pieces = []
    for at_z in range(blocks_z):
        pieces += split3(near_dens_ref[at_z])
    density = dot(jnp.concatenate(pieces, 1), table_ref[base : base + blocks_z * 3 * 128, 256:384])
    added = (hartree + EXCHANGE_COEF * cube_root(density)) * (2.0 / HALF_WIDTH)
    for level in range(pk.depth):
        coef_ref[level] = start_coef_ref[level] + added[level * side : (level + 1) * side]

    result_ref = filtered_field(pk, one_ref, two_ref, coef_ref)

    for row in range(half):
        at = row + jnp.where(is_lower, 0, DEG)
        shift = 128 * pk.blocks - at // pk.depth * span
        own_ref[row * side : (row + 1) * side, :] = pltpu.roll(
            result_ref[at % pk.depth, 8 : 8 + side, :], shift % 128, 1
        )
    for y in range(side):
        lined_ref[:, y * side : (y + 1) * side] = own_ref[pl.ds(y, half, stride=side), :][:, 0:side]
    out_ref[:, 0, :] = lined_ref[...]


SMEM = pl.BlockSpec(memory_space=pltpu.SMEM)
VMEM = pl.BlockSpec(memory_space=pltpu.VMEM)
params = pltpu.CompilerParams(vmem_limit_bytes=32 * 1024 * 1024)


def local(psi_in, v_in, offsets):
    band_count = lax.axis_size("band")
    dom_count = lax.axis_size("dom")
    dom_idx = lax.axis_index("dom")
    slab_idx = lax.axis_index("band") % 2
    is_lower = slab_idx == 0
    slab_scalar = slab_idx.astype(jnp.int32).reshape(1)
    side = v_in.shape[1]
    pk = Packing(side)
    half = side // 2
    cells = side * side
    bands = band_count // 2
    grid_z = CORE * dom_count // 4
    lanes = 4 * grid_z
    slab_rows = CORE // 2 * 8

    f32, bf16 = jnp.float32, jnp.bfloat16
    field_type = jax.ShapeDtypeStruct(pk.shape, f32)
    padded_field = pltpu.VMEM(pk.padded_shape, f32)

    rows = psi_in.reshape(half, 1, cells)
    edge = pl.pallas_call(
        functools.partial(edge_kernel, pk),
        out_shape=jax.ShapeDtypeStruct((DEG, 1, cells), f32),
        in_specs=[SMEM, VMEM],
        out_specs=VMEM,
        compiler_params=params,
    )(slab_scalar, rows)
    halo = swapped(edge, "band", 1)
    start, coef = pl.pallas_call(
        functools.partial(start_kernel, pk),
        out_shape=(field_type, field_type),
        in_specs=[SMEM, VMEM, VMEM],
        out_specs=(VMEM, VMEM),
        scratch_shapes=[pltpu.VMEM((pk.rows, cells), f32), pltpu.VMEM((side * pk.pitch, 128), f32)],
        compiler_params=params,
    )(slab_scalar, rows, v_in[0])

    filt, edge, dens = pl.pallas_call(
        functools.partial(first_kernel, pk, bands),
        out_shape=(
            field_type,
            jax.ShapeDtypeStruct((pk.edge_groups * side, 128), f32),
            jax.ShapeDtypeStruct((slab_rows, 128), f32),
        ),
        in_specs=[SMEM, VMEM, VMEM, VMEM],
        out_specs=(VMEM, VMEM, VMEM),
        scratch_shapes=[padded_field, padded_field, pltpu.VMEM((side * DEG, 128), f32)],
        compiler_params=params,
    )(slab_scalar, start, halo, coef)

    mask = 2
    while mask < band_count:
        dens = dens + swapped(dens, "band", mask)
        mask *= 2

    far = dom_count // 2
    both = ("dom", "band")
    count = dom_count * band_count

    def crossed(value, mask):
        return lax.ppermute(value, both, [(source, source ^ mask) for source in range(count)])

    beside_all = crossed(jnp.concatenate([dens, edge], 0), 1)
    beside = beside_all[:slab_rows]
    across = crossed(dens, far * band_count)
    diagonal = crossed(dens, far * band_count + 1)

    def cube_of(own, other):
        return jnp.concatenate([jnp.where(is_lower, own, other), jnp.where(is_lower, other, own)], 0)

    cubes = jnp.stack([cube_of(dens, beside), cube_of(across, diagonal)])
    masks = [0, far]
    bit = far // 2
    while bit:
        if bit > 1:
            cubes = jnp.concatenate([cubes, swapped(cubes, "dom", bit)], 0)
        masks = masks + [one | bit for one in masks]
        bit //= 2
    cubes_across = swapped(cubes, "dom", 1)

    table, factor = solver_tables(side, grid_z)
    dom_scalar = dom_idx.astype(jnp.int32).reshape(1)
    pitch = CORE + 8
    result = pl.pallas_call(
        functools.partial(second_kernel, pk, masks),
        out_shape=jax.ShapeDtypeStruct((half, 1, cells), f32),
        in_specs=[SMEM, SMEM] + [VMEM] * 8,
        out_specs=VMEM,
        scratch_shapes=[
            pltpu.VMEM((dom_count, CORE * 8, 128), f32),
            padded_field,
            padded_field,
            pltpu.VMEM(pk.shape, f32),
            pltpu.VMEM((CORE * 8, dom_count * 3 * 128), bf16),
            pltpu.VMEM((lanes // 128, CORE * pitch, 128), f32),
            pltpu.VMEM((lanes // 128, CORE * pitch, 128), f32),
            pltpu.VMEM((lanes // 128, CORE * pitch, 128), f32),
            pltpu.VMEM((pk.blocks, pk.depth * side, lanes), f32),
            pltpu.VMEM((dom_count // 4, pk.depth * side, 128), f32),
            pltpu.VMEM((half * side, 128), f32),
            pltpu.VMEM((half, cells), f32),
            pltpu.SMEM((3 * dom_count,), jnp.int32),
            pltpu.SemaphoreType.DMA,
        ],
        compiler_params=params,
    )(
        slab_scalar, dom_scalar, offsets.reshape(-1), cubes, cubes_across, filt, beside_all, coef,
        jnp.asarray(table), jnp.asarray(factor),
    )
    return result.reshape(1, 1, half, cells)


def solution(mesh):
    in_specs = (P("dom", "band", None, None), P("dom", None, None), P())
    out_specs = P("dom", "band", None, None)
    return jax.shard_map(local, mesh=mesh, in_specs=in_specs, out_specs=out_specs, check_vma=False)
```

```python
import functools
import math

import jax
import jax.numpy as jnp
import ml_dtypes
import numpy as np
from jax import lax
from jax.experimental import pallas as pl
from jax.experimental.pallas import tpu as pltpu
from jax.sharding import PartitionSpec as P

CORE = 32
BUF = 4
DEG = 8

HALF_WIDTH = 4.5
FOUR_PI = 4.0 * math.pi
EXCHANGE_COEF = -((3.0 / math.pi) ** (1.0 / 3.0))


def swapped(value, axis, mask):
    pairs = [(source, source ^ mask) for source in range(lax.axis_size(axis))]
    return lax.ppermute(value, axis, pairs)


def wave_basis(length):
    cells = np.arange(length)
    rows, waves = [], []
    for wave in range(length // 2 + 1):
        angle = 2.0 * np.pi * ((wave * cells) % length) / length
        if wave in (0, length // 2):
            rows.append(np.cos(angle) / np.sqrt(length))
            waves.append(wave)
        else:
            rows.append(np.cos(angle) * np.sqrt(2.0 / length))
            rows.append(np.sin(angle) * np.sqrt(2.0 / length))
            waves += [wave, wave]
    return np.array(rows), np.array(waves)


def parity_basis():
    rows, waves = wave_basis(2 * CORE)
    return np.stack([rows[waves % 2 == 0], rows[waves % 2 == 1]]), np.stack(
        [waves[waves % 2 == 0], waves[waves % 2 == 1]]
    )


def eigenvalue(waves, length):
    return 2.0 - 2.0 * np.cos(2.0 * np.pi * waves / length)


def padded(length, unit):
    return -(-length // unit) * unit


class Packing:
    def __init__(self, side):
        self.side = side
        self.half = side // 2
        self.rows = self.half + DEG
        self.blocks = 128 // (side + 1)
        self.span = 128 // self.blocks
        self.depth = -(-self.rows // self.blocks)
        self.shape = (self.depth, side, 128)
        self.padded_shape = (self.depth, side + 16, 128)
        self.edge_groups = -(-DEG // self.blocks)
        self.pitch = padded(self.rows, 16) + 8

    def where(self, row):
        return row // self.depth, row % self.depth


def lanes_of(shape):
    return lax.broadcasted_iota(jnp.int32, shape, len(shape) - 1)


def roll(values, shift):
    return values if isinstance(shift, int) and shift % 128 == 0 else pltpu.roll(values, shift % 128, 1)


def pack(pk, flat, pitched_ref, field_ref):
    count = flat.shape[0]
    for y in range(pk.side):
        pitched_ref[y * pk.pitch : y * pk.pitch + count, 0 : pk.side] = flat[:, y * pk.side : (y + 1) * pk.side]
    for level in range(pk.depth):
        total = None
        for block in range(pk.blocks):
            row = block * pk.depth + level
            if row < pk.rows:
                part = roll(pitched_ref[pl.ds(row, pk.side, stride=pk.pitch), :], block * pk.span)
                total = part if total is None else total + part
        field_ref[level] = total


def edge_kernel(pk, slab_ref, psi_ref, edge_ref, own_ref, sem):
    copy = pltpu.make_async_copy(psi_ref, own_ref, sem)
    copy.start()
    first = jnp.where(slab_ref[0] == 0, pk.half - DEG, 0)
    copy.wait()
    edge_ref[...] = own_ref[pl.ds(first, DEG)]


def start_kernel(pk, slab_ref, psi_ref, pot_in_ref, field_ref, coef_ref, flat_ref, pitched_ref, pot_ref, sem):
    copy = pltpu.make_async_copy(pot_in_ref, pot_ref, sem)
    copy.start()
    half, side = pk.half, pk.side
    cells = side * side
    is_lower = slab_ref[0] == 0
    flat_ref[...] = jnp.zeros(flat_ref.shape, jnp.float32)
    pitched_ref[...] = jnp.zeros(pitched_ref.shape, jnp.float32)
    own = psi_ref[:, 0, :]

    @pl.when(is_lower)
    def _():
        flat_ref[0:half] = own

    @pl.when(jnp.logical_not(is_lower))
    def _():
        flat_ref[DEG : DEG + half] = own

    pack(pk, flat_ref[...], pitched_ref, field_ref)
    copy.wait()

    @pl.when(is_lower)
    def _():
        flat_ref[0 : pk.rows] = pot_ref[0 : pk.rows] * (2.0 / HALF_WIDTH)

    @pl.when(jnp.logical_not(is_lower))
    def _():
        flat_ref[0 : pk.rows] = pot_ref[side - pk.rows : side] * (2.0 / HALF_WIDTH)

    pack(pk, flat_ref[...], pitched_ref, coef_ref)


def filtered_field(pk, first_ref, second_ref, coef_ref):
    lane = lanes_of((8, 128))
    is_cell = (lane % pk.span < pk.side) & (lane < pk.blocks * pk.span)
    full_weight = jnp.where(is_cell, 1.0 / HALF_WIDTH, 0.0)
    part_weight = jnp.where(is_cell & (lane < (pk.blocks - 1) * pk.span), 1.0 / HALF_WIDTH, 0.0)
    after_first = lane >= pk.span
    before_last = lane < (pk.blocks - 1) * pk.span
    current_ref, other_ref = first_ref, second_ref
    for order in range(DEG):
        for tile in range(pk.side // 8):
            at = 8 + 8 * tile
            values = [current_ref[level, at : at + 8, :] for level in range(pk.depth)]
            before = jnp.where(after_first, roll(values[-1], pk.span), 0.0)
            after = jnp.where(before_last, roll(values[0], -pk.span), 0.0)
            around = [before] + values + [after]
            for level in range(pk.depth):
                value = values[level]
                total = around[level] + around[level + 2]
                total = total + (
                    current_ref[level, at - 1 : at + 7, :] + current_ref[level, at + 1 : at + 9, :]
                )
                total = total + (roll(value, 1) + roll(value, -1))
                weight = full_weight if (pk.blocks - 1) * pk.depth + level < pk.rows else part_weight
                following = coef_ref[level, at - 8 : at, :] * value - weight * total
                if order == 0:
                    following = 0.5 * following
                else:
                    following = following - other_ref[level, at : at + 8, :]
                other_ref[level, at : at + 8, :] = following
        current_ref, other_ref = other_ref, current_ref
    return current_ref


def clear_margins(pk, ref):
    zeros = jnp.zeros((pk.depth, 8, 128), jnp.float32)
    ref[:, 0:8, :] = zeros
    ref[:, 8 + pk.side : 16 + pk.side, :] = zeros


def first_kernel(
    pk, bands, slab_ref, start_ref, halo_ref, coef_ref, filt_ref, edge_ref, dens_ref, one_ref, two_ref, lines_ref
):
    side, span = pk.side, pk.span
    slab = slab_ref[0]
    is_lower = slab == 0
    clear_margins(pk, one_ref)
    clear_margins(pk, two_ref)
    one_ref[:, 8 : 8 + side, :] = start_ref[...]
    halo = halo_ref[:, 0, :]
    lines_ref[...] = jnp.zeros(lines_ref.shape, jnp.float32)
    for y in range(side):
        lines_ref[y * DEG : (y + 1) * DEG, 0:side] = halo[:, y * side : (y + 1) * side]
    for row in range(DEG):
        line = lines_ref[pl.ds(row, side, stride=DEG), :]
        low_block, low_level = pk.where(pk.half + row)
        high_block, high_level = pk.where(row)
        if low_level == high_level:
            line = jnp.where(is_lower, roll(line, low_block * span), roll(line, high_block * span))
            one_ref[low_level, 8 : 8 + side, :] = one_ref[low_level, 8 : 8 + side, :] + line
        else:
            low_line = jnp.where(is_lower, roll(line, low_block * span), 0.0)
            high_line = jnp.where(is_lower, 0.0, roll(line, high_block * span))
            one_ref[low_level, 8 : 8 + side, :] = one_ref[low_level, 8 : 8 + side, :] + low_line
            one_ref[high_level, 8 : 8 + side, :] = one_ref[high_level, 8 : 8 + side, :] + high_line

    result_ref = filtered_field(pk, one_ref, two_ref, coef_ref)
    filt_ref[...] = result_ref[:, 8 : 8 + side, :]

    lane = lanes_of((side, 128))
    for group in range(pk.edge_groups):
        total = jnp.zeros((side, 128), jnp.float32)
        for slot in range(min(pk.blocks, DEG - group * pk.blocks)):
            row = group * pk.blocks + slot + jnp.where(is_lower, pk.half - DEG, DEG)
            shift = slot * span - row // pk.depth * span + 128 * pk.blocks
            line = pltpu.roll(result_ref[row % pk.depth, 8 : 8 + side, :], shift % 128, 1)
            total = jnp.where((lane >= slot * span) & (lane < slot * span + side), line, total)
        edge_ref[group * side : (group + 1) * side] = total

    lane = lanes_of((8, 128))
    lines = 128 // CORE
    for cell in range(CORE // 2):
        row = cell + jnp.where(is_lower, BUF, DEG)
        block, level = row // pk.depth, row % pk.depth
        total = jnp.zeros((8, 128), jnp.float32)
        for line in range(lines):
            value = result_ref[level, 8 + BUF + 8 * line : 16 + BUF + 8 * line, :]
            shift = line * CORE - BUF - block * span + 128 * pk.blocks
            total = jnp.where(lane // CORE == line, pltpu.roll(value, shift % 128, 1), total)
        dens_ref[cell * 8 : (cell + 1) * 8] = total * total * (1.0 / bands)


def split2(values):
    high = values.astype(jnp.bfloat16)
    return high, (values - high.astype(jnp.float32)).astype(jnp.bfloat16)


def split3(values):
    high = values.astype(jnp.bfloat16)
    rest = values - high.astype(jnp.float32)
    middle = rest.astype(jnp.bfloat16)
    return high, middle, (rest - middle.astype(jnp.float32)).astype(jnp.bfloat16)


def dot(left, right):
    return jnp.dot(left, right, preferred_element_type=jnp.float32)


def table_parts(table):
    high = table.astype(ml_dtypes.bfloat16)
    return high, (table - high.astype(np.float64)).astype(ml_dtypes.bfloat16)


def left_table(table):
    high, low = table_parts(table)
    return np.concatenate([high, low, high], -1)


def stacked(values):
    high, low = split2(values)
    return jnp.concatenate([high, high, low], 0)


@functools.lru_cache(maxsize=None)
def solver_tables(side, grid_z):
    pk = Packing(side)
    blocks_z = grid_z // CORE
    lanes = 4 * grid_z
    basis, waves = parity_basis()
    z_basis, z_waves = wave_basis(grid_z)
    lines = 128 // CORE
    into = []
    for place_z in range(blocks_z):
        along_z = z_basis[:, place_z * CORE : (place_z + 1) * CORE].T
        high, low = table_parts(np.kron(np.eye(lines), along_z))
        into += [high, high, low]
    into = np.concatenate(into, 0)
    region = np.arange(side) - BUF
    outer = basis[:, :, region % (2 * CORE)]
    small = [left_table(np.concatenate([basis[0, :, :CORE], basis[1, :, :CORE]], 0))]
    small.append(left_table(np.concatenate([outer[0].T, outer[1].T], 0)))
    for first_row in (0, side - pk.rows):
        rows = outer[:, :, first_row : first_row + pk.rows]
        rows = np.pad(rows, ((0, 0), (0, 0), (0, padded(pk.rows, 8) - pk.rows)))
        small.append(left_table(np.concatenate([rows[0].T, rows[1].T], 0)))
    small = np.concatenate(small, 0)
    back_z = []
    spread = np.zeros((blocks_z, 3, 128, 128))
    for block in range(pk.blocks):
        start = block * pk.span
        table = np.zeros((4, grid_z, 128))
        table[:, :, start : start + side] = z_basis[:, region % grid_z]
        high, low = table_parts(table.reshape(lanes, 128))
        back_z.append(np.block([[high, low], [high, np.zeros_like(low)]]))
        for cell, pos in enumerate(region % grid_z):
            spread[pos // CORE, :, block * CORE + pos % CORE, start + cell] = 1.0
    back_z = np.concatenate(back_z, 0)
    spread = spread.reshape(blocks_z * 3 * 128, 128).astype(ml_dtypes.bfloat16)
    eigen = eigenvalue(waves, 2 * CORE)
    lam = (
        eigen.T[:, None, None, :, None]
        + eigen.T[None, :, :, None, None]
        + eigenvalue(z_waves, grid_z)[None, None, None, None, :]
    )
    lam[0, 0, 0, 0, 0] = np.inf
    factor = (FOUR_PI / lam).reshape(CORE * CORE, lanes).astype(np.float32)
    pieces = [back_z, np.concatenate([into, np.pad(spread, ((0, 0), (0, lanes - 128)))], 0), small]
    height = max(len(piece) for piece in pieces)
    pieces = [np.pad(piece, ((0, height - len(piece)), (0, -piece.shape[1] % 128))) for piece in pieces]
    return np.concatenate(pieces, 1), factor


def cube_root(values):
    positive = values > 0.0
    safe = jnp.where(positive, values, 1.0)
    root = jnp.exp(jnp.log(safe) * (1.0 / 3.0))
    root = root - (root - safe / (root * root)) * (1.0 / 3.0)
    return jnp.where(positive, root, 0.0)


def second_kernel(
    pk, masks, slab_ref, dom_ref, info_in_ref, near_ref, across_ref, filt_ref, beside_ref, start_coef_ref,
    table_ref, factor_ref,
    out_ref, cubes_ref, one_ref, two_ref, coef_ref, left_ref, rows_ref, waves_ref, mixed_ref, flat_ref,
    near_dens_ref, own_ref, lined_ref, info_ref, sem,
):
    side, half, span = pk.side, pk.half, pk.span
    slab, dom = slab_ref[0], dom_ref[0]
    is_lower = slab == 0
    dom_count = len(masks)
    blocks_z = dom_count // 4
    grid_z = CORE * blocks_z
    lanes = 4 * grid_z
    columns = lanes // 128
    lines = 128 // CORE
    pitch = CORE + 8
    kept = padded(pk.rows, 8)

    copy = pltpu.make_async_copy(info_in_ref, info_ref, sem)
    copy.start()
    cubes_ref[0 : dom_count // 2] = near_ref[...]
    cubes_ref[dom_count // 2 : dom_count] = across_ref[...]
    mean = jnp.sum(cubes_ref[...]) * (1.0 / (dom_count * CORE * CORE * CORE))

    clear_margins(pk, one_ref)
    clear_margins(pk, two_ref)
    one_ref[:, 8 : 8 + side, :] = filt_ref[...]
    lane = lanes_of((side, 128))
    base = CORE // 2 * 8
    for row in range(DEG):
        group_at, slot = row // pk.blocks, row % pk.blocks
        line = beside_ref[base + group_at * side : base + (group_at + 1) * side, :]
        for wanted, (block, level) in ((True, pk.where(half + row)), (False, pk.where(row))):
            here = (lane >= block * span) & (lane < block * span + side) & (is_lower == wanted)
            old = one_ref[level, 8 : 8 + side, :]
            one_ref[level, 8 : 8 + side, :] = jnp.where(here, roll(line, (block - slot) * span), old)
    copy.wait()

    def offset(which, axis):
        return info_ref[3 * which + axis]

    place_of = []
    for mask in masks:
        other = dom ^ mask
        at_x = (offset(other, 0) != offset(dom, 0)).astype(jnp.int32)
        at_y = (offset(other, 1) != offset(dom, 1)).astype(jnp.int32)
        at_z = (offset(other, 2) - offset(dom, 2)) // CORE
        at_z = jnp.where(at_z < 0, at_z + blocks_z, at_z)
        place_of.append((at_z * 2 + at_y) * 2 + at_x)
    cube_at = []
    for where in range(dom_count):
        found = jnp.int32(0)
        for idx in range(dom_count):
            found = found + jnp.where(place_of[idx] == where, idx, 0)
        cube_at.append(found)

    for at_z in range(blocks_z):
        near, at_x, at_y, at_xy = [cubes_ref[cube_at[at_z * 4 + place]] for place in range(4)]
        sums, others = near + at_x, at_y + at_xy
        diffs, other_diffs = near - at_x, at_y - at_xy
        parities = (sums + others - 4.0 * mean, sums - others, diffs + other_diffs, diffs - other_diffs)
        for parity, value in enumerate(parities):
            high, low = split2(value)
            for idx, piece in enumerate((high, low, high)):
                cols = slice((at_z * 3 + idx) * 128, (at_z * 3 + idx + 1) * 128)
                left_ref[parity * CORE * 8 : (parity + 1) * CORE * 8, cols] = piece
    product = dot(left_ref[...], table_ref[0 : blocks_z * 3 * 128, 256 : 256 + lanes])
    lane = lanes_of((8, 128))
    for x in range(CORE):
        for line in range(lines):
            for col in range(columns):
                total = None
                for parity in range(4):
                    into = parity * grid_z - col * 128
                    if 0 <= into < 128:
                        at = line * grid_z
                        part = product[(parity * CORE + x) * 8 : (parity * CORE + x + 1) * 8, at // 128 * 128 : at // 128 * 128 + 128]
                        part = roll(part, into - at % 128)
                        total = part if total is None else jnp.where(lane >= into, part, total)
                rows_ref[col, x * pitch + line * 8 : x * pitch + line * 8 + 8, :] = total

    lane = lanes_of((8, 128))
    for at_z in range(blocks_z):
        for level in range(pk.depth):
            inner, low_wrap, high_wrap = [], None, None
            for block in range(pk.blocks):
                row = block * pk.depth + level
                if row >= pk.rows:
                    continue
                x = row - BUF + jnp.where(is_lower, 0, side - pk.rows)
                inside = (x >= 0) & (x < CORE)
                cell = pl.multiple_of((x + CORE) % CORE * 8, 8)

                def source(at_y):
                    place = (at_z * 2 + at_y) * 2
                    cube = jnp.where(inside, cube_at[place], cube_at[place + 1])
                    return cubes_ref[cube, pl.ds(cell, 8), :]

                def put(value, line, total):
                    value = roll(value, (block - line) * CORE)
                    return jnp.where((lane >= block * CORE) & (lane < (block + 1) * CORE), value, total)

                own, beside = source(0), source(1)
                zeros = jnp.zeros((8, 128), jnp.float32)
                inner = inner or [zeros] * lines
                inner = [put(own, line, total) for line, total in enumerate(inner)]
                low_wrap = put(beside, lines - 1, zeros if low_wrap is None else low_wrap)
                high_wrap = put(beside, 0, zeros if high_wrap is None else high_wrap)
            base = level * side
            near_dens_ref[at_z, base : base + BUF, :] = low_wrap[8 - BUF :]
            for line in range(lines):
                near_dens_ref[at_z, base + BUF + 8 * line : base + BUF + 8 * line + 8, :] = inner[line]
            near_dens_ref[at_z, base + BUF + CORE : base + side, :] = high_wrap[:BUF]

    group = max(1, 256 // lanes)
    lane_id = lanes_of((1, group * lanes)) % lanes
    even_x = lane_id < 2 * grid_z
    even_y = (lane_id // grid_z) % 2 == 0

    def side_by_side(ref, starts, stride, count):
        pieces = []
        for start in starts:
            for col in range(columns):
                if stride == 1:
                    pieces.append(ref[col, pl.ds(start, count), :])
                else:
                    pieces.append(ref[col, pl.ds(start, count, stride=stride), :])
        return jnp.concatenate(pieces, 1)

    def scatter(ref, starts, values, count):
        for idx, start in enumerate(starts):
            for col in range(columns):
                at = (idx * columns + col) * 128
                ref[col, start : start + count, :] = values[:, at : at + 128]

    def small(first, count):
        return table_ref[first : first + count, 256 + lanes : 256 + lanes + 3 * CORE]

    forward = small(0, 2 * CORE)
    back_y = small(2 * CORE, 2 * side)
    first = 2 * CORE + 2 * side
    back_x = jnp.where(is_lower, small(first, 2 * kept), small(first + 2 * kept, 2 * kept))
    for first in range(0, CORE, group):
        starts = [x * pitch for x in range(first, first + group)]
        both = dot(forward, stacked(side_by_side(rows_ref, starts, 1, CORE)))
        scatter(waves_ref, starts, jnp.where(even_y, both[:CORE], both[CORE:]), CORE)

    for first in range(0, CORE, group):
        waves_y = list(range(first, first + group))
        both = dot(forward, stacked(side_by_side(waves_ref, waves_y, pitch, CORE)))
        modes = jnp.where(even_x, both[:CORE], both[CORE:])
        scale = jnp.concatenate([factor_ref[wave * CORE : (wave + 1) * CORE] for wave in waves_y], 1)
        both = dot(back_x, stacked(modes * scale))
        scatter(mixed_ref, [wave * pitch for wave in waves_y], jnp.where(even_x, both[:kept], both[kept:]), kept)

    for level in range(pk.depth):
        rows = [block * pk.depth + level for block in range(pk.blocks)]
        rows = [row for row in rows if row < pk.rows]
        for first in range(0, len(rows), group):
            taken = rows[first : first + group]
            both = dot(back_y, stacked(side_by_side(mixed_ref, taken, pitch, CORE)))
            width = both.shape[1]
            field = jnp.where(even_y[:, :width], both[:side], both[side:])
            for idx in range(len(taken)):
                flat_ref[first + idx, level * side : (level + 1) * side, :] = field[:, idx * lanes : (idx + 1) * lanes]
        for block in range(len(rows), pk.blocks):
            flat_ref[block, level * side : (level + 1) * side, :] = jnp.zeros((side, lanes), jnp.float32)

    pieces = []
    for block in range(pk.blocks):
        pieces += split2(flat_ref[block])
    product = dot(jnp.concatenate(pieces, 1), table_ref[0 : pk.blocks * 2 * lanes, 0:256])
    hartree = product[:, 0:128] + product[:, 128:256]
    pieces = []
    for at_z in range(blocks_z):
        pieces += split3(near_dens_ref[at_z])
    density = dot(jnp.concatenate(pieces, 1), table_ref[blocks_z * 3 * 128 : blocks_z * 6 * 128, 256:384])
    added = (hartree + EXCHANGE_COEF * cube_root(density)) * (2.0 / HALF_WIDTH)
    for level in range(pk.depth):
        coef_ref[level] = start_coef_ref[level] + added[level * side : (level + 1) * side]

    result_ref = filtered_field(pk, one_ref, two_ref, coef_ref)

    for row in range(half):
        at = row + jnp.where(is_lower, 0, DEG)
        shift = 128 * pk.blocks - at // pk.depth * span
        own_ref[row * side : (row + 1) * side, :] = pltpu.roll(
            result_ref[at % pk.depth, 8 : 8 + side, :], shift % 128, 1
        )
    for y in range(side):
        lined_ref[:, y * side : (y + 1) * side] = own_ref[pl.ds(y, half, stride=side), :][:, 0:side]
    out_ref[:, 0, :] = lined_ref[...]


SMEM = pl.BlockSpec(memory_space=pltpu.SMEM)
VMEM = pl.BlockSpec(memory_space=pltpu.VMEM)
HBM = pl.BlockSpec(memory_space=pltpu.HBM)
params = pltpu.CompilerParams(vmem_limit_bytes=32 * 1024 * 1024)


def in_vmem(*shape):
    return pltpu.VMEM(shape, jnp.float32)


def in_hbm(value):
    return pltpu.with_memory_space_constraint(value, pltpu.HBM)


def local(psi_in, v_in, offsets):
    band_count = lax.axis_size("band")
    dom_count = lax.axis_size("dom")
    dom_idx = lax.axis_index("dom")
    slab_idx = lax.axis_index("band") % 2
    is_lower = slab_idx == 0
    slab_scalar = slab_idx.astype(jnp.int32).reshape(1)
    side = v_in.shape[1]
    pk = Packing(side)
    half = side // 2
    cells = side * side
    bands = band_count // 2
    grid_z = CORE * dom_count // 4
    lanes = 4 * grid_z
    slab_rows = CORE // 2 * 8

    f32, bf16 = jnp.float32, jnp.bfloat16
    field_type = in_vmem(*pk.shape)
    padded_field = pltpu.VMEM(pk.padded_shape, f32)

    rows = psi_in.reshape(half, 1, cells)
    edge, rows = pl.pallas_call(
        functools.partial(edge_kernel, pk),
        out_shape=(in_vmem(DEG, 1, cells), in_vmem(half, 1, cells)),
        in_specs=[SMEM, HBM],
        out_specs=(VMEM, VMEM),
        scratch_shapes=[pltpu.SemaphoreType.DMA],
        compiler_params=params,
    )(slab_scalar, in_hbm(rows))
    halo = swapped(edge, "band", 1)
    start, coef = pl.pallas_call(
        functools.partial(start_kernel, pk),
        out_shape=(field_type, field_type),
        in_specs=[SMEM, VMEM, HBM],
        out_specs=(VMEM, VMEM),
        scratch_shapes=[
            pltpu.VMEM((pk.rows, cells), f32),
            pltpu.VMEM((side * pk.pitch, 128), f32),
            pltpu.VMEM((side, cells), f32),
            pltpu.SemaphoreType.DMA,
        ],
        compiler_params=params,
    )(slab_scalar, rows, in_hbm(v_in[0]))

    filt, edge, dens = pl.pallas_call(
        functools.partial(first_kernel, pk, bands),
        out_shape=(
            field_type,
            in_vmem(pk.edge_groups * side, 128),
            in_vmem(slab_rows, 128),
        ),
        in_specs=[SMEM, VMEM, VMEM, VMEM],
        out_specs=(VMEM, VMEM, VMEM),
        scratch_shapes=[padded_field, padded_field, pltpu.VMEM((side * DEG, 128), f32)],
        compiler_params=params,
    )(slab_scalar, start, halo, coef)

    mask = 2
    while mask < band_count:
        dens = dens + swapped(dens, "band", mask)
        mask *= 2

    far = dom_count // 2
    both = ("dom", "band")
    count = dom_count * band_count

    def crossed(value, mask):
        return lax.ppermute(value, both, [(source, source ^ mask) for source in range(count)])

    beside_all = crossed(jnp.concatenate([dens, edge], 0), 1)
    beside = beside_all[:slab_rows]
    across = crossed(dens, far * band_count)
    diagonal = crossed(dens, far * band_count + 1)

    def cube_of(own, other):
        return jnp.concatenate([jnp.where(is_lower, own, other), jnp.where(is_lower, other, own)], 0)

    cubes = jnp.stack([cube_of(dens, beside), cube_of(across, diagonal)])
    masks = [0, far]
    bit = far // 2
    while bit:
        if bit > 1:
            cubes = jnp.concatenate([cubes, swapped(cubes, "dom", bit)], 0)
        masks = masks + [one | bit for one in masks]
        bit //= 2
    cubes_across = swapped(cubes, "dom", 1)

    table, factor = solver_tables(side, grid_z)
    dom_scalar = dom_idx.astype(jnp.int32).reshape(1)
    pitch = CORE + 8
    result = pl.pallas_call(
        functools.partial(second_kernel, pk, masks),
        out_shape=jax.ShapeDtypeStruct((half, 1, cells), f32),
        in_specs=[SMEM, SMEM] + [VMEM] * 8,
        out_specs=VMEM,
        scratch_shapes=[
            pltpu.VMEM((dom_count, CORE * 8, 128), f32),
            padded_field,
            padded_field,
            pltpu.VMEM(pk.shape, f32),
            pltpu.VMEM((4 * CORE * 8, dom_count // 4 * 3 * 128), bf16),
            pltpu.VMEM((lanes // 128, CORE * pitch, 128), f32),
            pltpu.VMEM((lanes // 128, CORE * pitch, 128), f32),
            pltpu.VMEM((lanes // 128, CORE * pitch, 128), f32),
            pltpu.VMEM((pk.blocks, pk.depth * side, lanes), f32),
            pltpu.VMEM((dom_count // 4, pk.depth * side, 128), f32),
            pltpu.VMEM((half * side, 128), f32),
            pltpu.VMEM((half, cells), f32),
            pltpu.SMEM((3 * dom_count,), jnp.int32),
            pltpu.SemaphoreType.DMA,
        ],
        compiler_params=params,
    )(
        slab_scalar, dom_scalar, offsets.reshape(-1), cubes, cubes_across, filt, beside_all, coef,
        jnp.asarray(table), jnp.asarray(factor),
    )
    return result.reshape(1, 1, half, cells)


def solution(mesh):
    in_specs = (P("dom", "band", None, None), P("dom", None, None), P())
    out_specs = P("dom", "band", None, None)
    return jax.shard_map(local, mesh=mesh, in_specs=in_specs, out_specs=out_specs, check_vma=False)
```

```python
import functools
import math

import jax
import jax.numpy as jnp
import ml_dtypes
import numpy as np
from jax import lax
from jax.experimental import pallas as pl
from jax.experimental.pallas import tpu as pltpu
from jax.sharding import PartitionSpec as P

CORE = 32
BUF = 4
DEG = 8

HALF_WIDTH = 4.5
FOUR_PI = 4.0 * math.pi
EXCHANGE_COEF = -((3.0 / math.pi) ** (1.0 / 3.0))


def swapped(value, axis, mask):
    pairs = [(source, source ^ mask) for source in range(lax.axis_size(axis))]
    return lax.ppermute(value, axis, pairs)


def wave_basis(length):
    cells = np.arange(length)
    rows, waves = [], []
    for wave in range(length // 2 + 1):
        angle = 2.0 * np.pi * ((wave * cells) % length) / length
        if wave in (0, length // 2):
            rows.append(np.cos(angle) / np.sqrt(length))
            waves.append(wave)
        else:
            rows.append(np.cos(angle) * np.sqrt(2.0 / length))
            rows.append(np.sin(angle) * np.sqrt(2.0 / length))
            waves += [wave, wave]
    return np.array(rows), np.array(waves)


def parity_basis():
    rows, waves = wave_basis(2 * CORE)
    return np.stack([rows[waves % 2 == 0], rows[waves % 2 == 1]]), np.stack(
        [waves[waves % 2 == 0], waves[waves % 2 == 1]]
    )


def eigenvalue(waves, length):
    return 2.0 - 2.0 * np.cos(2.0 * np.pi * waves / length)


def padded(length, unit):
    return -(-length // unit) * unit


class Packing:
    def __init__(self, side):
        self.side = side
        self.half = side // 2
        self.rows = self.half + DEG
        self.blocks = 128 // (side + 1)
        self.span = 128 // self.blocks
        self.depth = -(-self.rows // self.blocks)
        self.shape = (self.depth, side, 128)
        self.padded_shape = (self.depth, side + 16, 128)
        self.edge_groups = -(-DEG // self.blocks)
        self.pitch = padded(self.rows, 16) + 8

    def where(self, row):
        return row // self.depth, row % self.depth


def lanes_of(shape):
    return lax.broadcasted_iota(jnp.int32, shape, len(shape) - 1)


def roll(values, shift):
    return values if isinstance(shift, int) and shift % 128 == 0 else pltpu.roll(values, shift % 128, 1)


def pack(pk, flat, pitched_ref, field_ref):
    count = flat.shape[0]
    for y in range(pk.side):
        pitched_ref[y * pk.pitch : y * pk.pitch + count, 0 : pk.side] = flat[:, y * pk.side : (y + 1) * pk.side]
    for level in range(pk.depth):
        total = None
        for block in range(pk.blocks):
            row = block * pk.depth + level
            if row < pk.rows:
                part = roll(pitched_ref[pl.ds(row, pk.side, stride=pk.pitch), :], block * pk.span)
                total = part if total is None else total + part
        field_ref[level] = total


def edge_kernel(pk, slab_ref, psi_ref, edge_ref, own_ref, sem):
    copy = pltpu.make_async_copy(psi_ref, own_ref, sem)
    copy.start()
    first = jnp.where(slab_ref[0] == 0, pk.half - DEG, 0)
    copy.wait()
    edge_ref[...] = own_ref[pl.ds(first, DEG)]


def start_kernel(
    pk, masks, slab_ref, dom_ref, psi_ref, pot_in_ref, offsets_in_ref,
    field_ref, coef_ref, code_ref, flat_ref, pitched_ref, pot_ref, offsets_ref, sems,
):
    copy = pltpu.make_async_copy(pot_in_ref, pot_ref, sems.at[0])
    offsets_copy = pltpu.make_async_copy(offsets_in_ref, offsets_ref, sems.at[1])
    copy.start()
    offsets_copy.start()
    half, side = pk.half, pk.side
    cells = side * side
    is_lower = slab_ref[0] == 0
    flat_ref[...] = jnp.zeros(flat_ref.shape, jnp.float32)
    pitched_ref[...] = jnp.zeros(pitched_ref.shape, jnp.float32)
    own = psi_ref[:, 0, :]

    @pl.when(is_lower)
    def _():
        flat_ref[0:half] = own

    @pl.when(jnp.logical_not(is_lower))
    def _():
        flat_ref[DEG : DEG + half] = own

    pack(pk, flat_ref[...], pitched_ref, field_ref)
    copy.wait()

    @pl.when(is_lower)
    def _():
        flat_ref[0 : pk.rows] = pot_ref[0 : pk.rows] * (2.0 / HALF_WIDTH)

    @pl.when(jnp.logical_not(is_lower))
    def _():
        flat_ref[0 : pk.rows] = pot_ref[side - pk.rows : side] * (2.0 / HALF_WIDTH)

    pack(pk, flat_ref[...], pitched_ref, coef_ref)

    offsets_copy.wait()
    dom, dom_count = dom_ref[0], len(masks)
    blocks_z = dom_count // 4
    code = jnp.int32(0)
    for idx, mask in enumerate(masks):
        other = dom ^ mask
        at_x = (offsets_ref[other, 0] != offsets_ref[dom, 0]).astype(jnp.int32)
        at_y = (offsets_ref[other, 1] != offsets_ref[dom, 1]).astype(jnp.int32)
        at_z = (offsets_ref[other, 2] - offsets_ref[dom, 2]) // CORE
        at_z = jnp.where(at_z < 0, at_z + blocks_z, at_z)
        place = (at_z * 2 + at_y) * 2 + at_x
        for where in range(dom_count):
            code = code + jnp.where(place == where, idx * dom_count**where, 0)
    code_ref[...] = jnp.full(code_ref.shape, code.astype(jnp.float32))


def filtered_field(pk, start_ref, one_ref, two_ref, coef_ref):
    lane = lanes_of((8, 128))
    is_cell = (lane % pk.span < pk.side) & (lane < pk.blocks * pk.span)
    full_weight = jnp.where(is_cell, 1.0 / HALF_WIDTH, 0.0)
    part_weight = jnp.where(is_cell & (lane < (pk.blocks - 1) * pk.span), 1.0 / HALF_WIDTH, 0.0)
    after_first = lane >= pk.span
    before_last = lane < (pk.blocks - 1) * pk.span
    previous_ref, current_ref = None, start_ref
    for order in range(DEG):
        target_ref = (one_ref, two_ref)[order % 2]
        for tile in range(pk.side // 8):
            at = 8 + 8 * tile
            values = [current_ref[level, at : at + 8, :] for level in range(pk.depth)]
            before = jnp.where(after_first, roll(values[-1], pk.span), 0.0)
            after = jnp.where(before_last, roll(values[0], -pk.span), 0.0)
            around = [before] + values + [after]
            for level in range(pk.depth):
                value = values[level]
                total = around[level] + around[level + 2]
                total = total + (
                    current_ref[level, at - 1 : at + 7, :] + current_ref[level, at + 1 : at + 9, :]
                )
                total = total + (roll(value, 1) + roll(value, -1))
                weight = full_weight if (pk.blocks - 1) * pk.depth + level < pk.rows else part_weight
                following = coef_ref[level, at - 8 : at, :] * value - weight * total
                if order == 0:
                    following = 0.5 * following
                else:
                    following = following - previous_ref[level, at : at + 8, :]
                target_ref[level, at : at + 8, :] = following
        previous_ref, current_ref = current_ref, target_ref


def clear_margins(pk, ref):
    zeros = jnp.zeros((pk.depth, 8, 128), jnp.float32)
    ref[:, 0:8, :] = zeros
    ref[:, 8 + pk.side : 16 + pk.side, :] = zeros


def first_kernel(
    pk, bands, slab_ref, start_ref, halo_ref, coef_ref, filt_ref, dens_ref, field_ref, one_ref, lines_ref
):
    side, span = pk.side, pk.span
    slab = slab_ref[0]
    is_lower = slab == 0
    clear_margins(pk, field_ref)
    clear_margins(pk, one_ref)
    clear_margins(pk, filt_ref)
    field_ref[:, 8 : 8 + side, :] = start_ref[...]
    halo = halo_ref[:, 0, :]
    lines_ref[...] = jnp.zeros(lines_ref.shape, jnp.float32)
    for y in range(side):
        lines_ref[y * DEG : (y + 1) * DEG, 0:side] = halo[:, y * side : (y + 1) * side]
    for row in range(DEG):
        line = lines_ref[pl.ds(row, side, stride=DEG), :]
        low_block, low_level = pk.where(pk.half + row)
        high_block, high_level = pk.where(row)
        if low_level == high_level:
            line = jnp.where(is_lower, roll(line, low_block * span), roll(line, high_block * span))
            field_ref[low_level, 8 : 8 + side, :] = field_ref[low_level, 8 : 8 + side, :] + line
        else:
            low_line = jnp.where(is_lower, roll(line, low_block * span), 0.0)
            high_line = jnp.where(is_lower, 0.0, roll(line, high_block * span))
            field_ref[low_level, 8 : 8 + side, :] = field_ref[low_level, 8 : 8 + side, :] + low_line
            field_ref[high_level, 8 : 8 + side, :] = field_ref[high_level, 8 : 8 + side, :] + high_line

    filtered_field(pk, field_ref, one_ref, filt_ref, coef_ref)
    result_ref = filt_ref

    lane = lanes_of((8, 128))
    lines = 128 // CORE
    for cell in range(CORE // 2):
        row = cell + jnp.where(is_lower, BUF, DEG)
        block, level = row // pk.depth, row % pk.depth
        total = jnp.zeros((8, 128), jnp.float32)
        for line in range(lines):
            value = result_ref[level, 8 + BUF + 8 * line : 16 + BUF + 8 * line, :]
            shift = line * CORE - BUF - block * span + 128 * pk.blocks
            total = jnp.where(lane // CORE == line, pltpu.roll(value, shift % 128, 1), total)
        dens_ref[cell * 8 : (cell + 1) * 8] = total * total * (1.0 / bands)


def send_kernel(pk, slab_ref, result_ref, edge_ref):
    side, span = pk.side, pk.span
    is_lower = slab_ref[0] == 0
    lane = lanes_of((side, 128))
    for group in range(pk.edge_groups):
        total = jnp.zeros((side, 128), jnp.float32)
        for slot in range(min(pk.blocks, DEG - group * pk.blocks)):
            row = group * pk.blocks + slot + jnp.where(is_lower, pk.half - DEG, DEG)
            shift = slot * span - row // pk.depth * span + 128 * pk.blocks
            line = pltpu.roll(result_ref[row % pk.depth, 8 : 8 + side, :], shift % 128, 1)
            total = jnp.where((lane >= slot * span) & (lane < slot * span + side), line, total)
        edge_ref[group * side : (group + 1) * side] = total


def take_kernel(pk, slab_ref, filt_ref, beside_ref, field_ref):
    side, span, half = pk.side, pk.span, pk.half
    is_lower = slab_ref[0] == 0
    field_ref[...] = filt_ref[...]
    lane = lanes_of((side, 128))
    base = CORE // 2 * 8
    for row in range(DEG):
        group_at, slot = row // pk.blocks, row % pk.blocks
        line = beside_ref[base + group_at * side : base + (group_at + 1) * side, :]
        for wanted, (block, level) in ((True, pk.where(half + row)), (False, pk.where(row))):
            here = (lane >= block * span) & (lane < block * span + side) & (is_lower == wanted)
            old = field_ref[level, 8 : 8 + side, :]
            field_ref[level, 8 : 8 + side, :] = jnp.where(here, roll(line, (block - slot) * span), old)


def split2(values):
    high = values.astype(jnp.bfloat16)
    return high, (values - high.astype(jnp.float32)).astype(jnp.bfloat16)


def split3(values):
    high = values.astype(jnp.bfloat16)
    rest = values - high.astype(jnp.float32)
    middle = rest.astype(jnp.bfloat16)
    return high, middle, (rest - middle.astype(jnp.float32)).astype(jnp.bfloat16)


def dot(left, right):
    return jnp.dot(left, right, preferred_element_type=jnp.float32)


def table_parts(table):
    high = table.astype(ml_dtypes.bfloat16)
    return high, (table - high.astype(np.float64)).astype(ml_dtypes.bfloat16)


def left_table(table):
    high, low = table_parts(table)
    return np.concatenate([high, low, high], -1)


def stacked(values):
    high, low = split2(values)
    return jnp.concatenate([high, high, low], 0)


@functools.lru_cache(maxsize=None)
def solver_tables(side, grid_z):
    pk = Packing(side)
    blocks_z = grid_z // CORE
    lanes = 4 * grid_z
    basis, waves = parity_basis()
    z_basis, z_waves = wave_basis(grid_z)
    lines = 128 // CORE
    into = []
    for place_z in range(blocks_z):
        along_z = z_basis[:, place_z * CORE : (place_z + 1) * CORE].T
        high, low = table_parts(np.kron(np.eye(lines), along_z))
        into += [high, high, low]
    into = np.concatenate(into, 0)
    region = np.arange(side) - BUF
    outer = basis[:, :, region % (2 * CORE)]
    small = [left_table(np.concatenate([basis[0, :, :CORE], basis[1, :, :CORE]], 0))]
    small.append(left_table(np.concatenate([outer[0].T, outer[1].T], 0)))
    for first_row in (0, side - pk.rows):
        rows = outer[:, :, first_row : first_row + pk.rows]
        rows = np.pad(rows, ((0, 0), (0, 0), (0, padded(pk.rows, 8) - pk.rows)))
        small.append(left_table(np.concatenate([rows[0].T, rows[1].T], 0)))
    small = np.concatenate(small, 0)
    back_z = []
    spread = np.zeros((blocks_z, 3, 128, 128))
    for block in range(pk.blocks):
        start = block * pk.span
        table = np.zeros((4, grid_z, 128))
        table[:, :, start : start + side] = z_basis[:, region % grid_z]
        high, low = table_parts(table.reshape(lanes, 128))
        back_z.append(np.block([[high, low], [high, np.zeros_like(low)]]))
        for cell, pos in enumerate(region % grid_z):
            spread[pos // CORE, :, block * CORE + pos % CORE, start + cell] = 1.0
    back_z = np.concatenate(back_z, 0)
    spread = spread.reshape(blocks_z * 3 * 128, 128).astype(ml_dtypes.bfloat16)
    eigen = eigenvalue(waves, 2 * CORE)
    lam = (
        eigen.T[:, None, None, :, None]
        + eigen.T[None, :, :, None, None]
        + eigenvalue(z_waves, grid_z)[None, None, None, None, :]
    )
    lam[0, 0, 0, 0, 0] = np.inf
    factor = (FOUR_PI / lam).reshape(CORE * CORE, lanes).astype(np.float32)
    pieces = [back_z, np.concatenate([into, np.pad(spread, ((0, 0), (0, lanes - 128)))], 0), small]
    height = max(len(piece) for piece in pieces)
    pieces = [np.pad(piece, ((0, height - len(piece)), (0, -piece.shape[1] % 128))) for piece in pieces]
    return np.concatenate(pieces, 1), factor


def cube_root(values):
    positive = values > 0.0
    safe = jnp.where(positive, values, 1.0)
    root = jnp.exp(jnp.log(safe) * (1.0 / 3.0))
    root = root - (root - safe / (root * root)) * (1.0 / 3.0)
    return jnp.where(positive, root, 0.0)


def second_kernel(
    pk, dom_count, slab_ref, code_ref, near_ref, across_ref, field_ref, start_coef_ref,
    table_ref, factor_ref,
    out_ref, cubes_ref, one_ref, two_ref, coef_ref, left_ref, rows_ref, waves_ref, mixed_ref, flat_ref,
    near_dens_ref, own_ref,
):
    side, half, span = pk.side, pk.half, pk.span
    is_lower = slab_ref[0] == 0
    blocks_z = dom_count // 4
    grid_z = CORE * blocks_z
    lanes = 4 * grid_z
    columns = lanes // 128
    lines = 128 // CORE
    pitch = CORE + 8
    kept = padded(pk.rows, 8)

    cubes_ref[0 : dom_count // 2] = near_ref[...]
    cubes_ref[dom_count // 2 : dom_count] = across_ref[...]
    mean = jnp.sum(cubes_ref[...]) * (1.0 / (dom_count * CORE * CORE * CORE))

    code = jnp.max(code_ref[...]).astype(jnp.int32)
    cube_at = [code // dom_count**where % dom_count for where in range(dom_count)]

    for at_z in range(blocks_z):
        near, at_x, at_y, at_xy = [cubes_ref[cube_at[at_z * 4 + place]] for place in range(4)]
        sums, others = near + at_x, at_y + at_xy
        diffs, other_diffs = near - at_x, at_y - at_xy
        parities = (sums + others - 4.0 * mean, sums - others, diffs + other_diffs, diffs - other_diffs)
        for parity, value in enumerate(parities):
            high, low = split2(value)
            for idx, piece in enumerate((high, low, high)):
                cols = slice((at_z * 3 + idx) * 128, (at_z * 3 + idx + 1) * 128)
                left_ref[parity * CORE * 8 : (parity + 1) * CORE * 8, cols] = piece
    product = dot(left_ref[...], table_ref[0 : blocks_z * 3 * 128, 256 : 256 + lanes])
    lane = lanes_of((8, 128))
    for x in range(CORE):
        for line in range(lines):
            for col in range(columns):
                total = None
                for parity in range(4):
                    into = parity * grid_z - col * 128
                    if 0 <= into < 128:
                        at = line * grid_z
                        part = product[(parity * CORE + x) * 8 : (parity * CORE + x + 1) * 8, at // 128 * 128 : at // 128 * 128 + 128]
                        part = roll(part, into - at % 128)
                        total = part if total is None else jnp.where(lane >= into, part, total)
                rows_ref[col, x * pitch + line * 8 : x * pitch + line * 8 + 8, :] = total

    lane = lanes_of((8, 128))
    for at_z in range(blocks_z):
        for level in range(pk.depth):
            inner, low_wrap, high_wrap = [], None, None
            for block in range(pk.blocks):
                row = block * pk.depth + level
                if row >= pk.rows:
                    continue
                x = row - BUF + jnp.where(is_lower, 0, side - pk.rows)
                inside = (x >= 0) & (x < CORE)
                cell = pl.multiple_of((x + CORE) % CORE * 8, 8)

                def source(at_y):
                    place = (at_z * 2 + at_y) * 2
                    cube = jnp.where(inside, cube_at[place], cube_at[place + 1])
                    return cubes_ref[cube, pl.ds(cell, 8), :]

                def put(value, line, total):
                    value = roll(value, (block - line) * CORE)
                    return jnp.where((lane >= block * CORE) & (lane < (block + 1) * CORE), value, total)

                own, beside = source(0), source(1)
                zeros = jnp.zeros((8, 128), jnp.float32)
                inner = inner or [zeros] * lines
                inner = [put(own, line, total) for line, total in enumerate(inner)]
                low_wrap = put(beside, lines - 1, zeros if low_wrap is None else low_wrap)
                high_wrap = put(beside, 0, zeros if high_wrap is None else high_wrap)
            base = level * side
            near_dens_ref[at_z, base : base + BUF, :] = low_wrap[8 - BUF :]
            for line in range(lines):
                near_dens_ref[at_z, base + BUF + 8 * line : base + BUF + 8 * line + 8, :] = inner[line]
            near_dens_ref[at_z, base + BUF + CORE : base + side, :] = high_wrap[:BUF]

    group = max(1, 256 // lanes)
    lane_id = lanes_of((1, group * lanes)) % lanes
    even_x = lane_id < 2 * grid_z
    even_y = (lane_id // grid_z) % 2 == 0

    def side_by_side(ref, starts, stride, count):
        pieces = []
        for start in starts:
            for col in range(columns):
                if stride == 1:
                    pieces.append(ref[col, pl.ds(start, count), :])
                else:
                    pieces.append(ref[col, pl.ds(start, count, stride=stride), :])
        return jnp.concatenate(pieces, 1)

    def scatter(ref, starts, values, count):
        for idx, start in enumerate(starts):
            for col in range(columns):
                at = (idx * columns + col) * 128
                ref[col, start : start + count, :] = values[:, at : at + 128]

    def small(first, count):
        return table_ref[first : first + count, 256 + lanes : 256 + lanes + 3 * CORE]

    forward = small(0, 2 * CORE)
    back_y = small(2 * CORE, 2 * side)
    first = 2 * CORE + 2 * side
    back_x = jnp.where(is_lower, small(first, 2 * kept), small(first + 2 * kept, 2 * kept))
    for first in range(0, CORE, group):
        starts = [x * pitch for x in range(first, first + group)]
        both = dot(forward, stacked(side_by_side(rows_ref, starts, 1, CORE)))
        scatter(waves_ref, starts, jnp.where(even_y, both[:CORE], both[CORE:]), CORE)

    for first in range(0, CORE, group):
        waves_y = list(range(first, first + group))
        both = dot(forward, stacked(side_by_side(waves_ref, waves_y, pitch, CORE)))
        modes = jnp.where(even_x, both[:CORE], both[CORE:])
        scale = jnp.concatenate([factor_ref[wave * CORE : (wave + 1) * CORE] for wave in waves_y], 1)
        both = dot(back_x, stacked(modes * scale))
        scatter(mixed_ref, [wave * pitch for wave in waves_y], jnp.where(even_x, both[:kept], both[kept:]), kept)

    for level in range(pk.depth):
        rows = [block * pk.depth + level for block in range(pk.blocks)]
        rows = [row for row in rows if row < pk.rows]
        for first in range(0, len(rows), group):
            taken = rows[first : first + group]
            both = dot(back_y, stacked(side_by_side(mixed_ref, taken, pitch, CORE)))
            width = both.shape[1]
            field = jnp.where(even_y[:, :width], both[:side], both[side:])
            for idx in range(len(taken)):
                flat_ref[first + idx, level * side : (level + 1) * side, :] = field[:, idx * lanes : (idx + 1) * lanes]
        for block in range(len(rows), pk.blocks):
            flat_ref[block, level * side : (level + 1) * side, :] = jnp.zeros((side, lanes), jnp.float32)

    pieces = []
    for block in range(pk.blocks):
        pieces += split2(flat_ref[block])
    product = dot(jnp.concatenate(pieces, 1), table_ref[0 : pk.blocks * 2 * lanes, 0:256])
    hartree = product[:, 0:128] + product[:, 128:256]
    pieces = []
    for at_z in range(blocks_z):
        pieces += split3(near_dens_ref[at_z])
    density = dot(jnp.concatenate(pieces, 1), table_ref[blocks_z * 3 * 128 : blocks_z * 6 * 128, 256:384])
    added = (hartree + EXCHANGE_COEF * cube_root(density)) * (2.0 / HALF_WIDTH)
    for level in range(pk.depth):
        coef_ref[level] = start_coef_ref[level] + added[level * side : (level + 1) * side]

    clear_margins(pk, one_ref)
    clear_margins(pk, two_ref)
    filtered_field(pk, field_ref, one_ref, two_ref, coef_ref)

    for row in range(half):
        at = row + jnp.where(is_lower, 0, DEG)
        shift = 128 * pk.blocks - at // pk.depth * span
        own_ref[row * side : (row + 1) * side, :] = pltpu.roll(
            two_ref[at % pk.depth, 8 : 8 + side, :], shift % 128, 1
        )
    cells = side * side
    parts = [roll(own_ref[pl.ds(y, half, stride=side), :], y * side) for y in range(side)]
    for tile in range(-(-cells // 128)):
        first, last = tile * 128 // side, min(side - 1, (tile * 128 + 127) // side)
        lane = lanes_of((half, 128)) + tile * 128
        total = None
        for y in range(first, last + 1):
            total = parts[y] if total is None else jnp.where(lane >= y * side, parts[y], total)
        width = min(128, cells - tile * 128)
        out_ref[:, 0, tile * 128 : tile * 128 + width] = total[:, :width]


SMEM = pl.BlockSpec(memory_space=pltpu.SMEM)
VMEM = pl.BlockSpec(memory_space=pltpu.VMEM)
HBM = pl.BlockSpec(memory_space=pltpu.HBM)
params = pltpu.CompilerParams(vmem_limit_bytes=32 * 1024 * 1024)


def in_vmem(*shape):
    return pltpu.VMEM(shape, jnp.float32)


def in_hbm(value):
    return pltpu.with_memory_space_constraint(value, pltpu.HBM)


def local(psi_in, v_in, offsets):
    band_count = lax.axis_size("band")
    dom_count = lax.axis_size("dom")
    dom_idx = lax.axis_index("dom")
    slab_idx = lax.axis_index("band") % 2
    is_lower = slab_idx == 0
    slab_scalar = slab_idx.astype(jnp.int32).reshape(1)
    side = v_in.shape[1]
    pk = Packing(side)
    half = side // 2
    cells = side * side
    bands = band_count // 2
    grid_z = CORE * dom_count // 4
    lanes = 4 * grid_z
    slab_rows = CORE // 2 * 8

    f32, bf16 = jnp.float32, jnp.bfloat16
    field_type = in_vmem(*pk.shape)
    padded_field = pltpu.VMEM(pk.padded_shape, f32)

    rows = psi_in.reshape(half, 1, cells)
    edge, rows = pl.pallas_call(
        functools.partial(edge_kernel, pk),
        out_shape=(in_vmem(DEG, 1, cells), in_vmem(half, 1, cells)),
        in_specs=[SMEM, HBM],
        out_specs=(VMEM, VMEM),
        scratch_shapes=[pltpu.SemaphoreType.DMA],
        compiler_params=params,
    )(slab_scalar, in_hbm(rows))
    halo = swapped(edge, "band", 1)
    masks = [0]
    bit = dom_count // 2
    while bit:
        masks = masks + [one | bit for one in masks]
        bit //= 2
    dom_scalar = dom_idx.astype(jnp.int32).reshape(1)
    start, coef, code = pl.pallas_call(
        functools.partial(start_kernel, pk, masks),
        out_shape=(field_type, field_type, in_vmem(8, 128)),
        in_specs=[SMEM, SMEM, VMEM, HBM, HBM],
        out_specs=(VMEM, VMEM, VMEM),
        scratch_shapes=[
            pltpu.VMEM((pk.rows, cells), f32),
            pltpu.VMEM((side * pk.pitch, 128), f32),
            pltpu.VMEM((side, cells), f32),
            pltpu.SMEM((dom_count, 3), jnp.int32),
            pltpu.SemaphoreType.DMA((2,)),
        ],
        compiler_params=params,
    )(slab_scalar, dom_scalar, rows, in_hbm(v_in[0]), in_hbm(offsets))

    padded_type = in_vmem(*pk.padded_shape)
    filt, dens = pl.pallas_call(
        functools.partial(first_kernel, pk, bands),
        out_shape=(padded_type, in_vmem(slab_rows, 128)),
        in_specs=[SMEM, VMEM, VMEM, VMEM],
        out_specs=(VMEM, VMEM),
        scratch_shapes=[padded_field, padded_field, pltpu.VMEM((side * DEG, 128), f32)],
        compiler_params=params,
    )(slab_scalar, start, halo, coef)
    edge = pl.pallas_call(
        functools.partial(send_kernel, pk),
        out_shape=in_vmem(pk.edge_groups * side, 128),
        in_specs=[SMEM, VMEM],
        out_specs=VMEM,
        compiler_params=params,
    )(slab_scalar, filt)

    mask = 2
    while mask < band_count:
        dens = dens + swapped(dens, "band", mask)
        mask *= 2

    far = dom_count // 2
    both = ("dom", "band")
    count = dom_count * band_count

    def crossed(value, mask):
        return lax.ppermute(value, both, [(source, source ^ mask) for source in range(count)])

    beside_all = crossed(jnp.concatenate([dens, edge], 0), 1)
    beside = beside_all[:slab_rows]
    across = crossed(dens, far * band_count)
    diagonal = crossed(dens, far * band_count + 1)

    def cube_of(own, other):
        return jnp.concatenate([jnp.where(is_lower, own, other), jnp.where(is_lower, other, own)], 0)

    cubes = jnp.stack([cube_of(dens, beside), cube_of(across, diagonal)])
    bit = far // 2
    while bit:
        if bit > 1:
            cubes = jnp.concatenate([cubes, swapped(cubes, "dom", bit)], 0)
        bit //= 2
    cubes_across = swapped(cubes, "dom", 1)

    field = pl.pallas_call(
        functools.partial(take_kernel, pk),
        out_shape=padded_type,
        in_specs=[SMEM, VMEM, VMEM],
        out_specs=VMEM,
        compiler_params=params,
    )(slab_scalar, filt, beside_all)
    table, factor = solver_tables(side, grid_z)
    pitch = CORE + 8
    result = pl.pallas_call(
        functools.partial(second_kernel, pk, dom_count),
        out_shape=jax.ShapeDtypeStruct((half, 1, cells), f32),
        in_specs=[SMEM] + [VMEM] * 7,
        out_specs=VMEM,
        scratch_shapes=[
            pltpu.VMEM((dom_count, CORE * 8, 128), f32),
            padded_field,
            padded_field,
            pltpu.VMEM(pk.shape, f32),
            pltpu.VMEM((4 * CORE * 8, dom_count // 4 * 3 * 128), bf16),
            pltpu.VMEM((lanes // 128, CORE * pitch, 128), f32),
            pltpu.VMEM((lanes // 128, CORE * pitch, 128), f32),
            pltpu.VMEM((lanes // 128, CORE * pitch, 128), f32),
            pltpu.VMEM((pk.blocks, pk.depth * side, lanes), f32),
            pltpu.VMEM((dom_count // 4, pk.depth * side, 128), f32),
            pltpu.VMEM((half * side, 128), f32),
        ],
        compiler_params=params,
    )(
        slab_scalar, code, cubes, cubes_across, field, coef,
        jnp.asarray(table), jnp.asarray(factor),
    )
    return result.reshape(1, 1, half, cells)


def solution(mesh):
    in_specs = (P("dom", "band", None, None), P("dom", None, None), P())
    out_specs = P("dom", "band", None, None)
    return jax.shard_map(local, mesh=mesh, in_specs=in_specs, out_specs=out_specs, check_vma=False)
```

```python
import functools
import math

import jax
import jax.numpy as jnp
import ml_dtypes
import numpy as np
from jax import lax
from jax.experimental import pallas as pl
from jax.experimental.pallas import tpu as pltpu
from jax.sharding import PartitionSpec as P

CORE = 32
BUF = 4
DEG = 8

HALF_WIDTH = 4.5
FOUR_PI = 4.0 * math.pi
EXCHANGE_COEF = -((3.0 / math.pi) ** (1.0 / 3.0))


def swapped(value, axis, mask):
    pairs = [(source, source ^ mask) for source in range(lax.axis_size(axis))]
    return lax.ppermute(value, axis, pairs)


def wave_basis(length):
    cells = np.arange(length)
    rows, waves = [], []
    for wave in range(length // 2 + 1):
        angle = 2.0 * np.pi * ((wave * cells) % length) / length
        if wave in (0, length // 2):
            rows.append(np.cos(angle) / np.sqrt(length))
            waves.append(wave)
        else:
            rows.append(np.cos(angle) * np.sqrt(2.0 / length))
            rows.append(np.sin(angle) * np.sqrt(2.0 / length))
            waves += [wave, wave]
    return np.array(rows), np.array(waves)


def parity_basis():
    rows, waves = wave_basis(2 * CORE)
    return np.stack([rows[waves % 2 == 0], rows[waves % 2 == 1]]), np.stack(
        [waves[waves % 2 == 0], waves[waves % 2 == 1]]
    )


def eigenvalue(waves, length):
    return 2.0 - 2.0 * np.cos(2.0 * np.pi * waves / length)


def padded(length, unit):
    return -(-length // unit) * unit


class Packing:
    def __init__(self, side):
        self.side = side
        self.half = side // 2
        self.rows = self.half + DEG
        self.blocks = 128 // (side + 1)
        self.span = 128 // self.blocks
        self.depth = -(-self.rows // self.blocks)
        self.shape = (self.depth, side, 128)
        self.padded_shape = (self.depth, side + 16, 128)
        self.edge_groups = -(-DEG // self.blocks)
        self.pitch = padded(self.rows, 16) + 8

    def where(self, row):
        return row // self.depth, row % self.depth


def lanes_of(shape):
    return lax.broadcasted_iota(jnp.int32, shape, len(shape) - 1)


def roll(values, shift):
    return values if isinstance(shift, int) and shift % 128 == 0 else pltpu.roll(values, shift % 128, 1)


def pack(pk, flat, pitched_ref, field_ref):
    count = flat.shape[0]
    for y in range(pk.side):
        pitched_ref[y * pk.pitch : y * pk.pitch + count, 0 : pk.side] = flat[:, y * pk.side : (y + 1) * pk.side]
    for level in range(pk.depth):
        total = None
        for block in range(pk.blocks):
            row = block * pk.depth + level
            if row < pk.rows:
                part = roll(pitched_ref[pl.ds(row, pk.side, stride=pk.pitch), :], block * pk.span)
                total = part if total is None else total + part
        field_ref[level] = total


def edge_kernel(pk, slab_ref, psi_ref, edge_ref, sem):
    first = jnp.where(slab_ref[0] == 0, pk.half - DEG, 0)
    copy = pltpu.make_async_copy(psi_ref.at[pl.ds(first, DEG)], edge_ref, sem)
    copy.start()
    copy.wait()


def start_kernel(
    pk, masks, slab_ref, dom_ref, psi_in_ref, pot_in_ref, offsets_in_ref,
    field_ref, coef_ref, code_ref, flat_ref, pitched_ref, psi_ref, pot_ref, offsets_ref, sems,
):
    psi_copy = pltpu.make_async_copy(psi_in_ref, psi_ref, sems.at[2])
    copy = pltpu.make_async_copy(pot_in_ref, pot_ref, sems.at[0])
    psi_copy.start()
    offsets_copy = pltpu.make_async_copy(offsets_in_ref, offsets_ref, sems.at[1])
    copy.start()
    offsets_copy.start()
    half, side = pk.half, pk.side
    cells = side * side
    is_lower = slab_ref[0] == 0
    flat_ref[...] = jnp.zeros(flat_ref.shape, jnp.float32)
    pitched_ref[...] = jnp.zeros(pitched_ref.shape, jnp.float32)
    psi_copy.wait()
    own = psi_ref[:, 0, :]

    @pl.when(is_lower)
    def _():
        flat_ref[0:half] = own

    @pl.when(jnp.logical_not(is_lower))
    def _():
        flat_ref[DEG : DEG + half] = own

    pack(pk, flat_ref[...], pitched_ref, field_ref)
    copy.wait()

    @pl.when(is_lower)
    def _():
        flat_ref[0 : pk.rows] = pot_ref[0 : pk.rows] * (2.0 / HALF_WIDTH)

    @pl.when(jnp.logical_not(is_lower))
    def _():
        flat_ref[0 : pk.rows] = pot_ref[side - pk.rows : side] * (2.0 / HALF_WIDTH)

    pack(pk, flat_ref[...], pitched_ref, coef_ref)

    offsets_copy.wait()
    dom, dom_count = dom_ref[0], len(masks)
    blocks_z = dom_count // 4
    code = jnp.int32(0)
    for idx, mask in enumerate(masks):
        other = dom ^ mask
        at_x = (offsets_ref[other, 0] != offsets_ref[dom, 0]).astype(jnp.int32)
        at_y = (offsets_ref[other, 1] != offsets_ref[dom, 1]).astype(jnp.int32)
        at_z = (offsets_ref[other, 2] - offsets_ref[dom, 2]) // CORE
        at_z = jnp.where(at_z < 0, at_z + blocks_z, at_z)
        place = (at_z * 2 + at_y) * 2 + at_x
        for where in range(dom_count):
            code = code + jnp.where(place == where, idx * dom_count**where, 0)
    code_ref[...] = jnp.full(code_ref.shape, code.astype(jnp.float32))


def filtered_field(pk, start_ref, one_ref, two_ref, coef_ref):
    lane = lanes_of((8, 128))
    is_cell = (lane % pk.span < pk.side) & (lane < pk.blocks * pk.span)
    full_weight = jnp.where(is_cell, 1.0 / HALF_WIDTH, 0.0)
    part_weight = jnp.where(is_cell & (lane < (pk.blocks - 1) * pk.span), 1.0 / HALF_WIDTH, 0.0)
    after_first = lane >= pk.span
    before_last = lane < (pk.blocks - 1) * pk.span
    previous_ref, current_ref = None, start_ref
    for order in range(DEG):
        target_ref = (one_ref, two_ref)[order % 2]
        for tile in range(pk.side // 8):
            at = 8 + 8 * tile
            values = [current_ref[level, at : at + 8, :] for level in range(pk.depth)]
            before = jnp.where(after_first, roll(values[-1], pk.span), 0.0)
            after = jnp.where(before_last, roll(values[0], -pk.span), 0.0)
            around = [before] + values + [after]
            for level in range(pk.depth):
                value = values[level]
                total = around[level] + around[level + 2]
                total = total + (
                    current_ref[level, at - 1 : at + 7, :] + current_ref[level, at + 1 : at + 9, :]
                )
                total = total + (roll(value, 1) + roll(value, -1))
                weight = full_weight if (pk.blocks - 1) * pk.depth + level < pk.rows else part_weight
                following = coef_ref[level, at - 8 : at, :] * value - weight * total
                if order == 0:
                    following = 0.5 * following
                else:
                    following = following - previous_ref[level, at : at + 8, :]
                target_ref[level, at : at + 8, :] = following
        previous_ref, current_ref = current_ref, target_ref


def clear_margins(pk, ref):
    zeros = jnp.zeros((pk.depth, 8, 128), jnp.float32)
    ref[:, 0:8, :] = zeros
    ref[:, 8 + pk.side : 16 + pk.side, :] = zeros


def first_kernel(
    pk, bands, slab_ref, start_ref, halo_ref, coef_ref, filt_ref, dens_ref, field_ref, one_ref, lines_ref
):
    side, span = pk.side, pk.span
    slab = slab_ref[0]
    is_lower = slab == 0
    clear_margins(pk, field_ref)
    clear_margins(pk, one_ref)
    clear_margins(pk, filt_ref)
    field_ref[:, 8 : 8 + side, :] = start_ref[...]
    low_block, low_level = pk.where(pk.half)
    high_block, high_level = pk.where(0)
    shift = jnp.where(is_lower, low_block * span, high_block * span)
    past = lanes_of((DEG, 128)) - shift
    is_line = (past >= 0) & (past < side)
    cells = side * side
    tiles = []
    for tile in range(-(-cells // 128)):
        width = min(128, cells - tile * 128)
        part = halo_ref[:, 0, tile * 128 : tile * 128 + width]
        tiles.append(part if width == 128 else jnp.concatenate([part, jnp.zeros((DEG, 128 - width), jnp.float32)], 1))
    for y in range(side):
        tile, start = y * side // 128, y * side % 128
        line = pltpu.roll(tiles[tile], shift + (128 - start), 1)
        if start + side > 128:
            line = jnp.where(past < 128 - start, line, pltpu.roll(tiles[tile + 1], shift + (128 - start), 1))
        lines_ref[y * DEG : (y + 1) * DEG, :] = jnp.where(is_line, line, 0.0)
    for row in range(DEG):
        level = jnp.where(is_lower, low_level, high_level) + row
        line = lines_ref[pl.ds(row, side, stride=DEG), :]
        field_ref[level, 8 : 8 + side, :] = field_ref[level, 8 : 8 + side, :] + line

    filtered_field(pk, field_ref, one_ref, filt_ref, coef_ref)
    result_ref = filt_ref

    lane = lanes_of((8, 128))
    lines = 128 // CORE
    for cell in range(CORE // 2):
        row = cell + jnp.where(is_lower, BUF, DEG)
        block, level = row // pk.depth, row % pk.depth
        total = jnp.zeros((8, 128), jnp.float32)
        for line in range(lines):
            value = result_ref[level, 8 + BUF + 8 * line : 16 + BUF + 8 * line, :]
            shift = line * CORE - BUF - block * span + 128 * pk.blocks
            total = jnp.where(lane // CORE == line, pltpu.roll(value, shift % 128, 1), total)
        dens_ref[cell * 8 : (cell + 1) * 8] = total * total * (1.0 / bands)


def send_kernel(pk, slab_ref, result_ref, edge_ref):
    side, span = pk.side, pk.span
    is_lower = slab_ref[0] == 0
    lane = lanes_of((side, 128))
    for group in range(pk.edge_groups):
        total = jnp.zeros((side, 128), jnp.float32)
        for slot in range(min(pk.blocks, DEG - group * pk.blocks)):
            row = group * pk.blocks + slot + jnp.where(is_lower, pk.half - DEG, DEG)
            shift = slot * span - row // pk.depth * span + 128 * pk.blocks
            line = pltpu.roll(result_ref[row % pk.depth, 8 : 8 + side, :], shift % 128, 1)
            total = jnp.where((lane >= slot * span) & (lane < slot * span + side), line, total)
        edge_ref[group * side : (group + 1) * side] = total


def take_kernel(pk, slab_ref, filt_ref, beside_ref, field_ref):
    side, span, half = pk.side, pk.span, pk.half
    is_lower = slab_ref[0] == 0
    field_ref[...] = filt_ref[...]
    lane = lanes_of((side, 128))
    base = CORE // 2 * 8
    for row in range(DEG):
        group_at, slot = row // pk.blocks, row % pk.blocks
        line = beside_ref[base + group_at * side : base + (group_at + 1) * side, :]
        for wanted, (block, level) in ((True, pk.where(half + row)), (False, pk.where(row))):
            here = (lane >= block * span) & (lane < block * span + side) & (is_lower == wanted)
            old = field_ref[level, 8 : 8 + side, :]
            field_ref[level, 8 : 8 + side, :] = jnp.where(here, roll(line, (block - slot) * span), old)


def split2(values):
    high = values.astype(jnp.bfloat16)
    return high, (values - high.astype(jnp.float32)).astype(jnp.bfloat16)


def split3(values):
    high = values.astype(jnp.bfloat16)
    rest = values - high.astype(jnp.float32)
    middle = rest.astype(jnp.bfloat16)
    return high, middle, (rest - middle.astype(jnp.float32)).astype(jnp.bfloat16)


def dot(left, right):
    return jnp.dot(left, right, preferred_element_type=jnp.float32)


def table_parts(table):
    high = table.astype(ml_dtypes.bfloat16)
    return high, (table - high.astype(np.float64)).astype(ml_dtypes.bfloat16)


def left_table(table):
    high, low = table_parts(table)
    return np.concatenate([high, low, high], -1)


def stacked(values):
    high, low = split2(values)
    return jnp.concatenate([high, high, low], 0)


@functools.lru_cache(maxsize=None)
def solver_tables(side, grid_z):
    pk = Packing(side)
    blocks_z = grid_z // CORE
    lanes = 4 * grid_z
    basis, waves = parity_basis()
    z_basis, z_waves = wave_basis(grid_z)
    lines = 128 // CORE
    into = []
    for place_z in range(blocks_z):
        along_z = z_basis[:, place_z * CORE : (place_z + 1) * CORE].T
        high, low = table_parts(np.kron(np.eye(lines), along_z))
        into += [high, high, low]
    into = np.concatenate(into, 0)
    region = np.arange(side) - BUF
    outer = basis[:, :, region % (2 * CORE)]
    small = [left_table(np.concatenate([basis[0, :, :CORE], basis[1, :, :CORE]], 0))]
    small.append(left_table(np.concatenate([outer[0].T, outer[1].T], 0)))
    for first_row in (0, side - pk.rows):
        rows = outer[:, :, first_row : first_row + pk.rows]
        rows = np.pad(rows, ((0, 0), (0, 0), (0, padded(pk.rows, 8) - pk.rows)))
        small.append(left_table(np.concatenate([rows[0].T, rows[1].T], 0)))
    small = np.concatenate(small, 0)
    back_z = []
    spread = np.zeros((blocks_z, 3, 128, 128))
    for block in range(pk.blocks):
        start = block * pk.span
        table = np.zeros((4, grid_z, 128))
        table[:, :, start : start + side] = z_basis[:, region % grid_z]
        high, low = table_parts(table.reshape(lanes, 128))
        back_z.append(np.block([[high, low], [high, np.zeros_like(low)]]))
        for cell, pos in enumerate(region % grid_z):
            spread[pos // CORE, :, block * CORE + pos % CORE, start + cell] = 1.0
    back_z = np.concatenate(back_z, 0)
    spread = spread.reshape(blocks_z * 3 * 128, 128).astype(ml_dtypes.bfloat16)
    eigen = eigenvalue(waves, 2 * CORE)
    lam = (
        eigen.T[:, None, None, :, None]
        + eigen.T[None, :, :, None, None]
        + eigenvalue(z_waves, grid_z)[None, None, None, None, :]
    )
    lam[0, 0, 0, 0, 0] = np.inf
    factor = (FOUR_PI / lam).reshape(CORE * CORE, lanes).astype(np.float32)
    pieces = [back_z, np.concatenate([into, np.pad(spread, ((0, 0), (0, lanes - 128)))], 0), small]
    height = max(len(piece) for piece in pieces)
    pieces = [np.pad(piece, ((0, height - len(piece)), (0, -piece.shape[1] % 128))) for piece in pieces]
    return np.concatenate(pieces, 1), factor


def cube_root(values):
    positive = values > 0.0
    safe = jnp.where(positive, values, 1.0)
    root = jnp.exp(jnp.log(safe) * (1.0 / 3.0))
    root = root - (root - safe / (root * root)) * (1.0 / 3.0)
    return jnp.where(positive, root, 0.0)


def second_kernel(
    pk, dom_count, slab_ref, code_ref, near_ref, across_ref, field_ref, start_coef_ref,
    table_ref, factor_ref,
    out_ref, cubes_ref, one_ref, two_ref, coef_ref, left_ref, rows_ref, waves_ref, mixed_ref, flat_ref,
    near_dens_ref, own_ref,
):
    side, half, span = pk.side, pk.half, pk.span
    is_lower = slab_ref[0] == 0
    blocks_z = dom_count // 4
    grid_z = CORE * blocks_z
    lanes = 4 * grid_z
    columns = lanes // 128
    lines = 128 // CORE
    pitch = CORE + 8
    kept = padded(pk.rows, 8)

    cubes_ref[0 : dom_count // 2] = near_ref[...]
    cubes_ref[dom_count // 2 : dom_count] = across_ref[...]
    mean = jnp.sum(cubes_ref[...]) * (1.0 / (dom_count * CORE * CORE * CORE))

    code = jnp.max(code_ref[...]).astype(jnp.int32)
    cube_at = [code // dom_count**where % dom_count for where in range(dom_count)]

    for at_z in range(blocks_z):
        near, at_x, at_y, at_xy = [cubes_ref[cube_at[at_z * 4 + place]] for place in range(4)]
        sums, others = near + at_x, at_y + at_xy
        diffs, other_diffs = near - at_x, at_y - at_xy
        parities = (sums + others - 4.0 * mean, sums - others, diffs + other_diffs, diffs - other_diffs)
        for parity, value in enumerate(parities):
            high, low = split2(value)
            for idx, piece in enumerate((high, low, high)):
                cols = slice((at_z * 3 + idx) * 128, (at_z * 3 + idx + 1) * 128)
                left_ref[parity * CORE * 8 : (parity + 1) * CORE * 8, cols] = piece
    product = dot(left_ref[...], table_ref[0 : blocks_z * 3 * 128, 256 : 256 + lanes])
    lane = lanes_of((8, 128))
    for x in range(CORE):
        for line in range(lines):
            for col in range(columns):
                total = None
                for parity in range(4):
                    into = parity * grid_z - col * 128
                    if 0 <= into < 128:
                        at = line * grid_z
                        part = product[(parity * CORE + x) * 8 : (parity * CORE + x + 1) * 8, at // 128 * 128 : at // 128 * 128 + 128]
                        part = roll(part, into - at % 128)
                        total = part if total is None else jnp.where(lane >= into, part, total)
                rows_ref[col, x * pitch + line * 8 : x * pitch + line * 8 + 8, :] = total

    lane = lanes_of((8, 128))
    for at_z in range(blocks_z):
        for level in range(pk.depth):
            inner, low_wrap, high_wrap = [], None, None
            for block in range(pk.blocks):
                row = block * pk.depth + level
                if row >= pk.rows:
                    continue
                x = row - BUF + jnp.where(is_lower, 0, side - pk.rows)
                inside = (x >= 0) & (x < CORE)
                cell = pl.multiple_of((x + CORE) % CORE * 8, 8)

                def source(at_y):
                    place = (at_z * 2 + at_y) * 2
                    cube = jnp.where(inside, cube_at[place], cube_at[place + 1])
                    return cubes_ref[cube, pl.ds(cell, 8), :]

                def put(value, line, total):
                    value = roll(value, (block - line) * CORE)
                    return jnp.where((lane >= block * CORE) & (lane < (block + 1) * CORE), value, total)

                own, beside = source(0), source(1)
                zeros = jnp.zeros((8, 128), jnp.float32)
                inner = inner or [zeros] * lines
                inner = [put(own, line, total) for line, total in enumerate(inner)]
                low_wrap = put(beside, lines - 1, zeros if low_wrap is None else low_wrap)
                high_wrap = put(beside, 0, zeros if high_wrap is None else high_wrap)
            base = level * side
            near_dens_ref[at_z, base : base + BUF, :] = low_wrap[8 - BUF :]
            for line in range(lines):
                near_dens_ref[at_z, base + BUF + 8 * line : base + BUF + 8 * line + 8, :] = inner[line]
            near_dens_ref[at_z, base + BUF + CORE : base + side, :] = high_wrap[:BUF]

    group = max(1, 256 // lanes)
    lane_id = lanes_of((1, group * lanes)) % lanes
    even_x = lane_id < 2 * grid_z
    even_y = (lane_id // grid_z) % 2 == 0

    def side_by_side(ref, starts, stride, count):
        pieces = []
        for start in starts:
            for col in range(columns):
                if stride == 1:
                    pieces.append(ref[col, pl.ds(start, count), :])
                else:
                    pieces.append(ref[col, pl.ds(start, count, stride=stride), :])
        return jnp.concatenate(pieces, 1)

    def scatter(ref, starts, values, count):
        for idx, start in enumerate(starts):
            for col in range(columns):
                at = (idx * columns + col) * 128
                ref[col, start : start + count, :] = values[:, at : at + 128]

    def small(first, count):
        return table_ref[first : first + count, 256 + lanes : 256 + lanes + 3 * CORE]

    forward = small(0, 2 * CORE)
    back_y = small(2 * CORE, 2 * side)
    first = 2 * CORE + 2 * side
    back_x = jnp.where(is_lower, small(first, 2 * kept), small(first + 2 * kept, 2 * kept))
    for first in range(0, CORE, group):
        starts = [x * pitch for x in range(first, first + group)]
        both = dot(forward, stacked(side_by_side(rows_ref, starts, 1, CORE)))
        scatter(waves_ref, starts, jnp.where(even_y, both[:CORE], both[CORE:]), CORE)

    for first in range(0, CORE, group):
        waves_y = list(range(first, first + group))
        both = dot(forward, stacked(side_by_side(waves_ref, waves_y, pitch, CORE)))
        modes = jnp.where(even_x, both[:CORE], both[CORE:])
        scale = jnp.concatenate([factor_ref[wave * CORE : (wave + 1) * CORE] for wave in waves_y], 1)
        both = dot(back_x, stacked(modes * scale))
        scatter(mixed_ref, [wave * pitch for wave in waves_y], jnp.where(even_x, both[:kept], both[kept:]), kept)

    for level in range(pk.depth):
        rows = [block * pk.depth + level for block in range(pk.blocks)]
        rows = [row for row in rows if row < pk.rows]
        for first in range(0, len(rows), group):
            taken = rows[first : first + group]
            both = dot(back_y, stacked(side_by_side(mixed_ref, taken, pitch, CORE)))
            width = both.shape[1]
            field = jnp.where(even_y[:, :width], both[:side], both[side:])
            for idx in range(len(taken)):
                flat_ref[first + idx, level * side : (level + 1) * side, :] = field[:, idx * lanes : (idx + 1) * lanes]
        for block in range(len(rows), pk.blocks):
            flat_ref[block, level * side : (level + 1) * side, :] = jnp.zeros((side, lanes), jnp.float32)

    pieces = []
    for block in range(pk.blocks):
        pieces += split2(flat_ref[block])
    product = dot(jnp.concatenate(pieces, 1), table_ref[0 : pk.blocks * 2 * lanes, 0:256])
    hartree = product[:, 0:128] + product[:, 128:256]
    pieces = []
    for at_z in range(blocks_z):
        pieces += split3(near_dens_ref[at_z])
    density = dot(jnp.concatenate(pieces, 1), table_ref[blocks_z * 3 * 128 : blocks_z * 6 * 128, 256:384])
    added = (hartree + EXCHANGE_COEF * cube_root(density)) * (2.0 / HALF_WIDTH)
    for level in range(pk.depth):
        coef_ref[level] = start_coef_ref[level] + added[level * side : (level + 1) * side]

    clear_margins(pk, one_ref)
    clear_margins(pk, two_ref)
    filtered_field(pk, field_ref, one_ref, two_ref, coef_ref)

    for row in range(half):
        at = row + jnp.where(is_lower, 0, DEG)
        shift = 128 * pk.blocks - at // pk.depth * span
        own_ref[row * side : (row + 1) * side, :] = pltpu.roll(
            two_ref[at % pk.depth, 8 : 8 + side, :], shift % 128, 1
        )
    cells = side * side
    parts = [roll(own_ref[pl.ds(y, half, stride=side), :], y * side) for y in range(side)]
    for tile in range(-(-cells // 128)):
        first, last = tile * 128 // side, min(side - 1, (tile * 128 + 127) // side)
        lane = lanes_of((half, 128)) + tile * 128
        total = None
        for y in range(first, last + 1):
            total = parts[y] if total is None else jnp.where(lane >= y * side, parts[y], total)
        width = min(128, cells - tile * 128)
        out_ref[:, 0, tile * 128 : tile * 128 + width] = total[:, :width]


SMEM = pl.BlockSpec(memory_space=pltpu.SMEM)
VMEM = pl.BlockSpec(memory_space=pltpu.VMEM)
HBM = pl.BlockSpec(memory_space=pltpu.HBM)
params = pltpu.CompilerParams(vmem_limit_bytes=32 * 1024 * 1024)


def in_vmem(*shape):
    return pltpu.VMEM(shape, jnp.float32)


def in_hbm(value):
    return pltpu.with_memory_space_constraint(value, pltpu.HBM)


def local(psi_in, v_in, offsets):
    band_count = lax.axis_size("band")
    dom_count = lax.axis_size("dom")
    dom_idx = lax.axis_index("dom")
    slab_idx = lax.axis_index("band") % 2
    is_lower = slab_idx == 0
    slab_scalar = slab_idx.astype(jnp.int32).reshape(1)
    side = v_in.shape[1]
    pk = Packing(side)
    half = side // 2
    cells = side * side
    bands = band_count // 2
    grid_z = CORE * dom_count // 4
    lanes = 4 * grid_z
    slab_rows = CORE // 2 * 8

    f32, bf16 = jnp.float32, jnp.bfloat16
    field_type = in_vmem(*pk.shape)
    padded_field = pltpu.VMEM(pk.padded_shape, f32)

    rows = psi_in.reshape(half, 1, cells)
    rows = in_hbm(rows)
    edge = pl.pallas_call(
        functools.partial(edge_kernel, pk),
        out_shape=in_vmem(DEG, 1, cells),
        in_specs=[SMEM, HBM],
        out_specs=VMEM,
        scratch_shapes=[pltpu.SemaphoreType.DMA],
        compiler_params=params,
    )(slab_scalar, rows)
    halo = swapped(edge, "band", 1)
    masks = [0]
    bit = dom_count // 2
    while bit:
        masks = masks + [one | bit for one in masks]
        bit //= 2
    dom_scalar = dom_idx.astype(jnp.int32).reshape(1)
    start, coef, code = pl.pallas_call(
        functools.partial(start_kernel, pk, masks),
        out_shape=(field_type, field_type, in_vmem(8, 128)),
        in_specs=[SMEM, SMEM, HBM, HBM, HBM],
        out_specs=(VMEM, VMEM, VMEM),
        scratch_shapes=[
            pltpu.VMEM((pk.rows, cells), f32),
            pltpu.VMEM((side * pk.pitch, 128), f32),
            pltpu.VMEM((half, 1, cells), f32),
            pltpu.VMEM((side, cells), f32),
            pltpu.SMEM((dom_count, 3), jnp.int32),
            pltpu.SemaphoreType.DMA((3,)),
        ],
        compiler_params=params,
    )(slab_scalar, dom_scalar, rows, in_hbm(v_in[0]), in_hbm(offsets))

    padded_type = in_vmem(*pk.padded_shape)
    filt, dens = pl.pallas_call(
        functools.partial(first_kernel, pk, bands),
        out_shape=(padded_type, in_vmem(slab_rows, 128)),
        in_specs=[SMEM, VMEM, VMEM, VMEM],
        out_specs=(VMEM, VMEM),
        scratch_shapes=[padded_field, padded_field, pltpu.VMEM((side * DEG, 128), f32)],
        compiler_params=params,
    )(slab_scalar, start, halo, coef)
    edge = pl.pallas_call(
        functools.partial(send_kernel, pk),
        out_shape=in_vmem(pk.edge_groups * side, 128),
        in_specs=[SMEM, VMEM],
        out_specs=VMEM,
        compiler_params=params,
    )(slab_scalar, filt)

    mask = 2
    while mask < band_count:
        dens = dens + swapped(dens, "band", mask)
        mask *= 2

    far = dom_count // 2
    both = ("dom", "band")
    count = dom_count * band_count

    def crossed(value, mask):
        return lax.ppermute(value, both, [(source, source ^ mask) for source in range(count)])

    beside_all = crossed(jnp.concatenate([dens, edge], 0), 1)
    beside = beside_all[:slab_rows]
    across = crossed(dens, far * band_count)
    diagonal = crossed(dens, far * band_count + 1)

    def cube_of(own, other):
        return jnp.concatenate([jnp.where(is_lower, own, other), jnp.where(is_lower, other, own)], 0)

    cubes = jnp.stack([cube_of(dens, beside), cube_of(across, diagonal)])
    bit = far // 2
    while bit:
        if bit > 1:
            cubes = jnp.concatenate([cubes, swapped(cubes, "dom", bit)], 0)
        bit //= 2
    cubes_across = swapped(cubes, "dom", 1)

    field = pl.pallas_call(
        functools.partial(take_kernel, pk),
        out_shape=padded_type,
        in_specs=[SMEM, VMEM, VMEM],
        out_specs=VMEM,
        compiler_params=params,
    )(slab_scalar, filt, beside_all)
    table, factor = solver_tables(side, grid_z)
    pitch = CORE + 8
    result = pl.pallas_call(
        functools.partial(second_kernel, pk, dom_count),
        out_shape=jax.ShapeDtypeStruct((half, 1, cells), f32),
        in_specs=[SMEM] + [VMEM] * 7,
        out_specs=VMEM,
        scratch_shapes=[
            pltpu.VMEM((dom_count, CORE * 8, 128), f32),
            padded_field,
            padded_field,
            pltpu.VMEM(pk.shape, f32),
            pltpu.VMEM((4 * CORE * 8, dom_count // 4 * 3 * 128), bf16),
            pltpu.VMEM((lanes // 128, CORE * pitch, 128), f32),
            pltpu.VMEM((lanes // 128, CORE * pitch, 128), f32),
            pltpu.VMEM((lanes // 128, CORE * pitch, 128), f32),
            pltpu.VMEM((pk.blocks, pk.depth * side, lanes), f32),
            pltpu.VMEM((dom_count // 4, pk.depth * side, 128), f32),
            pltpu.VMEM((half * side, 128), f32),
        ],
        compiler_params=params,
    )(
        slab_scalar, code, cubes, cubes_across, field, coef,
        jnp.asarray(table), jnp.asarray(factor),
    )
    return result.reshape(1, 1, half, cells)


def solution(mesh):
    in_specs = (P("dom", "band", None, None), P("dom", None, None), P())
    out_specs = P("dom", "band", None, None)
    return jax.shard_map(local, mesh=mesh, in_specs=in_specs, out_specs=out_specs, check_vma=False)
```

```python
import functools
import math

import jax
import jax.numpy as jnp
import ml_dtypes
import numpy as np
from jax import lax
from jax.experimental import pallas as pl
from jax.experimental.pallas import tpu as pltpu
from jax.sharding import PartitionSpec as P

CORE = 32
BUF = 4
DEG = 8

HALF_WIDTH = 4.5
FOUR_PI = 4.0 * math.pi
EXCHANGE_COEF = -((3.0 / math.pi) ** (1.0 / 3.0))


def swapped(value, axis, mask):
    pairs = [(source, source ^ mask) for source in range(lax.axis_size(axis))]
    return lax.ppermute(value, axis, pairs)


def wave_basis(length):
    cells = np.arange(length)
    rows, waves = [], []
    for wave in range(length // 2 + 1):
        angle = 2.0 * np.pi * ((wave * cells) % length) / length
        if wave in (0, length // 2):
            rows.append(np.cos(angle) / np.sqrt(length))
            waves.append(wave)
        else:
            rows.append(np.cos(angle) * np.sqrt(2.0 / length))
            rows.append(np.sin(angle) * np.sqrt(2.0 / length))
            waves += [wave, wave]
    return np.array(rows), np.array(waves)


def parity_basis():
    rows, waves = wave_basis(2 * CORE)
    return np.stack([rows[waves % 2 == 0], rows[waves % 2 == 1]]), np.stack(
        [waves[waves % 2 == 0], waves[waves % 2 == 1]]
    )


def eigenvalue(waves, length):
    return 2.0 - 2.0 * np.cos(2.0 * np.pi * waves / length)


def padded(length, unit):
    return -(-length // unit) * unit


class Packing:
    def __init__(self, side):
        self.side = side
        self.half = side // 2
        self.rows = self.half + DEG
        self.blocks = 128 // (side + 1)
        self.span = 128 // self.blocks
        self.depth = -(-self.rows // self.blocks)
        self.shape = (self.depth, side, 128)
        self.padded_shape = (self.depth, side + 16, 128)
        self.edge_groups = -(-DEG // self.blocks)
        self.pitch = padded(self.rows, 16) + 8

    def where(self, row):
        return row // self.depth, row % self.depth


def lanes_of(shape):
    return lax.broadcasted_iota(jnp.int32, shape, len(shape) - 1)


def roll(values, shift):
    return values if isinstance(shift, int) and shift % 128 == 0 else pltpu.roll(values, shift % 128, 1)


def pack(pk, flat, pitched_ref, field_ref):
    count = flat.shape[0]
    for y in range(pk.side):
        pitched_ref[y * pk.pitch : y * pk.pitch + count, 0 : pk.side] = flat[:, y * pk.side : (y + 1) * pk.side]
    for level in range(pk.depth):
        total = None
        for block in range(pk.blocks):
            row = block * pk.depth + level
            if row < pk.rows:
                part = roll(pitched_ref[pl.ds(row, pk.side, stride=pk.pitch), :], block * pk.span)
                total = part if total is None else total + part
        field_ref[level] = total


def edge_kernel(pk, slab_ref, psi_ref, edge_ref, sem):
    first = jnp.where(slab_ref[0] == 0, pk.half - DEG, 0)
    copy = pltpu.make_async_copy(psi_ref.at[pl.ds(first, DEG)], edge_ref, sem)
    copy.start()
    copy.wait()


def start_kernel(
    pk, masks, slab_ref, dom_ref, psi_in_ref, pot_in_ref, offsets_in_ref,
    field_ref, coef_ref, code_ref, flat_ref, pitched_ref, psi_ref, pot_ref, offsets_ref, sems,
):
    psi_copy = pltpu.make_async_copy(psi_in_ref, psi_ref, sems.at[2])
    copy = pltpu.make_async_copy(pot_in_ref, pot_ref, sems.at[0])
    psi_copy.start()
    offsets_copy = pltpu.make_async_copy(offsets_in_ref, offsets_ref, sems.at[1])
    copy.start()
    offsets_copy.start()
    half, side = pk.half, pk.side
    cells = side * side
    is_lower = slab_ref[0] == 0
    flat_ref[...] = jnp.zeros(flat_ref.shape, jnp.float32)
    pitched_ref[...] = jnp.zeros(pitched_ref.shape, jnp.float32)
    psi_copy.wait()
    own = psi_ref[:, 0, :]

    @pl.when(is_lower)
    def _():
        flat_ref[0:half] = own

    @pl.when(jnp.logical_not(is_lower))
    def _():
        flat_ref[DEG : DEG + half] = own

    pack(pk, flat_ref[...], pitched_ref, field_ref)
    copy.wait()

    @pl.when(is_lower)
    def _():
        flat_ref[0 : pk.rows] = pot_ref[0 : pk.rows] * (2.0 / HALF_WIDTH)

    @pl.when(jnp.logical_not(is_lower))
    def _():
        flat_ref[0 : pk.rows] = pot_ref[side - pk.rows : side] * (2.0 / HALF_WIDTH)

    pack(pk, flat_ref[...], pitched_ref, coef_ref)

    offsets_copy.wait()
    dom, dom_count = dom_ref[0], len(masks)
    blocks_z = dom_count // 4
    code = jnp.int32(0)
    for idx, mask in enumerate(masks):
        other = dom ^ mask
        at_x = (offsets_ref[other, 0] != offsets_ref[dom, 0]).astype(jnp.int32)
        at_y = (offsets_ref[other, 1] != offsets_ref[dom, 1]).astype(jnp.int32)
        at_z = (offsets_ref[other, 2] - offsets_ref[dom, 2]) // CORE
        at_z = jnp.where(at_z < 0, at_z + blocks_z, at_z)
        place = (at_z * 2 + at_y) * 2 + at_x
        for where in range(dom_count):
            code = code + jnp.where(place == where, idx * dom_count**where, 0)
    code_ref[...] = jnp.full(code_ref.shape, code.astype(jnp.float32))


def filtered_field(pk, start_ref, one_ref, two_ref, coef_ref):
    lane = lanes_of((8, 128))
    is_cell = (lane % pk.span < pk.side) & (lane < pk.blocks * pk.span)
    full_weight = jnp.where(is_cell, 1.0 / HALF_WIDTH, 0.0)
    part_weight = jnp.where(is_cell & (lane < (pk.blocks - 1) * pk.span), 1.0 / HALF_WIDTH, 0.0)
    after_first = lane >= pk.span
    before_last = lane < (pk.blocks - 1) * pk.span
    previous_ref, current_ref = None, start_ref
    for order in range(DEG):
        target_ref = (one_ref, two_ref)[order % 2]
        for tile in range(pk.side // 8):
            at = 8 + 8 * tile
            values = [current_ref[level, at : at + 8, :] for level in range(pk.depth)]
            before = jnp.where(after_first, roll(values[-1], pk.span), 0.0)
            after = jnp.where(before_last, roll(values[0], -pk.span), 0.0)
            around = [before] + values + [after]
            for level in range(pk.depth):
                value = values[level]
                total = around[level] + around[level + 2]
                total = total + (
                    current_ref[level, at - 1 : at + 7, :] + current_ref[level, at + 1 : at + 9, :]
                )
                total = total + (roll(value, 1) + roll(value, -1))
                weight = full_weight if (pk.blocks - 1) * pk.depth + level < pk.rows else part_weight
                following = coef_ref[level, at - 8 : at, :] * value - weight * total
                if order == 0:
                    following = 0.5 * following
                else:
                    following = following - previous_ref[level, at : at + 8, :]
                target_ref[level, at : at + 8, :] = following
        previous_ref, current_ref = current_ref, target_ref


def clear_margins(pk, ref):
    zeros = jnp.zeros((pk.depth, 8, 128), jnp.float32)
    ref[:, 0:8, :] = zeros
    ref[:, 8 + pk.side : 16 + pk.side, :] = zeros


def first_kernel(
    pk, bands, slab_ref, start_ref, halo_ref, coef_ref, filt_ref, dens_ref, field_ref, one_ref, lines_ref
):
    side, span = pk.side, pk.span
    slab = slab_ref[0]
    is_lower = slab == 0
    clear_margins(pk, field_ref)
    clear_margins(pk, one_ref)
    clear_margins(pk, filt_ref)
    field_ref[:, 8 : 8 + side, :] = start_ref[...]
    low_block, low_level = pk.where(pk.half)
    high_block, high_level = pk.where(0)
    shift = jnp.where(is_lower, low_block * span, high_block * span)
    past = lanes_of((DEG, 128)) - shift
    is_line = (past >= 0) & (past < side)
    cells = side * side
    tiles = []
    for tile in range(-(-cells // 128)):
        width = min(128, cells - tile * 128)
        part = halo_ref[:, 0, tile * 128 : tile * 128 + width]
        tiles.append(part if width == 128 else jnp.concatenate([part, jnp.zeros((DEG, 128 - width), jnp.float32)], 1))
    for y in range(side):
        tile, start = y * side // 128, y * side % 128
        line = pltpu.roll(tiles[tile], shift + (128 - start), 1)
        if start + side > 128:
            line = jnp.where(past < 128 - start, line, pltpu.roll(tiles[tile + 1], shift + (128 - start), 1))
        lines_ref[y * DEG : (y + 1) * DEG, :] = jnp.where(is_line, line, 0.0)
    for row in range(DEG):
        level = jnp.where(is_lower, low_level, high_level) + row
        line = lines_ref[pl.ds(row, side, stride=DEG), :]
        field_ref[level, 8 : 8 + side, :] = field_ref[level, 8 : 8 + side, :] + line

    filtered_field(pk, field_ref, one_ref, filt_ref, coef_ref)
    result_ref = filt_ref

    lane = lanes_of((8, 128))
    lines = 128 // CORE
    for cell in range(CORE // 2):
        row = cell + jnp.where(is_lower, BUF, DEG)
        block, level = row // pk.depth, row % pk.depth
        total = jnp.zeros((8, 128), jnp.float32)
        for line in range(lines):
            value = result_ref[level, 8 + BUF + 8 * line : 16 + BUF + 8 * line, :]
            shift = line * CORE - BUF - block * span + 128 * pk.blocks
            total = jnp.where(lane // CORE == line, pltpu.roll(value, shift % 128, 1), total)
        dens_ref[cell * 8 : (cell + 1) * 8] = total * total * (1.0 / bands)


def send_kernel(pk, slab_ref, result_ref, edge_ref):
    side, span = pk.side, pk.span
    is_lower = slab_ref[0] == 0
    lane = lanes_of((side, 128))
    for group in range(pk.edge_groups):
        total = jnp.zeros((side, 128), jnp.float32)
        for slot in range(min(pk.blocks, DEG - group * pk.blocks)):
            row = group * pk.blocks + slot + jnp.where(is_lower, pk.half - DEG, DEG)
            shift = slot * span - row // pk.depth * span + 128 * pk.blocks
            line = pltpu.roll(result_ref[row % pk.depth, 8 : 8 + side, :], shift % 128, 1)
            total = jnp.where((lane >= slot * span) & (lane < slot * span + side), line, total)
        edge_ref[group * side : (group + 1) * side] = total


def take_kernel(pk, slab_ref, filt_ref, beside_ref, near_ref, field_ref, mean_ref):
    mean_ref[...] = jnp.full(mean_ref.shape, jnp.mean(near_ref[...]))
    side, span, half = pk.side, pk.span, pk.half
    is_lower = slab_ref[0] == 0
    field_ref[...] = filt_ref[...]
    lane = lanes_of((side, 128))
    base = CORE // 2 * 8
    for row in range(DEG):
        group_at, slot = row // pk.blocks, row % pk.blocks
        line = beside_ref[base + group_at * side : base + (group_at + 1) * side, :]
        for wanted, (block, level) in ((True, pk.where(half + row)), (False, pk.where(row))):
            here = (lane >= block * span) & (lane < block * span + side) & (is_lower == wanted)
            old = field_ref[level, 8 : 8 + side, :]
            field_ref[level, 8 : 8 + side, :] = jnp.where(here, roll(line, (block - slot) * span), old)


def split2(values):
    high = values.astype(jnp.bfloat16)
    return high, (values - high.astype(jnp.float32)).astype(jnp.bfloat16)


def split3(values):
    high = values.astype(jnp.bfloat16)
    rest = values - high.astype(jnp.float32)
    middle = rest.astype(jnp.bfloat16)
    return high, middle, (rest - middle.astype(jnp.float32)).astype(jnp.bfloat16)


def dot(left, right):
    return jnp.dot(left, right, preferred_element_type=jnp.float32)


def table_parts(table):
    high = table.astype(ml_dtypes.bfloat16)
    return high, (table - high.astype(np.float64)).astype(ml_dtypes.bfloat16)


def left_table(table):
    high, low = table_parts(table)
    return np.concatenate([high, low, high], -1)


def stacked(values):
    high, low = split2(values)
    return jnp.concatenate([high, high, low], 0)


@functools.lru_cache(maxsize=None)
def solver_tables(side, grid_z):
    pk = Packing(side)
    blocks_z = grid_z // CORE
    lanes = 4 * grid_z
    basis, waves = parity_basis()
    z_basis, z_waves = wave_basis(grid_z)
    lines = 128 // CORE
    into = []
    for place_z in range(blocks_z):
        along_z = z_basis[:, place_z * CORE : (place_z + 1) * CORE].T
        high, low = table_parts(np.kron(np.eye(lines), along_z))
        into += [high, high, low]
    into = np.concatenate(into, 0)
    region = np.arange(side) - BUF
    outer = basis[:, :, region % (2 * CORE)]
    small = [left_table(np.concatenate([basis[0, :, :CORE], basis[1, :, :CORE]], 0))]
    small.append(left_table(np.concatenate([outer[0].T, outer[1].T], 0)))
    for first_row in (0, side - pk.rows):
        rows = outer[:, :, first_row : first_row + pk.rows]
        rows = np.pad(rows, ((0, 0), (0, 0), (0, padded(pk.rows, 8) - pk.rows)))
        small.append(left_table(np.concatenate([rows[0].T, rows[1].T], 0)))
    small = np.concatenate(small, 0)
    back_z = []
    spread = np.zeros((blocks_z, 3, 128, 128))
    for block in range(pk.blocks):
        start = block * pk.span
        table = np.zeros((4, grid_z, 128))
        table[:, :, start : start + side] = z_basis[:, region % grid_z]
        high, low = table_parts(table.reshape(lanes, 128))
        back_z.append(np.block([[high, low], [high, np.zeros_like(low)]]))
        for cell, pos in enumerate(region % grid_z):
            spread[pos // CORE, :, block * CORE + pos % CORE, start + cell] = 1.0
    back_z = np.concatenate(back_z, 0)
    spread = spread.reshape(blocks_z * 3 * 128, 128).astype(ml_dtypes.bfloat16)
    eigen = eigenvalue(waves, 2 * CORE)
    lam = (
        eigen.T[:, None, None, :, None]
        + eigen.T[None, :, :, None, None]
        + eigenvalue(z_waves, grid_z)[None, None, None, None, :]
    )
    lam[0, 0, 0, 0, 0] = np.inf
    factor = (FOUR_PI / lam).reshape(CORE * CORE, lanes).astype(np.float32)
    pieces = [back_z, np.concatenate([into, np.pad(spread, ((0, 0), (0, lanes - 128)))], 0), small]
    height = max(len(piece) for piece in pieces)
    pieces = [np.pad(piece, ((0, height - len(piece)), (0, -piece.shape[1] % 128))) for piece in pieces]
    return np.concatenate(pieces, 1), factor


def cube_root(values):
    positive = values > 0.0
    safe = jnp.where(positive, values, 1.0)
    root = jnp.exp(jnp.log(safe) * (1.0 / 3.0))
    root = root - (root - safe / (root * root)) * (1.0 / 3.0)
    return jnp.where(positive, root, 0.0)


def second_kernel(
    pk, dom_count, slab_ref, code_ref, mean_ref, near_ref, across_ref, field_ref, start_coef_ref,
    table_ref, factor_ref,
    out_ref, cubes_ref, one_ref, two_ref, coef_ref, left_ref, rows_ref, waves_ref, mixed_ref, flat_ref,
    near_dens_ref, own_ref,
):
    side, half, span = pk.side, pk.half, pk.span
    is_lower = slab_ref[0] == 0
    blocks_z = dom_count // 4
    grid_z = CORE * blocks_z
    lanes = 4 * grid_z
    columns = lanes // 128
    lines = 128 // CORE
    pitch = CORE + 8
    kept = padded(pk.rows, 8)

    cubes_ref[0 : dom_count // 2] = near_ref[...]
    cubes_ref[dom_count // 2 : dom_count] = across_ref[...]
    mean = 4.0 * jnp.concatenate([mean_ref[...]] * CORE, 0)
    code = jnp.max(code_ref[...]).astype(jnp.int32)
    cube_at = [code // dom_count**where % dom_count for where in range(dom_count)]

    for at_z in range(blocks_z):
        near, at_x, at_y, at_xy = [cubes_ref[cube_at[at_z * 4 + place]] for place in range(4)]
        sums, others = near + at_x, at_y + at_xy
        diffs, other_diffs = near - at_x, at_y - at_xy
        parities = (sums + others - mean, sums - others, diffs + other_diffs, diffs - other_diffs)
        for parity, value in enumerate(parities):
            high, low = split2(value)
            for idx, piece in enumerate((high, low, high)):
                cols = slice((at_z * 3 + idx) * 128, (at_z * 3 + idx + 1) * 128)
                left_ref[parity * CORE * 8 : (parity + 1) * CORE * 8, cols] = piece
    product = dot(left_ref[...], table_ref[0 : blocks_z * 3 * 128, 256 : 256 + lanes])
    lane = lanes_of((8, 128))
    for x in range(CORE):
        for line in range(lines):
            for col in range(columns):
                total = None
                for parity in range(4):
                    into = parity * grid_z - col * 128
                    if 0 <= into < 128:
                        at = line * grid_z
                        part = product[(parity * CORE + x) * 8 : (parity * CORE + x + 1) * 8, at // 128 * 128 : at // 128 * 128 + 128]
                        part = roll(part, into - at % 128)
                        total = part if total is None else jnp.where(lane >= into, part, total)
                rows_ref[col, x * pitch + line * 8 : x * pitch + line * 8 + 8, :] = total

    lane = lanes_of((8, 128))
    for at_z in range(blocks_z):
        for level in range(pk.depth):
            inner, low_wrap, high_wrap = [], None, None
            for block in range(pk.blocks):
                row = block * pk.depth + level
                if row >= pk.rows:
                    continue
                x = row - BUF + jnp.where(is_lower, 0, side - pk.rows)
                inside = (x >= 0) & (x < CORE)
                cell = pl.multiple_of((x + CORE) % CORE * 8, 8)

                def source(at_y):
                    place = (at_z * 2 + at_y) * 2
                    cube = jnp.where(inside, cube_at[place], cube_at[place + 1])
                    return cubes_ref[cube, pl.ds(cell, 8), :]

                def put(value, line, total):
                    value = roll(value, (block - line) * CORE)
                    return jnp.where((lane >= block * CORE) & (lane < (block + 1) * CORE), value, total)

                own, beside = source(0), source(1)
                zeros = jnp.zeros((8, 128), jnp.float32)
                inner = inner or [zeros] * lines
                inner = [put(own, line, total) for line, total in enumerate(inner)]
                low_wrap = put(beside, lines - 1, zeros if low_wrap is None else low_wrap)
                high_wrap = put(beside, 0, zeros if high_wrap is None else high_wrap)
            base = level * side
            near_dens_ref[at_z, base : base + BUF, :] = low_wrap[8 - BUF :]
            for line in range(lines):
                near_dens_ref[at_z, base + BUF + 8 * line : base + BUF + 8 * line + 8, :] = inner[line]
            near_dens_ref[at_z, base + BUF + CORE : base + side, :] = high_wrap[:BUF]

    group = max(1, 256 // lanes)
    lane_id = lanes_of((1, group * lanes)) % lanes
    even_x = lane_id < 2 * grid_z
    even_y = (lane_id // grid_z) % 2 == 0

    def side_by_side(ref, starts, stride, count):
        pieces = []
        for start in starts:
            for col in range(columns):
                if stride == 1:
                    pieces.append(ref[col, pl.ds(start, count), :])
                else:
                    pieces.append(ref[col, pl.ds(start, count, stride=stride), :])
        return jnp.concatenate(pieces, 1)

    def scatter(ref, starts, values, count):
        for idx, start in enumerate(starts):
            for col in range(columns):
                at = (idx * columns + col) * 128
                ref[col, start : start + count, :] = values[:, at : at + 128]

    def small(first, count):
        return table_ref[first : first + count, 256 + lanes : 256 + lanes + 3 * CORE]

    forward = small(0, 2 * CORE)
    back_y = small(2 * CORE, 2 * side)
    first = 2 * CORE + 2 * side
    back_x = jnp.where(is_lower, small(first, 2 * kept), small(first + 2 * kept, 2 * kept))
    for first in range(0, CORE, group):
        starts = [x * pitch for x in range(first, first + group)]
        both = dot(forward, stacked(side_by_side(rows_ref, starts, 1, CORE)))
        scatter(waves_ref, starts, jnp.where(even_y, both[:CORE], both[CORE:]), CORE)

    for first in range(0, CORE, group):
        waves_y = list(range(first, first + group))
        both = dot(forward, stacked(side_by_side(waves_ref, waves_y, pitch, CORE)))
        modes = jnp.where(even_x, both[:CORE], both[CORE:])
        scale = jnp.concatenate([factor_ref[wave * CORE : (wave + 1) * CORE] for wave in waves_y], 1)
        both = dot(back_x, stacked(modes * scale))
        scatter(mixed_ref, [wave * pitch for wave in waves_y], jnp.where(even_x, both[:kept], both[kept:]), kept)

    for level in range(pk.depth):
        rows = [block * pk.depth + level for block in range(pk.blocks)]
        rows = [row for row in rows if row < pk.rows]
        for first in range(0, len(rows), group):
            taken = rows[first : first + group]
            both = dot(back_y, stacked(side_by_side(mixed_ref, taken, pitch, CORE)))
            width = both.shape[1]
            field = jnp.where(even_y[:, :width], both[:side], both[side:])
            for idx in range(len(taken)):
                flat_ref[first + idx, level * side : (level + 1) * side, :] = field[:, idx * lanes : (idx + 1) * lanes]
        for block in range(len(rows), pk.blocks):
            flat_ref[block, level * side : (level + 1) * side, :] = jnp.zeros((side, lanes), jnp.float32)

    pieces = []
    for block in range(pk.blocks):
        pieces += split2(flat_ref[block])
    product = dot(jnp.concatenate(pieces, 1), table_ref[0 : pk.blocks * 2 * lanes, 0:256])
    hartree = product[:, 0:128] + product[:, 128:256]
    pieces = []
    for at_z in range(blocks_z):
        pieces += split3(near_dens_ref[at_z])
    density = dot(jnp.concatenate(pieces, 1), table_ref[blocks_z * 3 * 128 : blocks_z * 6 * 128, 256:384])
    added = (hartree + EXCHANGE_COEF * cube_root(density)) * (2.0 / HALF_WIDTH)
    for level in range(pk.depth):
        coef_ref[level] = start_coef_ref[level] + added[level * side : (level + 1) * side]

    clear_margins(pk, one_ref)
    clear_margins(pk, two_ref)
    filtered_field(pk, field_ref, one_ref, two_ref, coef_ref)

    for row in range(half):
        at = row + jnp.where(is_lower, 0, DEG)
        shift = 128 * pk.blocks - at // pk.depth * span
        own_ref[row * side : (row + 1) * side, :] = pltpu.roll(
            two_ref[at % pk.depth, 8 : 8 + side, :], shift % 128, 1
        )
    cells = side * side
    parts = [roll(own_ref[pl.ds(y, half, stride=side), :], y * side) for y in range(side)]
    for tile in range(-(-cells // 128)):
        first, last = tile * 128 // side, min(side - 1, (tile * 128 + 127) // side)
        lane = lanes_of((half, 128)) + tile * 128
        total = None
        for y in range(first, last + 1):
            total = parts[y] if total is None else jnp.where(lane >= y * side, parts[y], total)
        width = min(128, cells - tile * 128)
        out_ref[:, 0, tile * 128 : tile * 128 + width] = total[:, :width]


SMEM = pl.BlockSpec(memory_space=pltpu.SMEM)
VMEM = pl.BlockSpec(memory_space=pltpu.VMEM)
HBM = pl.BlockSpec(memory_space=pltpu.HBM)
params = pltpu.CompilerParams(vmem_limit_bytes=32 * 1024 * 1024)


def in_vmem(*shape):
    return pltpu.VMEM(shape, jnp.float32)


def in_hbm(value):
    return pltpu.with_memory_space_constraint(value, pltpu.HBM)


def local(psi_in, v_in, offsets):
    band_count = lax.axis_size("band")
    dom_count = lax.axis_size("dom")
    dom_idx = lax.axis_index("dom")
    slab_idx = lax.axis_index("band") % 2
    is_lower = slab_idx == 0
    slab_scalar = slab_idx.astype(jnp.int32).reshape(1)
    side = v_in.shape[1]
    pk = Packing(side)
    half = side // 2
    cells = side * side
    bands = band_count // 2
    grid_z = CORE * dom_count // 4
    lanes = 4 * grid_z
    slab_rows = CORE // 2 * 8

    f32, bf16 = jnp.float32, jnp.bfloat16
    field_type = in_vmem(*pk.shape)
    padded_field = pltpu.VMEM(pk.padded_shape, f32)

    rows = psi_in.reshape(half, 1, cells)
    rows = in_hbm(rows)
    edge = pl.pallas_call(
        functools.partial(edge_kernel, pk),
        out_shape=in_vmem(DEG, 1, cells),
        in_specs=[SMEM, HBM],
        out_specs=VMEM,
        scratch_shapes=[pltpu.SemaphoreType.DMA],
        compiler_params=params,
    )(slab_scalar, rows)
    halo = swapped(edge, "band", 1)
    masks = [0]
    bit = dom_count // 2
    while bit:
        masks = masks + [one | bit for one in masks]
        bit //= 2
    dom_scalar = dom_idx.astype(jnp.int32).reshape(1)
    start, coef, code = pl.pallas_call(
        functools.partial(start_kernel, pk, masks),
        out_shape=(field_type, field_type, in_vmem(8, 128)),
        in_specs=[SMEM, SMEM, HBM, HBM, HBM],
        out_specs=(VMEM, VMEM, VMEM),
        scratch_shapes=[
            pltpu.VMEM((pk.rows, cells), f32),
            pltpu.VMEM((side * pk.pitch, 128), f32),
            pltpu.VMEM((half, 1, cells), f32),
            pltpu.VMEM((side, cells), f32),
            pltpu.SMEM((dom_count, 3), jnp.int32),
            pltpu.SemaphoreType.DMA((3,)),
        ],
        compiler_params=params,
    )(slab_scalar, dom_scalar, rows, in_hbm(v_in[0]), in_hbm(offsets))

    padded_type = in_vmem(*pk.padded_shape)
    filt, dens = pl.pallas_call(
        functools.partial(first_kernel, pk, bands),
        out_shape=(padded_type, in_vmem(slab_rows, 128)),
        in_specs=[SMEM, VMEM, VMEM, VMEM],
        out_specs=(VMEM, VMEM),
        scratch_shapes=[padded_field, padded_field, pltpu.VMEM((side * DEG, 128), f32)],
        compiler_params=params,
    )(slab_scalar, start, halo, coef)
    edge = pl.pallas_call(
        functools.partial(send_kernel, pk),
        out_shape=in_vmem(pk.edge_groups * side, 128),
        in_specs=[SMEM, VMEM],
        out_specs=VMEM,
        compiler_params=params,
    )(slab_scalar, filt)

    mask = 2
    while mask < band_count:
        dens = dens + swapped(dens, "band", mask)
        mask *= 2

    far = dom_count // 2
    both = ("dom", "band")
    count = dom_count * band_count

    def crossed(value, mask):
        return lax.ppermute(value, both, [(source, source ^ mask) for source in range(count)])

    beside_all = crossed(jnp.concatenate([dens, edge], 0), 1)
    beside = beside_all[:slab_rows]
    across = crossed(dens, far * band_count)
    diagonal = crossed(dens, far * band_count + 1)

    def cube_of(own, other):
        return jnp.concatenate([jnp.where(is_lower, own, other), jnp.where(is_lower, other, own)], 0)

    cubes = jnp.stack([cube_of(dens, beside), cube_of(across, diagonal)])
    bit = far // 2
    while bit:
        if bit > 1:
            cubes = jnp.concatenate([cubes, swapped(cubes, "dom", bit)], 0)
        bit //= 2
    cubes_across = swapped(cubes, "dom", 1)

    field, mean = pl.pallas_call(
        functools.partial(take_kernel, pk),
        out_shape=(padded_type, in_vmem(8, 128)),
        in_specs=[SMEM, VMEM, VMEM, VMEM],
        out_specs=(VMEM, VMEM),
        compiler_params=params,
    )(slab_scalar, filt, beside_all, cubes)
    table, factor = solver_tables(side, grid_z)
    pitch = CORE + 8
    result = pl.pallas_call(
        functools.partial(second_kernel, pk, dom_count),
        out_shape=jax.ShapeDtypeStruct((half, 1, cells), f32),
        in_specs=[SMEM] + [VMEM] * 8,
        out_specs=VMEM,
        scratch_shapes=[
            pltpu.VMEM((dom_count, CORE * 8, 128), f32),
            padded_field,
            padded_field,
            pltpu.VMEM(pk.shape, f32),
            pltpu.VMEM((4 * CORE * 8, dom_count // 4 * 3 * 128), bf16),
            pltpu.VMEM((lanes // 128, CORE * pitch, 128), f32),
            pltpu.VMEM((lanes // 128, CORE * pitch, 128), f32),
            pltpu.VMEM((lanes // 128, CORE * pitch, 128), f32),
            pltpu.VMEM((pk.blocks, pk.depth * side, lanes), f32),
            pltpu.VMEM((dom_count // 4, pk.depth * side, 128), f32),
            pltpu.VMEM((half * side, 128), f32),
        ],
        compiler_params=params,
    )(
        slab_scalar, code, mean, cubes, cubes_across, field, coef,
        jnp.asarray(table), jnp.asarray(factor),
    )
    return result.reshape(1, 1, half, cells)


def solution(mesh):
    in_specs = (P("dom", "band", None, None), P("dom", None, None), P())
    out_specs = P("dom", "band", None, None)
    return jax.shard_map(local, mesh=mesh, in_specs=in_specs, out_specs=out_specs, check_vma=False)
```

```python
import functools
import math

import jax
import jax.numpy as jnp
import ml_dtypes
import numpy as np
from jax import lax
from jax.experimental import pallas as pl
from jax.experimental.pallas import tpu as pltpu
from jax.sharding import PartitionSpec as P

CORE = 32
BUF = 4
DEG = 8

HALF_WIDTH = 4.5
FOUR_PI = 4.0 * math.pi
EXCHANGE_COEF = -((3.0 / math.pi) ** (1.0 / 3.0))


def swapped(value, axis, mask):
    pairs = [(source, source ^ mask) for source in range(lax.axis_size(axis))]
    return lax.ppermute(value, axis, pairs)


def wave_basis(length):
    cells = np.arange(length)
    rows, waves = [], []
    for wave in range(length // 2 + 1):
        angle = 2.0 * np.pi * ((wave * cells) % length) / length
        if wave in (0, length // 2):
            rows.append(np.cos(angle) / np.sqrt(length))
            waves.append(wave)
        else:
            rows.append(np.cos(angle) * np.sqrt(2.0 / length))
            rows.append(np.sin(angle) * np.sqrt(2.0 / length))
            waves += [wave, wave]
    return np.array(rows), np.array(waves)


def parity_basis():
    rows, waves = wave_basis(2 * CORE)
    return np.stack([rows[waves % 2 == 0], rows[waves % 2 == 1]]), np.stack(
        [waves[waves % 2 == 0], waves[waves % 2 == 1]]
    )


def eigenvalue(waves, length):
    return 2.0 - 2.0 * np.cos(2.0 * np.pi * waves / length)


def padded(length, unit):
    return -(-length // unit) * unit


class Packing:
    def __init__(self, side):
        self.side = side
        self.half = side // 2
        self.rows = self.half + DEG
        self.blocks = 128 // (side + 1)
        self.span = 128 // self.blocks
        self.depth = -(-self.rows // self.blocks)
        self.shape = (self.depth, side, 128)
        self.padded_shape = (self.depth, side + 16, 128)
        self.edge_groups = -(-DEG // self.blocks)
        self.pitch = padded(self.rows, 16) + 8

    def where(self, row):
        return row // self.depth, row % self.depth


def lanes_of(shape):
    return lax.broadcasted_iota(jnp.int32, shape, len(shape) - 1)


def roll(values, shift):
    return values if isinstance(shift, int) and shift % 128 == 0 else pltpu.roll(values, shift % 128, 1)


def pack(pk, flat, pitched_ref, field_ref):
    count = flat.shape[0]
    for y in range(pk.side):
        pitched_ref[y * pk.pitch : y * pk.pitch + count, 0 : pk.side] = flat[:, y * pk.side : (y + 1) * pk.side]
    for level in range(pk.depth):
        total = None
        for block in range(pk.blocks):
            row = block * pk.depth + level
            if row < pk.rows:
                part = roll(pitched_ref[pl.ds(row, pk.side, stride=pk.pitch), :], block * pk.span)
                total = part if total is None else total + part
        field_ref[level] = total


def edge_kernel(pk, slab_ref, psi_ref, edge_ref, sem):
    first = jnp.where(slab_ref[0] == 0, pk.half - DEG, 0)
    copy = pltpu.make_async_copy(psi_ref.at[pl.ds(first, DEG)], edge_ref, sem)
    copy.start()
    copy.wait()


def start_kernel(
    pk, masks, slab_ref, dom_ref, psi_in_ref, pot_in_ref, offsets_in_ref,
    field_ref, coef_ref, code_ref, flat_ref, pitched_ref, psi_ref, pot_ref, offsets_ref, sems,
):
    psi_copy = pltpu.make_async_copy(psi_in_ref, psi_ref, sems.at[2])
    copy = pltpu.make_async_copy(pot_in_ref, pot_ref, sems.at[0])
    psi_copy.start()
    offsets_copy = pltpu.make_async_copy(offsets_in_ref, offsets_ref, sems.at[1])
    copy.start()
    offsets_copy.start()
    half, side = pk.half, pk.side
    cells = side * side
    is_lower = slab_ref[0] == 0
    flat_ref[...] = jnp.zeros(flat_ref.shape, jnp.float32)
    pitched_ref[...] = jnp.zeros(pitched_ref.shape, jnp.float32)
    psi_copy.wait()
    own = psi_ref[:, 0, :]

    @pl.when(is_lower)
    def _():
        flat_ref[0:half] = own

    @pl.when(jnp.logical_not(is_lower))
    def _():
        flat_ref[DEG : DEG + half] = own

    pack(pk, flat_ref[...], pitched_ref, field_ref)
    copy.wait()

    @pl.when(is_lower)
    def _():
        flat_ref[0 : pk.rows] = pot_ref[0 : pk.rows] * (2.0 / HALF_WIDTH)

    @pl.when(jnp.logical_not(is_lower))
    def _():
        flat_ref[0 : pk.rows] = pot_ref[side - pk.rows : side] * (2.0 / HALF_WIDTH)

    pack(pk, flat_ref[...], pitched_ref, coef_ref)

    offsets_copy.wait()
    dom, dom_count = dom_ref[0], len(masks)
    blocks_z = dom_count // 4
    code = jnp.int32(0)
    for idx, mask in enumerate(masks):
        other = dom ^ mask
        at_x = (offsets_ref[other, 0] != offsets_ref[dom, 0]).astype(jnp.int32)
        at_y = (offsets_ref[other, 1] != offsets_ref[dom, 1]).astype(jnp.int32)
        at_z = (offsets_ref[other, 2] - offsets_ref[dom, 2]) // CORE
        at_z = jnp.where(at_z < 0, at_z + blocks_z, at_z)
        place = (at_z * 2 + at_y) * 2 + at_x
        for where in range(dom_count):
            code = code + jnp.where(place == where, idx * dom_count**where, 0)
    code_ref[...] = jnp.full(code_ref.shape, code.astype(jnp.float32))


def filtered_field(pk, start_ref, one_ref, two_ref, coef_ref):
    lane = lanes_of((8, 128))
    is_cell = (lane % pk.span < pk.side) & (lane < pk.blocks * pk.span)
    full_weight = jnp.where(is_cell, 1.0 / HALF_WIDTH, 0.0)
    part_weight = jnp.where(is_cell & (lane < (pk.blocks - 1) * pk.span), 1.0 / HALF_WIDTH, 0.0)
    after_first = lane >= pk.span
    before_last = lane < (pk.blocks - 1) * pk.span
    previous_ref, current_ref = None, start_ref
    for order in range(DEG):
        target_ref = (one_ref, two_ref)[order % 2]
        for tile in range(pk.side // 8):
            at = 8 + 8 * tile
            values = [current_ref[level, at : at + 8, :] for level in range(pk.depth)]
            before = jnp.where(after_first, roll(values[-1], pk.span), 0.0)
            after = jnp.where(before_last, roll(values[0], -pk.span), 0.0)
            around = [before] + values + [after]
            for level in range(pk.depth):
                value = values[level]
                total = around[level] + around[level + 2]
                total = total + (
                    current_ref[level, at - 1 : at + 7, :] + current_ref[level, at + 1 : at + 9, :]
                )
                total = total + (roll(value, 1) + roll(value, -1))
                weight = full_weight if (pk.blocks - 1) * pk.depth + level < pk.rows else part_weight
                following = coef_ref[level, at - 8 : at, :] * value - weight * total
                if order == 0:
                    following = 0.5 * following
                else:
                    following = following - previous_ref[level, at : at + 8, :]
                target_ref[level, at : at + 8, :] = following
        previous_ref, current_ref = current_ref, target_ref


def clear_margins(pk, ref):
    zeros = jnp.zeros((pk.depth, 8, 128), jnp.float32)
    ref[:, 0:8, :] = zeros
    ref[:, 8 + pk.side : 16 + pk.side, :] = zeros


def first_kernel(
    pk, bands, slab_ref, start_ref, halo_ref, coef_ref, filt_ref, dens_ref, field_ref, one_ref, lines_ref
):
    side, span = pk.side, pk.span
    slab = slab_ref[0]
    is_lower = slab == 0
    clear_margins(pk, field_ref)
    clear_margins(pk, one_ref)
    clear_margins(pk, filt_ref)
    field_ref[:, 8 : 8 + side, :] = start_ref[...]
    low_block, low_level = pk.where(pk.half)
    high_block, high_level = pk.where(0)
    shift = jnp.where(is_lower, low_block * span, high_block * span)
    past = lanes_of((DEG, 128)) - shift
    is_line = (past >= 0) & (past < side)
    cells = side * side
    tiles = []
    for tile in range(-(-cells // 128)):
        width = min(128, cells - tile * 128)
        part = halo_ref[:, 0, tile * 128 : tile * 128 + width]
        tiles.append(part if width == 128 else jnp.concatenate([part, jnp.zeros((DEG, 128 - width), jnp.float32)], 1))
    for y in range(side):
        tile, start = y * side // 128, y * side % 128
        line = pltpu.roll(tiles[tile], shift + (128 - start), 1)
        if start + side > 128:
            line = jnp.where(past < 128 - start, line, pltpu.roll(tiles[tile + 1], shift + (128 - start), 1))
        lines_ref[y * DEG : (y + 1) * DEG, :] = jnp.where(is_line, line, 0.0)
    for row in range(DEG):
        level = jnp.where(is_lower, low_level, high_level) + row
        line = lines_ref[pl.ds(row, side, stride=DEG), :]
        field_ref[level, 8 : 8 + side, :] = field_ref[level, 8 : 8 + side, :] + line

    filtered_field(pk, field_ref, one_ref, filt_ref, coef_ref)
    result_ref = filt_ref

    lane = lanes_of((8, 128))
    lines = 128 // CORE
    for cell in range(CORE // 2):
        row = cell + jnp.where(is_lower, BUF, DEG)
        block, level = row // pk.depth, row % pk.depth
        total = jnp.zeros((8, 128), jnp.float32)
        for line in range(lines):
            value = result_ref[level, 8 + BUF + 8 * line : 16 + BUF + 8 * line, :]
            shift = line * CORE - BUF - block * span + 128 * pk.blocks
            total = jnp.where(lane // CORE == line, pltpu.roll(value, shift % 128, 1), total)
        dens_ref[cell * 8 : (cell + 1) * 8] = total * total * (1.0 / bands)


def send_kernel(pk, slab_ref, result_ref, edge_ref):
    side, span = pk.side, pk.span
    is_lower = slab_ref[0] == 0
    lane = lanes_of((side, 128))
    for group in range(pk.edge_groups):
        total = jnp.zeros((side, 128), jnp.float32)
        for slot in range(min(pk.blocks, DEG - group * pk.blocks)):
            row = group * pk.blocks + slot + jnp.where(is_lower, pk.half - DEG, DEG)
            shift = slot * span - row // pk.depth * span + 128 * pk.blocks
            line = pltpu.roll(result_ref[row % pk.depth, 8 : 8 + side, :], shift % 128, 1)
            total = jnp.where((lane >= slot * span) & (lane < slot * span + side), line, total)
        edge_ref[group * side : (group + 1) * side] = total


def take_kernel(pk, slab_ref, filt_ref, beside_ref, near_ref, field_ref, mean_ref):
    mean_ref[...] = jnp.full(mean_ref.shape, jnp.mean(near_ref[...]))
    side, span, half = pk.side, pk.span, pk.half
    is_lower = slab_ref[0] == 0
    field_ref[...] = filt_ref[...]
    lane = lanes_of((side, 128))
    base = CORE // 2 * 8
    for row in range(DEG):
        group_at, slot = row // pk.blocks, row % pk.blocks
        line = beside_ref[base + group_at * side : base + (group_at + 1) * side, :]
        for wanted, (block, level) in ((True, pk.where(half + row)), (False, pk.where(row))):
            here = (lane >= block * span) & (lane < block * span + side) & (is_lower == wanted)
            old = field_ref[level, 8 : 8 + side, :]
            field_ref[level, 8 : 8 + side, :] = jnp.where(here, roll(line, (block - slot) * span), old)


def split2(values):
    high = values.astype(jnp.bfloat16)
    return high, (values - high.astype(jnp.float32)).astype(jnp.bfloat16)


def split3(values):
    high = values.astype(jnp.bfloat16)
    rest = values - high.astype(jnp.float32)
    middle = rest.astype(jnp.bfloat16)
    return high, middle, (rest - middle.astype(jnp.float32)).astype(jnp.bfloat16)


def dot(left, right):
    return jnp.dot(left, right, preferred_element_type=jnp.float32)


def table_parts(table):
    high = table.astype(ml_dtypes.bfloat16)
    return high, (table - high.astype(np.float64)).astype(ml_dtypes.bfloat16)


def left_table(table):
    high, low = table_parts(table)
    return np.concatenate([high, low, high], -1)


def stacked(values):
    high, low = split2(values)
    return jnp.concatenate([high, high, low], 0)


@functools.lru_cache(maxsize=None)
def solver_tables(side, grid_z):
    pk = Packing(side)
    blocks_z = grid_z // CORE
    lanes = 4 * grid_z
    basis, waves = parity_basis()
    z_basis, z_waves = wave_basis(grid_z)
    lines = 128 // CORE
    into = []
    for place_z in range(blocks_z):
        along_z = z_basis[:, place_z * CORE : (place_z + 1) * CORE].T
        high, low = table_parts(np.kron(np.eye(lines), along_z))
        into += [high, high, low]
    into = np.concatenate(into, 0)
    region = np.arange(side) - BUF
    outer = basis[:, :, region % (2 * CORE)]
    small = [left_table(np.concatenate([basis[0, :, :CORE], basis[1, :, :CORE]], 0))]
    small.append(left_table(np.concatenate([outer[0].T, outer[1].T], 0)))
    for first_row in (0, side - pk.rows):
        rows = outer[:, :, first_row : first_row + pk.rows]
        rows = np.pad(rows, ((0, 0), (0, 0), (0, padded(pk.rows, 8) - pk.rows)))
        small.append(left_table(np.concatenate([rows[0].T, rows[1].T], 0)))
    small = np.concatenate(small, 0)
    back_z = []
    spread = np.zeros((blocks_z, 3, 128, 128))
    for block in range(pk.blocks):
        start = block * pk.span
        table = np.zeros((4, grid_z, 128))
        table[:, :, start : start + side] = z_basis[:, region % grid_z]
        high, low = table_parts(table.reshape(lanes, 128))
        back_z.append(np.block([[high, low], [high, np.zeros_like(low)]]))
        for cell, pos in enumerate(region % grid_z):
            spread[pos // CORE, :, block * CORE + pos % CORE, start + cell] = 1.0
    back_z = np.concatenate(back_z, 0)
    spread = spread.reshape(blocks_z * 3 * 128, 128).astype(ml_dtypes.bfloat16)
    eigen = eigenvalue(waves, 2 * CORE)
    lam = (
        eigen.T[:, None, None, :, None]
        + eigen.T[None, :, :, None, None]
        + eigenvalue(z_waves, grid_z)[None, None, None, None, :]
    )
    lam[0, 0, 0, 0, 0] = np.inf
    factor = (FOUR_PI / lam).reshape(CORE * CORE, lanes).astype(np.float32)
    pieces = [back_z, np.concatenate([into, np.pad(spread, ((0, 0), (0, lanes - 128)))], 0), small]
    height = max(len(piece) for piece in pieces)
    pieces = [np.pad(piece, ((0, height - len(piece)), (0, -piece.shape[1] % 128))) for piece in pieces]
    return np.concatenate(pieces, 1), factor


def cube_root(values):
    positive = values > 0.0
    safe = jnp.where(positive, values, 1.0)
    root = jnp.exp(jnp.log(safe) * (1.0 / 3.0))
    root = root - (root - safe / (root * root)) * (1.0 / 3.0)
    return jnp.where(positive, root, 0.0)


def second_kernel(
    pk, dom_count, slab_ref, code_ref, mean_ref, field_ref, start_coef_ref, table_ref, factor_ref, *refs
):
    gathered_refs, refs = refs[:dom_count], refs[dom_count:]
    (
        out_ref, cubes_ref, one_ref, two_ref, coef_ref, left_ref, rows_ref, waves_ref, mixed_ref, flat_ref,
        near_dens_ref, own_ref,
    ) = refs
    side, half, span = pk.side, pk.half, pk.span
    is_lower = slab_ref[0] == 0
    blocks_z = dom_count // 4
    grid_z = CORE * blocks_z
    lanes = 4 * grid_z
    columns = lanes // 128
    lines = 128 // CORE
    pitch = CORE + 8
    kept = padded(pk.rows, 8)

    near_count = dom_count // 2
    early_ref, late_ref = gathered_refs[near_count : near_count + 2]
    whole, part = CORE * 8, CORE * 4
    for idx, ref in enumerate(gathered_refs):
        if idx not in (near_count, near_count + 1):
            cubes_ref[idx] = ref[...]
    cubes_ref[near_count] = early_ref[0:whole]
    own_part, other_part = early_ref[whole : whole + part], late_ref[...]
    cubes_ref[near_count + 1, 0:part] = jnp.where(is_lower, own_part, other_part)
    cubes_ref[near_count + 1, part:whole] = jnp.where(is_lower, other_part, own_part)
    mean = 4.0 * jnp.concatenate([mean_ref[...]] * CORE, 0)
    code = jnp.max(code_ref[...]).astype(jnp.int32)
    cube_at = [code // dom_count**where % dom_count for where in range(dom_count)]

    for at_z in range(blocks_z):
        near, at_x, at_y, at_xy = [cubes_ref[cube_at[at_z * 4 + place]] for place in range(4)]
        sums, others = near + at_x, at_y + at_xy
        diffs, other_diffs = near - at_x, at_y - at_xy
        parities = (sums + others - mean, sums - others, diffs + other_diffs, diffs - other_diffs)
        for parity, value in enumerate(parities):
            high, low = split2(value)
            for idx, piece in enumerate((high, low, high)):
                cols = slice((at_z * 3 + idx) * 128, (at_z * 3 + idx + 1) * 128)
                left_ref[parity * CORE * 8 : (parity + 1) * CORE * 8, cols] = piece
    product = dot(left_ref[...], table_ref[0 : blocks_z * 3 * 128, 256 : 256 + lanes])
    lane = lanes_of((8, 128))
    for x in range(CORE):
        for line in range(lines):
            for col in range(columns):
                total = None
                for parity in range(4):
                    into = parity * grid_z - col * 128
                    if 0 <= into < 128:
                        at = line * grid_z
                        part = product[(parity * CORE + x) * 8 : (parity * CORE + x + 1) * 8, at // 128 * 128 : at // 128 * 128 + 128]
                        part = roll(part, into - at % 128)
                        total = part if total is None else jnp.where(lane >= into, part, total)
                rows_ref[col, x * pitch + line * 8 : x * pitch + line * 8 + 8, :] = total

    lane = lanes_of((8, 128))
    for at_z in range(blocks_z):
        for level in range(pk.depth):
            inner, low_wrap, high_wrap = [], None, None
            for block in range(pk.blocks):
                row = block * pk.depth + level
                if row >= pk.rows:
                    continue
                x = row - BUF + jnp.where(is_lower, 0, side - pk.rows)
                inside = (x >= 0) & (x < CORE)
                cell = pl.multiple_of((x + CORE) % CORE * 8, 8)

                def source(at_y):
                    place = (at_z * 2 + at_y) * 2
                    cube = jnp.where(inside, cube_at[place], cube_at[place + 1])
                    return cubes_ref[cube, pl.ds(cell, 8), :]

                def put(value, line, total):
                    value = roll(value, (block - line) * CORE)
                    return jnp.where((lane >= block * CORE) & (lane < (block + 1) * CORE), value, total)

                own, beside = source(0), source(1)
                zeros = jnp.zeros((8, 128), jnp.float32)
                inner = inner or [zeros] * lines
                inner = [put(own, line, total) for line, total in enumerate(inner)]
                low_wrap = put(beside, lines - 1, zeros if low_wrap is None else low_wrap)
                high_wrap = put(beside, 0, zeros if high_wrap is None else high_wrap)
            base = level * side
            near_dens_ref[at_z, base : base + BUF, :] = low_wrap[8 - BUF :]
            for line in range(lines):
                near_dens_ref[at_z, base + BUF + 8 * line : base + BUF + 8 * line + 8, :] = inner[line]
            near_dens_ref[at_z, base + BUF + CORE : base + side, :] = high_wrap[:BUF]

    group = max(1, 256 // lanes)
    lane_id = lanes_of((1, group * lanes)) % lanes
    even_x = lane_id < 2 * grid_z
    even_y = (lane_id // grid_z) % 2 == 0

    def side_by_side(ref, starts, stride, count):
        pieces = []
        for start in starts:
            for col in range(columns):
                if stride == 1:
                    pieces.append(ref[col, pl.ds(start, count), :])
                else:
                    pieces.append(ref[col, pl.ds(start, count, stride=stride), :])
        return jnp.concatenate(pieces, 1)

    def scatter(ref, starts, values, count):
        for idx, start in enumerate(starts):
            for col in range(columns):
                at = (idx * columns + col) * 128
                ref[col, start : start + count, :] = values[:, at : at + 128]

    def small(first, count):
        return table_ref[first : first + count, 256 + lanes : 256 + lanes + 3 * CORE]

    forward = small(0, 2 * CORE)
    back_y = small(2 * CORE, 2 * side)
    first = 2 * CORE + 2 * side
    back_x = jnp.where(is_lower, small(first, 2 * kept), small(first + 2 * kept, 2 * kept))
    for first in range(0, CORE, group):
        starts = [x * pitch for x in range(first, first + group)]
        both = dot(forward, stacked(side_by_side(rows_ref, starts, 1, CORE)))
        scatter(waves_ref, starts, jnp.where(even_y, both[:CORE], both[CORE:]), CORE)

    for first in range(0, CORE, group):
        waves_y = list(range(first, first + group))
        both = dot(forward, stacked(side_by_side(waves_ref, waves_y, pitch, CORE)))
        modes = jnp.where(even_x, both[:CORE], both[CORE:])
        scale = jnp.concatenate([factor_ref[wave * CORE : (wave + 1) * CORE] for wave in waves_y], 1)
        both = dot(back_x, stacked(modes * scale))
        scatter(mixed_ref, [wave * pitch for wave in waves_y], jnp.where(even_x, both[:kept], both[kept:]), kept)

    for level in range(pk.depth):
        rows = [block * pk.depth + level for block in range(pk.blocks)]
        rows = [row for row in rows if row < pk.rows]
        for first in range(0, len(rows), group):
            taken = rows[first : first + group]
            both = dot(back_y, stacked(side_by_side(mixed_ref, taken, pitch, CORE)))
            width = both.shape[1]
            field = jnp.where(even_y[:, :width], both[:side], both[side:])
            for idx in range(len(taken)):
                flat_ref[first + idx, level * side : (level + 1) * side, :] = field[:, idx * lanes : (idx + 1) * lanes]
        for block in range(len(rows), pk.blocks):
            flat_ref[block, level * side : (level + 1) * side, :] = jnp.zeros((side, lanes), jnp.float32)

    pieces = []
    for block in range(pk.blocks):
        pieces += split2(flat_ref[block])
    product = dot(jnp.concatenate(pieces, 1), table_ref[0 : pk.blocks * 2 * lanes, 0:256])
    hartree = product[:, 0:128] + product[:, 128:256]
    pieces = []
    for at_z in range(blocks_z):
        pieces += split3(near_dens_ref[at_z])
    density = dot(jnp.concatenate(pieces, 1), table_ref[blocks_z * 3 * 128 : blocks_z * 6 * 128, 256:384])
    added = (hartree + EXCHANGE_COEF * cube_root(density)) * (2.0 / HALF_WIDTH)
    for level in range(pk.depth):
        coef_ref[level] = start_coef_ref[level] + added[level * side : (level + 1) * side]

    clear_margins(pk, one_ref)
    clear_margins(pk, two_ref)
    filtered_field(pk, field_ref, one_ref, two_ref, coef_ref)

    for row in range(half):
        at = row + jnp.where(is_lower, 0, DEG)
        shift = 128 * pk.blocks - at // pk.depth * span
        own_ref[row * side : (row + 1) * side, :] = pltpu.roll(
            two_ref[at % pk.depth, 8 : 8 + side, :], shift % 128, 1
        )
    cells = side * side
    parts = [roll(own_ref[pl.ds(y, half, stride=side), :], y * side) for y in range(side)]
    for tile in range(-(-cells // 128)):
        first, last = tile * 128 // side, min(side - 1, (tile * 128 + 127) // side)
        lane = lanes_of((half, 128)) + tile * 128
        total = None
        for y in range(first, last + 1):
            total = parts[y] if total is None else jnp.where(lane >= y * side, parts[y], total)
        width = min(128, cells - tile * 128)
        out_ref[:, 0, tile * 128 : tile * 128 + width] = total[:, :width]


SMEM = pl.BlockSpec(memory_space=pltpu.SMEM)
VMEM = pl.BlockSpec(memory_space=pltpu.VMEM)
HBM = pl.BlockSpec(memory_space=pltpu.HBM)
params = pltpu.CompilerParams(vmem_limit_bytes=32 * 1024 * 1024)


def in_vmem(*shape):
    return pltpu.VMEM(shape, jnp.float32)


def in_hbm(value):
    return pltpu.with_memory_space_constraint(value, pltpu.HBM)


def local(psi_in, v_in, offsets):
    band_count = lax.axis_size("band")
    dom_count = lax.axis_size("dom")
    dom_idx = lax.axis_index("dom")
    slab_idx = lax.axis_index("band") % 2
    is_lower = slab_idx == 0
    slab_scalar = slab_idx.astype(jnp.int32).reshape(1)
    side = v_in.shape[1]
    pk = Packing(side)
    half = side // 2
    cells = side * side
    bands = band_count // 2
    grid_z = CORE * dom_count // 4
    lanes = 4 * grid_z
    slab_rows = CORE // 2 * 8

    f32, bf16 = jnp.float32, jnp.bfloat16
    field_type = in_vmem(*pk.shape)
    padded_field = pltpu.VMEM(pk.padded_shape, f32)

    rows = psi_in.reshape(half, 1, cells)
    rows = in_hbm(rows)
    edge = pl.pallas_call(
        functools.partial(edge_kernel, pk),
        out_shape=in_vmem(DEG, 1, cells),
        in_specs=[SMEM, HBM],
        out_specs=VMEM,
        scratch_shapes=[pltpu.SemaphoreType.DMA],
        compiler_params=params,
    )(slab_scalar, rows)
    halo = swapped(edge, "band", 1)
    masks = [dom_count // 2, 0]
    bit = dom_count // 4
    while bit:
        masks = masks + [one | bit for one in masks]
        bit //= 2
    dom_scalar = dom_idx.astype(jnp.int32).reshape(1)
    start, coef, code = pl.pallas_call(
        functools.partial(start_kernel, pk, masks),
        out_shape=(field_type, field_type, in_vmem(8, 128)),
        in_specs=[SMEM, SMEM, HBM, HBM, HBM],
        out_specs=(VMEM, VMEM, VMEM),
        scratch_shapes=[
            pltpu.VMEM((pk.rows, cells), f32),
            pltpu.VMEM((side * pk.pitch, 128), f32),
            pltpu.VMEM((half, 1, cells), f32),
            pltpu.VMEM((side, cells), f32),
            pltpu.SMEM((dom_count, 3), jnp.int32),
            pltpu.SemaphoreType.DMA((3,)),
        ],
        compiler_params=params,
    )(slab_scalar, dom_scalar, rows, in_hbm(v_in[0]), in_hbm(offsets))

    padded_type = in_vmem(*pk.padded_shape)
    filt, dens = pl.pallas_call(
        functools.partial(first_kernel, pk, bands),
        out_shape=(padded_type, in_vmem(slab_rows, 128)),
        in_specs=[SMEM, VMEM, VMEM, VMEM],
        out_specs=(VMEM, VMEM),
        scratch_shapes=[padded_field, padded_field, pltpu.VMEM((side * DEG, 128), f32)],
        compiler_params=params,
    )(slab_scalar, start, halo, coef)
    edge = pl.pallas_call(
        functools.partial(send_kernel, pk),
        out_shape=in_vmem(pk.edge_groups * side, 128),
        in_specs=[SMEM, VMEM],
        out_specs=VMEM,
        compiler_params=params,
    )(slab_scalar, filt)

    mask = 2
    while mask < band_count:
        dens = dens + swapped(dens, "band", mask)
        mask *= 2

    far = dom_count // 2
    both = ("dom", "band")
    count = dom_count * band_count

    def crossed(value, mask):
        return lax.ppermute(value, both, [(source, source ^ mask) for source in range(count)])

    beside_all = crossed(jnp.concatenate([dens, edge], 0), 1)
    beside = beside_all[:slab_rows]
    across = crossed(dens, far * band_count)
    diagonal = crossed(dens, far * band_count + 1)

    def cube_of(own, other):
        return jnp.concatenate([jnp.where(is_lower, own, other), jnp.where(is_lower, other, own)], 0)

    cubes = [cube_of(across, diagonal), cube_of(dens, beside)]
    bit = far // 2
    while bit > 1:
        cubes = cubes + [swapped(cube, "dom", bit) for cube in cubes]
        bit //= 2
    early = swapped(jnp.concatenate([cubes[0], dens], 0), "dom", 1)
    late = swapped(beside, "dom", 1)
    cubes_across = [early, late] + [swapped(cube, "dom", 1) for cube in cubes[2:]]

    field, mean = pl.pallas_call(
        functools.partial(take_kernel, pk),
        out_shape=(padded_type, in_vmem(8, 128)),
        in_specs=[SMEM, VMEM, VMEM, VMEM],
        out_specs=(VMEM, VMEM),
        compiler_params=params,
    )(slab_scalar, filt, beside_all, cubes[1])
    table, factor = solver_tables(side, grid_z)
    pitch = CORE + 8
    result = pl.pallas_call(
        functools.partial(second_kernel, pk, dom_count),
        out_shape=jax.ShapeDtypeStruct((half, 1, cells), f32),
        in_specs=[SMEM] + [VMEM] * (6 + dom_count),
        out_specs=VMEM,
        scratch_shapes=[
            pltpu.VMEM((dom_count, CORE * 8, 128), f32),
            padded_field,
            padded_field,
            pltpu.VMEM(pk.shape, f32),
            pltpu.VMEM((4 * CORE * 8, dom_count // 4 * 3 * 128), bf16),
            pltpu.VMEM((lanes // 128, CORE * pitch, 128), f32),
            pltpu.VMEM((lanes // 128, CORE * pitch, 128), f32),
            pltpu.VMEM((lanes // 128, CORE * pitch, 128), f32),
            pltpu.VMEM((pk.blocks, pk.depth * side, lanes), f32),
            pltpu.VMEM((dom_count // 4, pk.depth * side, 128), f32),
            pltpu.VMEM((half * side, 128), f32),
        ],
        compiler_params=params,
    )(
        slab_scalar, code, mean, field, coef, jnp.asarray(table), jnp.asarray(factor), *cubes, *cubes_across
    )
    return result.reshape(1, 1, half, cells)


def solution(mesh):
    in_specs = (P("dom", "band", None, None), P("dom", None, None), P())
    out_specs = P("dom", "band", None, None)
    return jax.shard_map(local, mesh=mesh, in_specs=in_specs, out_specs=out_specs, check_vma=False)
```

```python
import functools
import math

import jax
import jax.numpy as jnp
import ml_dtypes
import numpy as np
from jax import lax
from jax.experimental import pallas as pl
from jax.experimental.pallas import tpu as pltpu
from jax.sharding import PartitionSpec as P

CORE = 32
BUF = 4
DEG = 8

HALF_WIDTH = 4.5
FOUR_PI = 4.0 * math.pi
EXCHANGE_COEF = -((3.0 / math.pi) ** (1.0 / 3.0))


def swapped(value, axis, mask):
    pairs = [(source, source ^ mask) for source in range(lax.axis_size(axis))]
    return lax.ppermute(value, axis, pairs)


def wave_basis(length):
    cells = np.arange(length)
    rows, waves = [], []
    for wave in range(length // 2 + 1):
        angle = 2.0 * np.pi * ((wave * cells) % length) / length
        if wave in (0, length // 2):
            rows.append(np.cos(angle) / np.sqrt(length))
            waves.append(wave)
        else:
            rows.append(np.cos(angle) * np.sqrt(2.0 / length))
            rows.append(np.sin(angle) * np.sqrt(2.0 / length))
            waves += [wave, wave]
    return np.array(rows), np.array(waves)


def parity_basis():
    rows, waves = wave_basis(2 * CORE)
    return np.stack([rows[waves % 2 == 0], rows[waves % 2 == 1]]), np.stack(
        [waves[waves % 2 == 0], waves[waves % 2 == 1]]
    )


def eigenvalue(waves, length):
    return 2.0 - 2.0 * np.cos(2.0 * np.pi * waves / length)


def padded(length, unit):
    return -(-length // unit) * unit


class Packing:
    def __init__(self, side):
        self.side = side
        self.half = side // 2
        self.rows = self.half + DEG
        self.blocks = 128 // (side + 1)
        self.span = 128 // self.blocks
        self.depth = -(-self.rows // self.blocks)
        self.shape = (self.depth, side, 128)
        self.padded_shape = (self.depth, side + 16, 128)
        self.edge_groups = -(-DEG // self.blocks)
        self.pitch = padded(self.rows, 16) + 8

    def where(self, row):
        return row // self.depth, row % self.depth


def lanes_of(shape):
    return lax.broadcasted_iota(jnp.int32, shape, len(shape) - 1)


def roll(values, shift):
    return values if isinstance(shift, int) and shift % 128 == 0 else pltpu.roll(values, shift % 128, 1)


def pack(pk, flat, pitched_ref, field_ref):
    count = flat.shape[0]
    for y in range(pk.side):
        pitched_ref[y * pk.pitch : y * pk.pitch + count, 0 : pk.side] = flat[:, y * pk.side : (y + 1) * pk.side]
    for level in range(pk.depth):
        total = None
        for block in range(pk.blocks):
            row = block * pk.depth + level
            if row < pk.rows:
                part = roll(pitched_ref[pl.ds(row, pk.side, stride=pk.pitch), :], block * pk.span)
                total = part if total is None else total + part
        field_ref[level] = total


def edge_kernel(pk, slab_ref, psi_ref, edge_ref, sem):
    first = jnp.where(slab_ref[0] == 0, pk.half - DEG, 0)
    copy = pltpu.make_async_copy(psi_ref.at[pl.ds(first, DEG)], edge_ref, sem)
    copy.start()
    copy.wait()


def start_kernel(
    pk, masks, slab_ref, dom_ref, psi_in_ref, pot_in_ref, offsets_in_ref,
    field_ref, coef_ref, code_ref, flat_ref, pitched_ref, psi_ref, pot_ref, offsets_ref, sems,
):
    psi_copy = pltpu.make_async_copy(psi_in_ref, psi_ref, sems.at[2])
    copy = pltpu.make_async_copy(pot_in_ref, pot_ref, sems.at[0])
    psi_copy.start()
    offsets_copy = pltpu.make_async_copy(offsets_in_ref, offsets_ref, sems.at[1])
    copy.start()
    offsets_copy.start()
    half, side = pk.half, pk.side
    cells = side * side
    is_lower = slab_ref[0] == 0
    flat_ref[...] = jnp.zeros(flat_ref.shape, jnp.float32)
    pitched_ref[...] = jnp.zeros(pitched_ref.shape, jnp.float32)
    psi_copy.wait()
    own = psi_ref[:, 0, :]

    @pl.when(is_lower)
    def _():
        flat_ref[0:half] = own

    @pl.when(jnp.logical_not(is_lower))
    def _():
        flat_ref[DEG : DEG + half] = own

    pack(pk, flat_ref[...], pitched_ref, field_ref)
    copy.wait()

    @pl.when(is_lower)
    def _():
        flat_ref[0 : pk.rows] = pot_ref[0 : pk.rows] * (2.0 / HALF_WIDTH)

    @pl.when(jnp.logical_not(is_lower))
    def _():
        flat_ref[0 : pk.rows] = pot_ref[side - pk.rows : side] * (2.0 / HALF_WIDTH)

    pack(pk, flat_ref[...], pitched_ref, coef_ref)

    offsets_copy.wait()
    dom, dom_count = dom_ref[0], len(masks)
    blocks_z = dom_count // 4
    code = jnp.int32(0)
    for idx, mask in enumerate(masks):
        other = dom ^ mask
        at_x = (offsets_ref[other, 0] != offsets_ref[dom, 0]).astype(jnp.int32)
        at_y = (offsets_ref[other, 1] != offsets_ref[dom, 1]).astype(jnp.int32)
        at_z = (offsets_ref[other, 2] - offsets_ref[dom, 2]) // CORE
        at_z = jnp.where(at_z < 0, at_z + blocks_z, at_z)
        place = (at_z * 2 + at_y) * 2 + at_x
        for where in range(dom_count):
            code = code + jnp.where(place == where, idx * dom_count**where, 0)
    code_ref[...] = jnp.full(code_ref.shape, code.astype(jnp.float32))


def filtered_field(pk, start_ref, one_ref, two_ref, coef_ref):
    lane = lanes_of((8, 128))
    is_cell = (lane % pk.span < pk.side) & (lane < pk.blocks * pk.span)
    full_weight = jnp.where(is_cell, 1.0 / HALF_WIDTH, 0.0)
    part_weight = jnp.where(is_cell & (lane < (pk.blocks - 1) * pk.span), 1.0 / HALF_WIDTH, 0.0)
    after_first = lane >= pk.span
    before_last = lane < (pk.blocks - 1) * pk.span
    previous_ref, current_ref = None, start_ref
    for order in range(DEG):
        target_ref = (one_ref, two_ref)[order % 2]
        for tile in range(pk.side // 8):
            at = 8 + 8 * tile
            values = [current_ref[level, at : at + 8, :] for level in range(pk.depth)]
            before = jnp.where(after_first, roll(values[-1], pk.span), 0.0)
            after = jnp.where(before_last, roll(values[0], -pk.span), 0.0)
            around = [before] + values + [after]
            for level in range(pk.depth):
                value = values[level]
                total = around[level] + around[level + 2]
                total = total + (
                    current_ref[level, at - 1 : at + 7, :] + current_ref[level, at + 1 : at + 9, :]
                )
                total = total + (roll(value, 1) + roll(value, -1))
                weight = full_weight if (pk.blocks - 1) * pk.depth + level < pk.rows else part_weight
                following = coef_ref[level, at - 8 : at, :] * value - weight * total
                if order == 0:
                    following = 0.5 * following
                else:
                    following = following - previous_ref[level, at : at + 8, :]
                target_ref[level, at : at + 8, :] = following
        previous_ref, current_ref = current_ref, target_ref


def clear_margins(pk, ref):
    zeros = jnp.zeros((pk.depth, 8, 128), jnp.float32)
    ref[:, 0:8, :] = zeros
    ref[:, 8 + pk.side : 16 + pk.side, :] = zeros


def first_kernel(
    pk, bands, slab_ref, start_ref, halo_ref, coef_ref, filt_ref, dens_ref, field_ref, one_ref, lines_ref
):
    side, span = pk.side, pk.span
    slab = slab_ref[0]
    is_lower = slab == 0
    clear_margins(pk, field_ref)
    clear_margins(pk, one_ref)
    clear_margins(pk, filt_ref)
    field_ref[:, 8 : 8 + side, :] = start_ref[...]
    low_block, low_level = pk.where(pk.half)
    high_block, high_level = pk.where(0)
    shift = jnp.where(is_lower, low_block * span, high_block * span)
    past = lanes_of((DEG, 128)) - shift
    is_line = (past >= 0) & (past < side)
    cells = side * side
    tiles = []
    for tile in range(-(-cells // 128)):
        width = min(128, cells - tile * 128)
        part = halo_ref[:, 0, tile * 128 : tile * 128 + width]
        tiles.append(part if width == 128 else jnp.concatenate([part, jnp.zeros((DEG, 128 - width), jnp.float32)], 1))
    for y in range(side):
        tile, start = y * side // 128, y * side % 128
        line = pltpu.roll(tiles[tile], shift + (128 - start), 1)
        if start + side > 128:
            line = jnp.where(past < 128 - start, line, pltpu.roll(tiles[tile + 1], shift + (128 - start), 1))
        lines_ref[y * DEG : (y + 1) * DEG, :] = jnp.where(is_line, line, 0.0)
    for row in range(DEG):
        level = jnp.where(is_lower, low_level, high_level) + row
        line = lines_ref[pl.ds(row, side, stride=DEG), :]
        field_ref[level, 8 : 8 + side, :] = field_ref[level, 8 : 8 + side, :] + line

    filtered_field(pk, field_ref, one_ref, filt_ref, coef_ref)
    result_ref = filt_ref

    lane = lanes_of((8, 128))
    lines = 128 // CORE
    for lower, offset in ((True, BUF), (False, DEG)):

        @pl.when(is_lower == lower)
        def _(offset=offset):
            for cell in range(CORE // 2):
                block, level = pk.where(cell + offset)
                total = None
                for line in range(lines):
                    value = result_ref[level, 8 + BUF + 8 * line : 16 + BUF + 8 * line, :]
                    value = roll(value, line * CORE - BUF - block * span)
                    total = value if total is None else jnp.where(lane >= line * CORE, value, total)
                dens_ref[cell * 8 : (cell + 1) * 8] = total * total * (1.0 / bands)


def send_kernel(pk, slab_ref, result_ref, edge_ref):
    side, span = pk.side, pk.span
    is_lower = slab_ref[0] == 0
    lane = lanes_of((side, 128))
    for group in range(pk.edge_groups):
        total = jnp.zeros((side, 128), jnp.float32)
        for slot in range(min(pk.blocks, DEG - group * pk.blocks)):
            row = group * pk.blocks + slot + jnp.where(is_lower, pk.half - DEG, DEG)
            shift = slot * span - row // pk.depth * span + 128 * pk.blocks
            line = pltpu.roll(result_ref[row % pk.depth, 8 : 8 + side, :], shift % 128, 1)
            total = jnp.where((lane >= slot * span) & (lane < slot * span + side), line, total)
        edge_ref[group * side : (group + 1) * side] = total


def take_kernel(pk, slab_ref, filt_ref, beside_ref, near_ref, field_ref, mean_ref):
    mean_ref[...] = jnp.full(mean_ref.shape, jnp.mean(near_ref[...]))
    side, span, half = pk.side, pk.span, pk.half
    is_lower = slab_ref[0] == 0
    field_ref[...] = filt_ref[...]
    lane = lanes_of((side, 128))
    base = CORE // 2 * 8
    for row in range(DEG):
        group_at, slot = row // pk.blocks, row % pk.blocks
        line = beside_ref[base + group_at * side : base + (group_at + 1) * side, :]
        for wanted, (block, level) in ((True, pk.where(half + row)), (False, pk.where(row))):
            here = (lane >= block * span) & (lane < block * span + side) & (is_lower == wanted)
            old = field_ref[level, 8 : 8 + side, :]
            field_ref[level, 8 : 8 + side, :] = jnp.where(here, roll(line, (block - slot) * span), old)


def split2(values):
    high = values.astype(jnp.bfloat16)
    return high, (values - high.astype(jnp.float32)).astype(jnp.bfloat16)


def split3(values):
    high = values.astype(jnp.bfloat16)
    rest = values - high.astype(jnp.float32)
    middle = rest.astype(jnp.bfloat16)
    return high, middle, (rest - middle.astype(jnp.float32)).astype(jnp.bfloat16)


def dot(left, right):
    return jnp.dot(left, right, preferred_element_type=jnp.float32)


def table_parts(table):
    high = table.astype(ml_dtypes.bfloat16)
    return high, (table - high.astype(np.float64)).astype(ml_dtypes.bfloat16)


def left_table(table):
    high, low = table_parts(table)
    return np.concatenate([high, low, high], -1)


def stacked(values):
    high, low = split2(values)
    return jnp.concatenate([high, high, low], 0)


@functools.lru_cache(maxsize=None)
def solver_tables(side, grid_z):
    pk = Packing(side)
    blocks_z = grid_z // CORE
    lanes = 4 * grid_z
    basis, waves = parity_basis()
    z_basis, z_waves = wave_basis(grid_z)
    lines = 128 // CORE
    into = []
    for place_z in range(blocks_z):
        along_z = z_basis[:, place_z * CORE : (place_z + 1) * CORE].T
        high, low = table_parts(np.kron(np.eye(lines), along_z))
        into += [high, high, low]
    into = np.concatenate(into, 0)
    region = np.arange(side) - BUF
    outer = basis[:, :, region % (2 * CORE)]
    small = [left_table(np.concatenate([basis[0, :, :CORE], basis[1, :, :CORE]], 0))]
    small.append(left_table(np.concatenate([outer[0].T, outer[1].T], 0)))
    for first_row in (0, side - pk.rows):
        rows = outer[:, :, first_row : first_row + pk.rows]
        rows = np.pad(rows, ((0, 0), (0, 0), (0, padded(pk.rows, 8) - pk.rows)))
        small.append(left_table(np.concatenate([rows[0].T, rows[1].T], 0)))
    small = np.concatenate(small, 0)
    back_z = []
    spread = np.zeros((blocks_z, 3, 128, 128))
    for block in range(pk.blocks):
        start = block * pk.span
        table = np.zeros((4, grid_z, 128))
        table[:, :, start : start + side] = z_basis[:, region % grid_z]
        high, low = table_parts(table.reshape(lanes, 128))
        back_z.append(np.block([[high, low], [high, np.zeros_like(low)]]))
        for cell, pos in enumerate(region % grid_z):
            spread[pos // CORE, :, block * CORE + pos % CORE, start + cell] = 1.0
    back_z = np.concatenate(back_z, 0)
    spread = spread.reshape(blocks_z * 3 * 128, 128).astype(ml_dtypes.bfloat16)
    eigen = eigenvalue(waves, 2 * CORE)
    lam = (
        eigen.T[:, None, None, :, None]
        + eigen.T[None, :, :, None, None]
        + eigenvalue(z_waves, grid_z)[None, None, None, None, :]
    )
    lam[0, 0, 0, 0, 0] = np.inf
    factor = (FOUR_PI / lam).reshape(CORE * CORE, lanes).astype(np.float32)
    pieces = [back_z, np.concatenate([into, np.pad(spread, ((0, 0), (0, lanes - 128)))], 0), small]
    height = max(len(piece) for piece in pieces)
    pieces = [np.pad(piece, ((0, height - len(piece)), (0, -piece.shape[1] % 128))) for piece in pieces]
    return np.concatenate(pieces, 1), factor


def cube_root(values):
    positive = values > 0.0
    safe = jnp.where(positive, values, 1.0)
    root = jnp.exp(jnp.log(safe) * (1.0 / 3.0))
    root = root - (root - safe / (root * root)) * (1.0 / 3.0)
    return jnp.where(positive, root, 0.0)


def second_kernel(
    pk, dom_count, slab_ref, code_ref, mean_ref, field_ref, start_coef_ref, table_ref, factor_ref, *refs
):
    gathered_refs, refs = refs[:dom_count], refs[dom_count:]
    (
        out_ref, cubes_ref, one_ref, two_ref, coef_ref, left_ref, rows_ref, waves_ref, mixed_ref, flat_ref,
        near_dens_ref, own_ref,
    ) = refs
    side, half, span = pk.side, pk.half, pk.span
    is_lower = slab_ref[0] == 0
    blocks_z = dom_count // 4
    grid_z = CORE * blocks_z
    lanes = 4 * grid_z
    columns = lanes // 128
    lines = 128 // CORE
    pitch = CORE + 8
    kept = padded(pk.rows, 8)

    near_count = dom_count // 2
    early_ref, late_ref = gathered_refs[near_count : near_count + 2]
    whole, part = CORE * 8, CORE * 4
    for idx, ref in enumerate(gathered_refs):
        if idx not in (near_count, near_count + 1):
            cubes_ref[idx] = ref[...]
    cubes_ref[near_count] = early_ref[0:whole]
    own_part, other_part = early_ref[whole : whole + part], late_ref[...]
    cubes_ref[near_count + 1, 0:part] = jnp.where(is_lower, own_part, other_part)
    cubes_ref[near_count + 1, part:whole] = jnp.where(is_lower, other_part, own_part)
    mean = 4.0 * jnp.concatenate([mean_ref[...]] * CORE, 0)
    code = jnp.max(code_ref[...]).astype(jnp.int32)
    cube_at = [code // dom_count**where % dom_count for where in range(dom_count)]

    stacks = [[] for _ in range(4)]
    for at_z in range(blocks_z):
        near, at_x, at_y, at_xy = [cubes_ref[cube_at[at_z * 4 + place]] for place in range(4)]
        sums, others = near + at_x, at_y + at_xy
        diffs, other_diffs = near - at_x, at_y - at_xy
        parities = (sums + others - mean, sums - others, diffs + other_diffs, diffs - other_diffs)
        for parity, value in enumerate(parities):
            high, low = split2(value)
            stacks[parity] += [high, low, high]
    z_table = table_ref[0 : blocks_z * 3 * 128, 256 : 256 + lanes]
    product = jnp.concatenate([dot(jnp.concatenate(stack, 1), z_table) for stack in stacks], 0)
    lane = lanes_of((8, 128))
    for x in range(CORE):
        for line in range(lines):
            for col in range(columns):
                total = None
                for parity in range(4):
                    into = parity * grid_z - col * 128
                    if 0 <= into < 128:
                        at = line * grid_z
                        part = product[(parity * CORE + x) * 8 : (parity * CORE + x + 1) * 8, at // 128 * 128 : at // 128 * 128 + 128]
                        part = roll(part, into - at % 128)
                        total = part if total is None else jnp.where(lane >= into, part, total)
                rows_ref[col, x * pitch + line * 8 : x * pitch + line * 8 + 8, :] = total

    lane = lanes_of((8, 128))
    for at_z in range(blocks_z):
        for level in range(pk.depth):
            inner, low_wrap, high_wrap = [], None, None
            for block in range(pk.blocks):
                row = block * pk.depth + level
                if row >= pk.rows:
                    continue
                x = row - BUF + jnp.where(is_lower, 0, side - pk.rows)
                inside = (x >= 0) & (x < CORE)
                cell = pl.multiple_of((x + CORE) % CORE * 8, 8)

                def source(at_y):
                    place = (at_z * 2 + at_y) * 2
                    cube = jnp.where(inside, cube_at[place], cube_at[place + 1])
                    return cubes_ref[cube, pl.ds(cell, 8), :]

                def put(value, line, total):
                    value = roll(value, (block - line) * CORE)
                    return jnp.where((lane >= block * CORE) & (lane < (block + 1) * CORE), value, total)

                own, beside = source(0), source(1)
                zeros = jnp.zeros((8, 128), jnp.float32)
                inner = inner or [zeros] * lines
                inner = [put(own, line, total) for line, total in enumerate(inner)]
                low_wrap = put(beside, lines - 1, zeros if low_wrap is None else low_wrap)
                high_wrap = put(beside, 0, zeros if high_wrap is None else high_wrap)
            base = level * side
            near_dens_ref[at_z, base : base + BUF, :] = low_wrap[8 - BUF :]
            for line in range(lines):
                near_dens_ref[at_z, base + BUF + 8 * line : base + BUF + 8 * line + 8, :] = inner[line]
            near_dens_ref[at_z, base + BUF + CORE : base + side, :] = high_wrap[:BUF]

    group = max(1, 256 // lanes)
    lane_id = lanes_of((1, group * lanes)) % lanes
    even_x = lane_id < 2 * grid_z
    even_y = (lane_id // grid_z) % 2 == 0

    def side_by_side(ref, starts, stride, count):
        pieces = []
        for start in starts:
            for col in range(columns):
                if stride == 1:
                    pieces.append(ref[col, pl.ds(start, count), :])
                else:
                    pieces.append(ref[col, pl.ds(start, count, stride=stride), :])
        return jnp.concatenate(pieces, 1)

    def scatter(ref, starts, values, count):
        for idx, start in enumerate(starts):
            for col in range(columns):
                at = (idx * columns + col) * 128
                ref[col, start : start + count, :] = values[:, at : at + 128]

    def small(first, count):
        return table_ref[first : first + count, 256 + lanes : 256 + lanes + 3 * CORE]

    forward = small(0, 2 * CORE)
    back_y = small(2 * CORE, 2 * side)
    first = 2 * CORE + 2 * side
    back_x = jnp.where(is_lower, small(first, 2 * kept), small(first + 2 * kept, 2 * kept))
    for first in range(0, CORE, group):
        starts = [x * pitch for x in range(first, first + group)]
        both = dot(forward, stacked(side_by_side(rows_ref, starts, 1, CORE)))
        scatter(waves_ref, starts, jnp.where(even_y, both[:CORE], both[CORE:]), CORE)

    for first in range(0, CORE, group):
        waves_y = list(range(first, first + group))
        both = dot(forward, stacked(side_by_side(waves_ref, waves_y, pitch, CORE)))
        modes = jnp.where(even_x, both[:CORE], both[CORE:])
        scale = jnp.concatenate([factor_ref[wave * CORE : (wave + 1) * CORE] for wave in waves_y], 1)
        both = dot(back_x, stacked(modes * scale))
        scatter(mixed_ref, [wave * pitch for wave in waves_y], jnp.where(even_x, both[:kept], both[kept:]), kept)

    for level in range(pk.depth):
        rows = [block * pk.depth + level for block in range(pk.blocks)]
        rows = [row for row in rows if row < pk.rows]
        for first in range(0, len(rows), group):
            taken = rows[first : first + group]
            both = dot(back_y, stacked(side_by_side(mixed_ref, taken, pitch, CORE)))
            width = both.shape[1]
            field = jnp.where(even_y[:, :width], both[:side], both[side:])
            for idx in range(len(taken)):
                flat_ref[first + idx, level * side : (level + 1) * side, :] = field[:, idx * lanes : (idx + 1) * lanes]
        for block in range(len(rows), pk.blocks):
            flat_ref[block, level * side : (level + 1) * side, :] = jnp.zeros((side, lanes), jnp.float32)

    pieces = []
    for block in range(pk.blocks):
        pieces += split2(flat_ref[block])
    product = dot(jnp.concatenate(pieces, 1), table_ref[0 : pk.blocks * 2 * lanes, 0:256])
    hartree = product[:, 0:128] + product[:, 128:256]
    pieces = []
    for at_z in range(blocks_z):
        pieces += split3(near_dens_ref[at_z])
    density = dot(jnp.concatenate(pieces, 1), table_ref[blocks_z * 3 * 128 : blocks_z * 6 * 128, 256:384])
    added = (hartree + EXCHANGE_COEF * cube_root(density)) * (2.0 / HALF_WIDTH)
    for level in range(pk.depth):
        coef_ref[level] = start_coef_ref[level] + added[level * side : (level + 1) * side]

    clear_margins(pk, one_ref)
    clear_margins(pk, two_ref)
    filtered_field(pk, field_ref, one_ref, two_ref, coef_ref)

    for lower, offset in ((True, 0), (False, DEG)):

        @pl.when(is_lower == lower)
        def _(offset=offset):
            for row in range(half):
                block, level = pk.where(row + offset)
                own_ref[row * side : (row + 1) * side, :] = roll(two_ref[level, 8 : 8 + side, :], -block * span)

    cells = side * side
    parts = [roll(own_ref[pl.ds(y, half, stride=side), :], y * side) for y in range(side)]
    for tile in range(-(-cells // 128)):
        first, last = tile * 128 // side, min(side - 1, (tile * 128 + 127) // side)
        lane = lanes_of((half, 128)) + tile * 128
        total = None
        for y in range(first, last + 1):
            total = parts[y] if total is None else jnp.where(lane >= y * side, parts[y], total)
        width = min(128, cells - tile * 128)
        out_ref[:, 0, tile * 128 : tile * 128 + width] = total[:, :width]


SMEM = pl.BlockSpec(memory_space=pltpu.SMEM)
VMEM = pl.BlockSpec(memory_space=pltpu.VMEM)
HBM = pl.BlockSpec(memory_space=pltpu.HBM)
params = pltpu.CompilerParams(vmem_limit_bytes=32 * 1024 * 1024)


def in_vmem(*shape):
    return pltpu.VMEM(shape, jnp.float32)


def in_hbm(value):
    return pltpu.with_memory_space_constraint(value, pltpu.HBM)


def local(psi_in, v_in, offsets):
    band_count = lax.axis_size("band")
    dom_count = lax.axis_size("dom")
    dom_idx = lax.axis_index("dom")
    slab_idx = lax.axis_index("band") % 2
    is_lower = slab_idx == 0
    slab_scalar = slab_idx.astype(jnp.int32).reshape(1)
    side = v_in.shape[1]
    pk = Packing(side)
    half = side // 2
    cells = side * side
    bands = band_count // 2
    grid_z = CORE * dom_count // 4
    lanes = 4 * grid_z
    slab_rows = CORE // 2 * 8

    f32, bf16 = jnp.float32, jnp.bfloat16
    field_type = in_vmem(*pk.shape)
    padded_field = pltpu.VMEM(pk.padded_shape, f32)

    rows = psi_in.reshape(half, 1, cells)
    rows = in_hbm(rows)
    edge = pl.pallas_call(
        functools.partial(edge_kernel, pk),
        out_shape=in_vmem(DEG, 1, cells),
        in_specs=[SMEM, HBM],
        out_specs=VMEM,
        scratch_shapes=[pltpu.SemaphoreType.DMA],
        compiler_params=params,
    )(slab_scalar, rows)
    halo = swapped(edge, "band", 1)
    masks = [dom_count // 2, 0]
    bit = dom_count // 4
    while bit:
        masks = masks + [one | bit for one in masks]
        bit //= 2
    dom_scalar = dom_idx.astype(jnp.int32).reshape(1)
    start, coef, code = pl.pallas_call(
        functools.partial(start_kernel, pk, masks),
        out_shape=(field_type, field_type, in_vmem(8, 128)),
        in_specs=[SMEM, SMEM, HBM, HBM, HBM],
        out_specs=(VMEM, VMEM, VMEM),
        scratch_shapes=[
            pltpu.VMEM((pk.rows, cells), f32),
            pltpu.VMEM((side * pk.pitch, 128), f32),
            pltpu.VMEM((half, 1, cells), f32),
            pltpu.VMEM((side, cells), f32),
            pltpu.SMEM((dom_count, 3), jnp.int32),
            pltpu.SemaphoreType.DMA((3,)),
        ],
        compiler_params=params,
    )(slab_scalar, dom_scalar, rows, in_hbm(v_in[0]), in_hbm(offsets))

    padded_type = in_vmem(*pk.padded_shape)
    filt, dens = pl.pallas_call(
        functools.partial(first_kernel, pk, bands),
        out_shape=(padded_type, in_vmem(slab_rows, 128)),
        in_specs=[SMEM, VMEM, VMEM, VMEM],
        out_specs=(VMEM, VMEM),
        scratch_shapes=[padded_field, padded_field, pltpu.VMEM((side * DEG, 128), f32)],
        compiler_params=params,
    )(slab_scalar, start, halo, coef)
    edge = pl.pallas_call(
        functools.partial(send_kernel, pk),
        out_shape=in_vmem(pk.edge_groups * side, 128),
        in_specs=[SMEM, VMEM],
        out_specs=VMEM,
        compiler_params=params,
    )(slab_scalar, filt)

    mask = 2
    while mask < band_count:
        dens = dens + swapped(dens, "band", mask)
        mask *= 2

    far = dom_count // 2
    both = ("dom", "band")
    count = dom_count * band_count

    def crossed(value, mask):
        return lax.ppermute(value, both, [(source, source ^ mask) for source in range(count)])

    beside_all = crossed(jnp.concatenate([dens, edge], 0), 1)
    beside = beside_all[:slab_rows]
    across = crossed(dens, far * band_count)
    diagonal = crossed(dens, far * band_count + 1)

    def cube_of(own, other):
        return jnp.concatenate([jnp.where(is_lower, own, other), jnp.where(is_lower, other, own)], 0)

    cubes = [cube_of(across, diagonal), cube_of(dens, beside)]
    bit = far // 2
    while bit > 1:
        cubes = cubes + [swapped(cube, "dom", bit) for cube in cubes]
        bit //= 2
    early = swapped(jnp.concatenate([cubes[0], dens], 0), "dom", 1)
    late = swapped(beside, "dom", 1)
    cubes_across = [early, late] + [swapped(cube, "dom", 1) for cube in cubes[2:]]

    field, mean = pl.pallas_call(
        functools.partial(take_kernel, pk),
        out_shape=(padded_type, in_vmem(8, 128)),
        in_specs=[SMEM, VMEM, VMEM, VMEM],
        out_specs=(VMEM, VMEM),
        compiler_params=params,
    )(slab_scalar, filt, beside_all, cubes[1])
    table, factor = solver_tables(side, grid_z)
    pitch = CORE + 8
    result = pl.pallas_call(
        functools.partial(second_kernel, pk, dom_count),
        out_shape=jax.ShapeDtypeStruct((half, 1, cells), f32),
        in_specs=[SMEM] + [VMEM] * (6 + dom_count),
        out_specs=VMEM,
        scratch_shapes=[
            pltpu.VMEM((dom_count, CORE * 8, 128), f32),
            padded_field,
            padded_field,
            pltpu.VMEM(pk.shape, f32),
            pltpu.VMEM((4 * CORE * 8, dom_count // 4 * 3 * 128), bf16),
            pltpu.VMEM((lanes // 128, CORE * pitch, 128), f32),
            pltpu.VMEM((lanes // 128, CORE * pitch, 128), f32),
            pltpu.VMEM((lanes // 128, CORE * pitch, 128), f32),
            pltpu.VMEM((pk.blocks, pk.depth * side, lanes), f32),
            pltpu.VMEM((dom_count // 4, pk.depth * side, 128), f32),
            pltpu.VMEM((half * side, 128), f32),
        ],
        compiler_params=params,
    )(
        slab_scalar, code, mean, field, coef, jnp.asarray(table), jnp.asarray(factor), *cubes, *cubes_across
    )
    return result.reshape(1, 1, half, cells)


def solution(mesh):
    in_specs = (P("dom", "band", None, None), P("dom", None, None), P())
    out_specs = P("dom", "band", None, None)
    return jax.shard_map(local, mesh=mesh, in_specs=in_specs, out_specs=out_specs, check_vma=False)
```

```python
import functools
import math

import jax
import jax.numpy as jnp
import ml_dtypes
import numpy as np
from jax import lax
from jax.experimental import pallas as pl
from jax.experimental.pallas import tpu as pltpu
from jax.sharding import PartitionSpec as P

CORE = 32
BUF = 4
DEG = 8

HALF_WIDTH = 4.5
FOUR_PI = 4.0 * math.pi
EXCHANGE_COEF = -((3.0 / math.pi) ** (1.0 / 3.0))


def swapped(value, axis, mask):
    pairs = [(source, source ^ mask) for source in range(lax.axis_size(axis))]
    return lax.ppermute(value, axis, pairs)


def wave_basis(length):
    cells = np.arange(length)
    rows, waves = [], []
    for wave in range(length // 2 + 1):
        angle = 2.0 * np.pi * ((wave * cells) % length) / length
        if wave in (0, length // 2):
            rows.append(np.cos(angle) / np.sqrt(length))
            waves.append(wave)
        else:
            rows.append(np.cos(angle) * np.sqrt(2.0 / length))
            rows.append(np.sin(angle) * np.sqrt(2.0 / length))
            waves += [wave, wave]
    return np.array(rows), np.array(waves)


def parity_basis():
    rows, waves = wave_basis(2 * CORE)
    return np.stack([rows[waves % 2 == 0], rows[waves % 2 == 1]]), np.stack(
        [waves[waves % 2 == 0], waves[waves % 2 == 1]]
    )


def eigenvalue(waves, length):
    return 2.0 - 2.0 * np.cos(2.0 * np.pi * waves / length)


def padded(length, unit):
    return -(-length // unit) * unit


class Packing:
    def __init__(self, side):
        self.side = side
        self.half = side // 2
        self.rows = self.half + DEG
        self.blocks = 128 // (side + 1)
        self.span = 128 // self.blocks
        self.depth = -(-self.rows // self.blocks)
        self.shape = (self.depth, side, 128)
        self.padded_shape = (self.depth, side + 16, 128)
        self.edge_groups = -(-DEG // self.blocks)
        self.pitch = padded(self.rows, 16) + 8

    def where(self, row):
        return row // self.depth, row % self.depth


def lanes_of(shape):
    return lax.broadcasted_iota(jnp.int32, shape, len(shape) - 1)


def roll(values, shift):
    return values if isinstance(shift, int) and shift % 128 == 0 else pltpu.roll(values, shift % 128, 1)


def pack(pk, flat, pitched_ref, field_ref):
    count = flat.shape[0]
    for y in range(pk.side):
        pitched_ref[y * pk.pitch : y * pk.pitch + count, 0 : pk.side] = flat[:, y * pk.side : (y + 1) * pk.side]
    for level in range(pk.depth):
        total = None
        for block in range(pk.blocks):
            row = block * pk.depth + level
            if row < pk.rows:
                part = roll(pitched_ref[pl.ds(row, pk.side, stride=pk.pitch), :], block * pk.span)
                total = part if total is None else total + part
        field_ref[level] = total


def edge_kernel(pk, slab_ref, psi_ref, edge_ref, sem):
    first = jnp.where(slab_ref[0] == 0, pk.half - DEG, 0)
    copy = pltpu.make_async_copy(psi_ref.at[pl.ds(first, DEG)], edge_ref, sem)
    copy.start()
    copy.wait()


def start_kernel(
    pk, masks, slab_ref, dom_ref, psi_in_ref, pot_in_ref, offsets_in_ref,
    field_ref, coef_ref, code_ref, flat_ref, pitched_ref, psi_ref, pot_ref, offsets_ref, sems,
):
    psi_copy = pltpu.make_async_copy(psi_in_ref, psi_ref, sems.at[2])
    copy = pltpu.make_async_copy(pot_in_ref, pot_ref, sems.at[0])
    psi_copy.start()
    offsets_copy = pltpu.make_async_copy(offsets_in_ref, offsets_ref, sems.at[1])
    copy.start()
    offsets_copy.start()
    half, side = pk.half, pk.side
    cells = side * side
    is_lower = slab_ref[0] == 0
    flat_ref[...] = jnp.zeros(flat_ref.shape, jnp.float32)
    pitched_ref[...] = jnp.zeros(pitched_ref.shape, jnp.float32)
    psi_copy.wait()
    own = psi_ref[:, 0, :]

    @pl.when(is_lower)
    def _():
        flat_ref[0:half] = own

    @pl.when(jnp.logical_not(is_lower))
    def _():
        flat_ref[DEG : DEG + half] = own

    pack(pk, flat_ref[...], pitched_ref, field_ref)
    copy.wait()

    @pl.when(is_lower)
    def _():
        flat_ref[0 : pk.rows] = pot_ref[0 : pk.rows] * (2.0 / HALF_WIDTH)

    @pl.when(jnp.logical_not(is_lower))
    def _():
        flat_ref[0 : pk.rows] = pot_ref[side - pk.rows : side] * (2.0 / HALF_WIDTH)

    pack(pk, flat_ref[...], pitched_ref, coef_ref)

    offsets_copy.wait()
    dom, dom_count = dom_ref[0], len(masks)
    blocks_z = dom_count // 4
    code = jnp.int32(0)
    for idx, mask in enumerate(masks):
        other = dom ^ mask
        at_x = (offsets_ref[other, 0] != offsets_ref[dom, 0]).astype(jnp.int32)
        at_y = (offsets_ref[other, 1] != offsets_ref[dom, 1]).astype(jnp.int32)
        at_z = (offsets_ref[other, 2] - offsets_ref[dom, 2]) // CORE
        at_z = jnp.where(at_z < 0, at_z + blocks_z, at_z)
        place = (at_z * 2 + at_y) * 2 + at_x
        for where in range(dom_count):
            code = code + jnp.where(place == where, idx * dom_count**where, 0)
    code_ref[...] = jnp.full(code_ref.shape, code.astype(jnp.float32))


def filtered_field(pk, start_ref, one_ref, two_ref, coef_ref):
    lane = lanes_of((8, 128))
    is_cell = (lane % pk.span < pk.side) & (lane < pk.blocks * pk.span)
    full_weight = jnp.where(is_cell, 1.0 / HALF_WIDTH, 0.0)
    part_weight = jnp.where(is_cell & (lane < (pk.blocks - 1) * pk.span), 1.0 / HALF_WIDTH, 0.0)
    after_first = lane >= pk.span
    before_last = lane < (pk.blocks - 1) * pk.span
    previous_ref, current_ref = None, start_ref
    for order in range(DEG):
        target_ref = (one_ref, two_ref)[order % 2]
        for tile in range(pk.side // 8):
            at = 8 + 8 * tile
            values = [current_ref[level, at : at + 8, :] for level in range(pk.depth)]
            before = jnp.where(after_first, roll(values[-1], pk.span), 0.0)
            after = jnp.where(before_last, roll(values[0], -pk.span), 0.0)
            around = [before] + values + [after]
            for level in range(pk.depth):
                value = values[level]
                total = around[level] + around[level + 2]
                total = total + (
                    current_ref[level, at - 1 : at + 7, :] + current_ref[level, at + 1 : at + 9, :]
                )
                total = total + (roll(value, 1) + roll(value, -1))
                weight = full_weight if (pk.blocks - 1) * pk.depth + level < pk.rows else part_weight
                following = coef_ref[level, at - 8 : at, :] * value - weight * total
                if order == 0:
                    following = 0.5 * following
                else:
                    following = following - previous_ref[level, at : at + 8, :]
                target_ref[level, at : at + 8, :] = following
        previous_ref, current_ref = current_ref, target_ref


def clear_margins(pk, ref):
    zeros = jnp.zeros((pk.depth, 8, 128), jnp.float32)
    ref[:, 0:8, :] = zeros
    ref[:, 8 + pk.side : 16 + pk.side, :] = zeros


def first_kernel(
    pk, bands, slab_ref, start_ref, halo_ref, coef_ref, filt_ref, dens_ref, field_ref, one_ref, lines_ref
):
    side, span = pk.side, pk.span
    slab = slab_ref[0]
    is_lower = slab == 0
    clear_margins(pk, field_ref)
    clear_margins(pk, one_ref)
    clear_margins(pk, filt_ref)
    field_ref[:, 8 : 8 + side, :] = start_ref[...]
    low_block, low_level = pk.where(pk.half)
    high_block, high_level = pk.where(0)
    shift = jnp.where(is_lower, low_block * span, high_block * span)
    past = lanes_of((DEG, 128)) - shift
    is_line = (past >= 0) & (past < side)
    cells = side * side
    tiles = []
    for tile in range(-(-cells // 128)):
        width = min(128, cells - tile * 128)
        part = halo_ref[:, 0, tile * 128 : tile * 128 + width]
        tiles.append(part if width == 128 else jnp.concatenate([part, jnp.zeros((DEG, 128 - width), jnp.float32)], 1))
    for y in range(side):
        tile, start = y * side // 128, y * side % 128
        line = pltpu.roll(tiles[tile], shift + (128 - start), 1)
        if start + side > 128:
            line = jnp.where(past < 128 - start, line, pltpu.roll(tiles[tile + 1], shift + (128 - start), 1))
        lines_ref[y * DEG : (y + 1) * DEG, :] = jnp.where(is_line, line, 0.0)
    for row in range(DEG):
        level = jnp.where(is_lower, low_level, high_level) + row
        line = lines_ref[pl.ds(row, side, stride=DEG), :]
        field_ref[level, 8 : 8 + side, :] = field_ref[level, 8 : 8 + side, :] + line

    filtered_field(pk, field_ref, one_ref, filt_ref, coef_ref)
    result_ref = filt_ref

    lane = lanes_of((8, 128))
    lines = 128 // CORE
    for lower, offset in ((True, BUF), (False, DEG)):

        @pl.when(is_lower == lower)
        def _(offset=offset):
            for cell in range(CORE // 2):
                block, level = pk.where(cell + offset)
                total = None
                for line in range(lines):
                    value = result_ref[level, 8 + BUF + 8 * line : 16 + BUF + 8 * line, :]
                    value = roll(value, line * CORE - BUF - block * span)
                    total = value if total is None else jnp.where(lane >= line * CORE, value, total)
                dens_ref[cell * 8 : (cell + 1) * 8] = total * total * (1.0 / bands)


def send_kernel(pk, slab_ref, result_ref, edge_ref):
    side, span = pk.side, pk.span
    is_lower = slab_ref[0] == 0
    lane = lanes_of((side, 128))
    for group in range(pk.edge_groups):
        total = jnp.zeros((side, 128), jnp.float32)
        for slot in range(min(pk.blocks, DEG - group * pk.blocks)):
            row = group * pk.blocks + slot + jnp.where(is_lower, pk.half - DEG, DEG)
            shift = slot * span - row // pk.depth * span + 128 * pk.blocks
            line = pltpu.roll(result_ref[row % pk.depth, 8 : 8 + side, :], shift % 128, 1)
            total = jnp.where((lane >= slot * span) & (lane < slot * span + side), line, total)
        edge_ref[group * side : (group + 1) * side] = total


def take_kernel(pk, slab_ref, filt_ref, beside_ref, near_ref, field_ref, mean_ref):
    mean_ref[...] = jnp.full(mean_ref.shape, jnp.mean(near_ref[...]))
    side, span, half = pk.side, pk.span, pk.half
    is_lower = slab_ref[0] == 0
    field_ref[...] = filt_ref[...]
    lane = lanes_of((side, 128))
    base = CORE // 2 * 8
    for row in range(DEG):
        group_at, slot = row // pk.blocks, row % pk.blocks
        line = beside_ref[base + group_at * side : base + (group_at + 1) * side, :]
        for wanted, (block, level) in ((True, pk.where(half + row)), (False, pk.where(row))):
            here = (lane >= block * span) & (lane < block * span + side) & (is_lower == wanted)
            old = field_ref[level, 8 : 8 + side, :]
            field_ref[level, 8 : 8 + side, :] = jnp.where(here, roll(line, (block - slot) * span), old)


def split2(values):
    high = values.astype(jnp.bfloat16)
    return high, (values - high.astype(jnp.float32)).astype(jnp.bfloat16)


def split3(values):
    high = values.astype(jnp.bfloat16)
    rest = values - high.astype(jnp.float32)
    middle = rest.astype(jnp.bfloat16)
    return high, middle, (rest - middle.astype(jnp.float32)).astype(jnp.bfloat16)


def dot(left, right):
    return jnp.dot(left, right, preferred_element_type=jnp.float32)


def table_parts(table):
    high = table.astype(ml_dtypes.bfloat16)
    return high, (table - high.astype(np.float64)).astype(ml_dtypes.bfloat16)


def left_table(table):
    high, low = table_parts(table)
    return np.concatenate([high, low, high], -1)


def stacked(values):
    high, low = split2(values)
    return jnp.concatenate([high, high, low], 0)


@functools.lru_cache(maxsize=None)
def solver_tables(side, grid_z):
    pk = Packing(side)
    blocks_z = grid_z // CORE
    lanes = 4 * grid_z
    basis, waves = parity_basis()
    z_basis, z_waves = wave_basis(grid_z)
    lines = 128 // CORE
    into = []
    for place_z in range(blocks_z):
        along_z = z_basis[:, place_z * CORE : (place_z + 1) * CORE].T
        high, low = table_parts(np.kron(np.eye(lines), along_z))
        into += [high, high, low]
    into = np.concatenate(into, 0)
    region = np.arange(side) - BUF
    outer = basis[:, :, region % (2 * CORE)]
    small = [left_table(np.concatenate([basis[0, :, :CORE], basis[1, :, :CORE]], 0))]
    small.append(left_table(np.concatenate([outer[0].T, outer[1].T], 0)))
    for first_row in (0, side - pk.rows):
        rows = outer[:, :, first_row : first_row + pk.rows]
        rows = np.pad(rows, ((0, 0), (0, 0), (0, padded(pk.rows, 8) - pk.rows)))
        small.append(left_table(np.concatenate([rows[0].T, rows[1].T], 0)))
    small = np.concatenate(small, 0)
    back_z = []
    spread = np.zeros((blocks_z, 3, 128, 128))
    for block in range(pk.blocks):
        start = block * pk.span
        table = np.zeros((4, grid_z, 128))
        table[:, :, start : start + side] = z_basis[:, region % grid_z]
        high, low = table_parts(table.reshape(lanes, 128))
        back_z.append(np.block([[high, low], [high, np.zeros_like(low)]]))
        for cell, pos in enumerate(region % grid_z):
            spread[pos // CORE, :, block * CORE + pos % CORE, start + cell] = 1.0
    back_z = np.concatenate(back_z, 0)
    spread = spread.reshape(blocks_z * 3 * 128, 128).astype(ml_dtypes.bfloat16)
    eigen = eigenvalue(waves, 2 * CORE)
    lam = (
        eigen.T[:, None, None, :, None]
        + eigen.T[None, :, :, None, None]
        + eigenvalue(z_waves, grid_z)[None, None, None, None, :]
    )
    lam[0, 0, 0, 0, 0] = np.inf
    factor = (FOUR_PI / lam).reshape(CORE * CORE, lanes).astype(np.float32)
    pieces = [back_z, np.concatenate([into, np.pad(spread, ((0, 0), (0, lanes - 128)))], 0), small]
    height = max(len(piece) for piece in pieces)
    pieces = [np.pad(piece, ((0, height - len(piece)), (0, -piece.shape[1] % 128))) for piece in pieces]
    return np.concatenate(pieces, 1), factor


def cube_root(values):
    positive = values > 0.0
    safe = jnp.where(positive, values, 1.0)
    root = jnp.exp(jnp.log(safe) * (1.0 / 3.0))
    root = root - (root - safe / (root * root)) * (1.0 / 3.0)
    return jnp.where(positive, root, 0.0)


def second_kernel(
    pk, dom_count, slab_ref, code_ref, mean_ref, field_ref, start_coef_ref, table_ref, factor_ref, *refs
):
    gathered_refs, refs = refs[:dom_count], refs[dom_count:]
    (
        out_ref, cubes_ref, one_ref, two_ref, coef_ref, rows_ref, waves_ref, mixed_ref, flat_ref,
        near_dens_ref, own_ref,
    ) = refs
    side, half, span = pk.side, pk.half, pk.span
    is_lower = slab_ref[0] == 0
    blocks_z = dom_count // 4
    grid_z = CORE * blocks_z
    lanes = 4 * grid_z
    columns = lanes // 128
    lines = 128 // CORE
    pitch = CORE + 8
    kept = padded(pk.rows, 8)

    near_count = dom_count // 2
    early_ref, late_ref = gathered_refs[near_count : near_count + 2]
    whole, part = CORE * 8, CORE * 4
    for idx, ref in enumerate(gathered_refs):
        if idx not in (near_count, near_count + 1):
            cubes_ref[idx] = ref[...]
    cubes_ref[near_count] = early_ref[0:whole]
    own_part, other_part = early_ref[whole : whole + part], late_ref[...]
    cubes_ref[near_count + 1, 0:part] = jnp.where(is_lower, own_part, other_part)
    cubes_ref[near_count + 1, part:whole] = jnp.where(is_lower, other_part, own_part)
    mean = 4.0 * jnp.concatenate([mean_ref[...]] * CORE, 0)
    code = jnp.max(code_ref[...]).astype(jnp.int32)
    cube_at = [code // dom_count**where % dom_count for where in range(dom_count)]

    stacks = [[] for _ in range(4)]
    for at_z in range(blocks_z):
        near, at_x, at_y, at_xy = [cubes_ref[cube_at[at_z * 4 + place]] for place in range(4)]
        sums, others = near + at_x, at_y + at_xy
        diffs, other_diffs = near - at_x, at_y - at_xy
        parities = (sums + others - mean, sums - others, diffs + other_diffs, diffs - other_diffs)
        for parity, value in enumerate(parities):
            high, low = split2(value)
            stacks[parity] += [high, low, high]
    z_table = table_ref[0 : blocks_z * 3 * 128, 256 : 256 + lanes]
    product = jnp.concatenate([dot(jnp.concatenate(stack, 1), z_table) for stack in stacks], 0)
    lane = lanes_of((8, 128))
    for x in range(CORE):
        for line in range(lines):
            for col in range(columns):
                total = None
                for parity in range(4):
                    into = parity * grid_z - col * 128
                    if 0 <= into < 128:
                        at = line * grid_z
                        part = product[(parity * CORE + x) * 8 : (parity * CORE + x + 1) * 8, at // 128 * 128 : at // 128 * 128 + 128]
                        part = roll(part, into - at % 128)
                        total = part if total is None else jnp.where(lane >= into, part, total)
                rows_ref[col, x * pitch + line * 8 : x * pitch + line * 8 + 8, :] = total

    lane = lanes_of((8, 128))
    for at_z in range(blocks_z):
        for level in range(pk.depth):
            inner, low_wrap, high_wrap = [], None, None
            for block in range(pk.blocks):
                row = block * pk.depth + level
                if row >= pk.rows:
                    continue
                x = row - BUF + jnp.where(is_lower, 0, side - pk.rows)
                inside = (x >= 0) & (x < CORE)
                cell = pl.multiple_of((x + CORE) % CORE * 8, 8)

                def source(at_y):
                    place = (at_z * 2 + at_y) * 2
                    cube = jnp.where(inside, cube_at[place], cube_at[place + 1])
                    return cubes_ref[cube, pl.ds(cell, 8), :]

                def put(value, line, total):
                    value = roll(value, (block - line) * CORE)
                    return jnp.where((lane >= block * CORE) & (lane < (block + 1) * CORE), value, total)

                own, beside = source(0), source(1)
                zeros = jnp.zeros((8, 128), jnp.float32)
                inner = inner or [zeros] * lines
                inner = [put(own, line, total) for line, total in enumerate(inner)]
                low_wrap = put(beside, lines - 1, zeros if low_wrap is None else low_wrap)
                high_wrap = put(beside, 0, zeros if high_wrap is None else high_wrap)
            base = level * side
            near_dens_ref[at_z, base : base + BUF, :] = low_wrap[8 - BUF :]
            for line in range(lines):
                near_dens_ref[at_z, base + BUF + 8 * line : base + BUF + 8 * line + 8, :] = inner[line]
            near_dens_ref[at_z, base + BUF + CORE : base + side, :] = high_wrap[:BUF]

    group = max(1, 256 // lanes)
    lane_id = lanes_of((1, group * lanes)) % lanes
    even_x = lane_id < 2 * grid_z
    even_y = (lane_id // grid_z) % 2 == 0

    def side_by_side(ref, starts, stride, count):
        pieces = []
        for start in starts:
            for col in range(columns):
                if stride == 1:
                    pieces.append(ref[col, pl.ds(start, count), :])
                else:
                    pieces.append(ref[col, pl.ds(start, count, stride=stride), :])
        return jnp.concatenate(pieces, 1)

    def scatter(ref, starts, values, count):
        for idx, start in enumerate(starts):
            for col in range(columns):
                at = (idx * columns + col) * 128
                ref[col, start : start + count, :] = values[:, at : at + 128]

    def small(first, count):
        return table_ref[first : first + count, 256 + lanes : 256 + lanes + 3 * CORE]

    forward = small(0, 2 * CORE)
    back_y = small(2 * CORE, 2 * side)
    first = 2 * CORE + 2 * side
    back_x = jnp.where(is_lower, small(first, 2 * kept), small(first + 2 * kept, 2 * kept))
    for first in range(0, CORE, group):
        starts = [x * pitch for x in range(first, first + group)]
        both = dot(forward, stacked(side_by_side(rows_ref, starts, 1, CORE)))
        scatter(waves_ref, starts, jnp.where(even_y, both[:CORE], both[CORE:]), CORE)

    for first in range(0, CORE, group):
        waves_y = list(range(first, first + group))
        both = dot(forward, stacked(side_by_side(waves_ref, waves_y, pitch, CORE)))
        modes = jnp.where(even_x, both[:CORE], both[CORE:])
        scale = jnp.concatenate([factor_ref[wave * CORE : (wave + 1) * CORE] for wave in waves_y], 1)
        both = dot(back_x, stacked(modes * scale))
        scatter(mixed_ref, [wave * pitch for wave in waves_y], jnp.where(even_x, both[:kept], both[kept:]), kept)

    for level in range(pk.depth):
        rows = [block * pk.depth + level for block in range(pk.blocks)]
        rows = [row for row in rows if row < pk.rows]
        for first in range(0, len(rows), group):
            taken = rows[first : first + group]
            both = dot(back_y, stacked(side_by_side(mixed_ref, taken, pitch, CORE)))
            width = both.shape[1]
            field = jnp.where(even_y[:, :width], both[:side], both[side:])
            for idx in range(len(taken)):
                flat_ref[first + idx, level * side : (level + 1) * side, :] = field[:, idx * lanes : (idx + 1) * lanes]
        for block in range(len(rows), pk.blocks):
            flat_ref[block, level * side : (level + 1) * side, :] = jnp.zeros((side, lanes), jnp.float32)

    pieces = []
    for block in range(pk.blocks):
        pieces += split2(flat_ref[block])
    product = dot(jnp.concatenate(pieces, 1), table_ref[0 : pk.blocks * 2 * lanes, 0:256])
    hartree = product[:, 0:128] + product[:, 128:256]
    pieces = []
    for at_z in range(blocks_z):
        pieces += split3(near_dens_ref[at_z])
    density = dot(jnp.concatenate(pieces, 1), table_ref[blocks_z * 3 * 128 : blocks_z * 6 * 128, 256:384])
    added = (hartree + EXCHANGE_COEF * cube_root(density)) * (2.0 / HALF_WIDTH)
    for level in range(pk.depth):
        coef_ref[level] = start_coef_ref[level] + added[level * side : (level + 1) * side]

    clear_margins(pk, one_ref)
    clear_margins(pk, two_ref)
    filtered_field(pk, field_ref, one_ref, two_ref, coef_ref)

    for lower, offset in ((True, 0), (False, DEG)):

        @pl.when(is_lower == lower)
        def _(offset=offset):
            for row in range(half):
                block, level = pk.where(row + offset)
                own_ref[row * side : (row + 1) * side, :] = roll(two_ref[level, 8 : 8 + side, :], -block * span)

    cells = side * side
    parts = [roll(own_ref[pl.ds(y, half, stride=side), :], y * side) for y in range(side)]
    for tile in range(-(-cells // 128)):
        first, last = tile * 128 // side, min(side - 1, (tile * 128 + 127) // side)
        lane = lanes_of((half, 128)) + tile * 128
        total = None
        for y in range(first, last + 1):
            total = parts[y] if total is None else jnp.where(lane >= y * side, parts[y], total)
        width = min(128, cells - tile * 128)
        out_ref[:, 0, tile * 128 : tile * 128 + width] = total[:, :width]


SMEM = pl.BlockSpec(memory_space=pltpu.SMEM)
VMEM = pl.BlockSpec(memory_space=pltpu.VMEM)
HBM = pl.BlockSpec(memory_space=pltpu.HBM)
params = pltpu.CompilerParams(vmem_limit_bytes=32 * 1024 * 1024)


def in_vmem(*shape):
    return pltpu.VMEM(shape, jnp.float32)


def in_hbm(value):
    return pltpu.with_memory_space_constraint(value, pltpu.HBM)


def local(psi_in, v_in, offsets):
    band_count = lax.axis_size("band")
    dom_count = lax.axis_size("dom")
    dom_idx = lax.axis_index("dom")
    slab_idx = lax.axis_index("band") % 2
    is_lower = slab_idx == 0
    slab_scalar = slab_idx.astype(jnp.int32).reshape(1)
    side = v_in.shape[1]
    pk = Packing(side)
    half = side // 2
    cells = side * side
    bands = band_count // 2
    grid_z = CORE * dom_count // 4
    lanes = 4 * grid_z
    slab_rows = CORE // 2 * 8

    f32, bf16 = jnp.float32, jnp.bfloat16
    field_type = in_vmem(*pk.shape)
    padded_field = pltpu.VMEM(pk.padded_shape, f32)

    rows = psi_in.reshape(half, 1, cells)
    rows = in_hbm(rows)
    edge = pl.pallas_call(
        functools.partial(edge_kernel, pk),
        out_shape=in_vmem(DEG, 1, cells),
        in_specs=[SMEM, HBM],
        out_specs=VMEM,
        scratch_shapes=[pltpu.SemaphoreType.DMA],
        compiler_params=params,
    )(slab_scalar, rows)
    halo = swapped(edge, "band", 1)
    masks = [dom_count // 2, 0]
    bit = dom_count // 4
    while bit:
        masks = masks + [one | bit for one in masks]
        bit //= 2
    dom_scalar = dom_idx.astype(jnp.int32).reshape(1)
    start, coef, code = pl.pallas_call(
        functools.partial(start_kernel, pk, masks),
        out_shape=(field_type, field_type, in_vmem(8, 128)),
        in_specs=[SMEM, SMEM, HBM, HBM, HBM],
        out_specs=(VMEM, VMEM, VMEM),
        scratch_shapes=[
            pltpu.VMEM((pk.rows, cells), f32),
            pltpu.VMEM((side * pk.pitch, 128), f32),
            pltpu.VMEM((half, 1, cells), f32),
            pltpu.VMEM((side, cells), f32),
            pltpu.SMEM((dom_count, 3), jnp.int32),
            pltpu.SemaphoreType.DMA((3,)),
        ],
        compiler_params=params,
    )(slab_scalar, dom_scalar, rows, in_hbm(v_in[0]), in_hbm(offsets))

    padded_type = in_vmem(*pk.padded_shape)
    filt, dens = pl.pallas_call(
        functools.partial(first_kernel, pk, bands),
        out_shape=(padded_type, in_vmem(slab_rows, 128)),
        in_specs=[SMEM, VMEM, VMEM, VMEM],
        out_specs=(VMEM, VMEM),
        scratch_shapes=[padded_field, padded_field, pltpu.VMEM((side * DEG, 128), f32)],
        compiler_params=params,
    )(slab_scalar, start, halo, coef)
    edge = pl.pallas_call(
        functools.partial(send_kernel, pk),
        out_shape=in_vmem(pk.edge_groups * side, 128),
        in_specs=[SMEM, VMEM],
        out_specs=VMEM,
        compiler_params=params,
    )(slab_scalar, filt)

    mask = 2
    while mask < band_count:
        dens = dens + swapped(dens, "band", mask)
        mask *= 2

    far = dom_count // 2
    both = ("dom", "band")
    count = dom_count * band_count

    def crossed(value, mask):
        return lax.ppermute(value, both, [(source, source ^ mask) for source in range(count)])

    beside_all = crossed(jnp.concatenate([dens, edge], 0), 1)
    beside = beside_all[:slab_rows]
    across = crossed(dens, far * band_count)
    diagonal = crossed(dens, far * band_count + 1)

    def cube_of(own, other):
        return jnp.concatenate([jnp.where(is_lower, own, other), jnp.where(is_lower, other, own)], 0)

    cubes = [cube_of(across, diagonal), cube_of(dens, beside)]
    bit = far // 2
    while bit > 1:
        cubes = cubes + [swapped(cube, "dom", bit) for cube in cubes]
        bit //= 2
    early = swapped(jnp.concatenate([cubes[0], dens], 0), "dom", 1)
    late = swapped(beside, "dom", 1)
    cubes_across = [early, late] + [swapped(cube, "dom", 1) for cube in cubes[2:]]

    field, mean = pl.pallas_call(
        functools.partial(take_kernel, pk),
        out_shape=(padded_type, in_vmem(8, 128)),
        in_specs=[SMEM, VMEM, VMEM, VMEM],
        out_specs=(VMEM, VMEM),
        compiler_params=params,
    )(slab_scalar, filt, beside_all, cubes[1])
    table, factor = solver_tables(side, grid_z)
    pitch = CORE + 8
    result = pl.pallas_call(
        functools.partial(second_kernel, pk, dom_count),
        out_shape=jax.ShapeDtypeStruct((half, 1, cells), f32),
        in_specs=[SMEM] + [VMEM] * (6 + dom_count),
        out_specs=VMEM,
        scratch_shapes=[
            pltpu.VMEM((dom_count, CORE * 8, 128), f32),
            padded_field,
            padded_field,
            pltpu.VMEM(pk.shape, f32),
            pltpu.VMEM((lanes // 128, CORE * pitch, 128), f32),
            pltpu.VMEM((lanes // 128, CORE * pitch, 128), f32),
            pltpu.VMEM((lanes // 128, CORE * pitch, 128), f32),
            pltpu.VMEM((pk.blocks, pk.depth * side, lanes), f32),
            pltpu.VMEM((dom_count // 4, pk.depth * side, 128), f32),
            pltpu.VMEM((padded(half, 8) * side, 128), f32),
        ],
        compiler_params=params,
    )(
        slab_scalar, code, mean, field, coef, jnp.asarray(table), jnp.asarray(factor), *cubes, *cubes_across
    )
    return result.reshape(1, 1, half, cells)


def solution(mesh):
    in_specs = (P("dom", "band", None, None), P("dom", None, None), P())
    out_specs = P("dom", "band", None, None)
    return jax.shard_map(local, mesh=mesh, in_specs=in_specs, out_specs=out_specs, check_vma=False)
```

```python
import functools
import math

import jax
import jax.numpy as jnp
import ml_dtypes
import numpy as np
from jax import lax
from jax.experimental import pallas as pl
from jax.experimental.pallas import tpu as pltpu
from jax.sharding import PartitionSpec as P

CORE = 32
BUF = 4
DEG = 8

HALF_WIDTH = 4.5
FOUR_PI = 4.0 * math.pi
EXCHANGE_COEF = -((3.0 / math.pi) ** (1.0 / 3.0))


def swapped(value, axis, mask):
    pairs = [(source, source ^ mask) for source in range(lax.axis_size(axis))]
    return lax.ppermute(value, axis, pairs)


def wave_basis(length):
    cells = np.arange(length)
    rows, waves = [], []
    for wave in range(length // 2 + 1):
        angle = 2.0 * np.pi * ((wave * cells) % length) / length
        if wave in (0, length // 2):
            rows.append(np.cos(angle) / np.sqrt(length))
            waves.append(wave)
        else:
            rows.append(np.cos(angle) * np.sqrt(2.0 / length))
            rows.append(np.sin(angle) * np.sqrt(2.0 / length))
            waves += [wave, wave]
    return np.array(rows), np.array(waves)


def parity_basis():
    rows, waves = wave_basis(2 * CORE)
    return np.stack([rows[waves % 2 == 0], rows[waves % 2 == 1]]), np.stack(
        [waves[waves % 2 == 0], waves[waves % 2 == 1]]
    )


def eigenvalue(waves, length):
    return 2.0 - 2.0 * np.cos(2.0 * np.pi * waves / length)


def padded(length, unit):
    return -(-length // unit) * unit


class Packing:
    def __init__(self, side):
        self.side = side
        self.half = side // 2
        self.rows = self.half + DEG
        self.blocks = 128 // (side + 1)
        self.span = 128 // self.blocks
        self.depth = -(-self.rows // self.blocks)
        self.shape = (self.depth, side, 128)
        self.padded_shape = (self.depth, side + 16, 128)
        self.edge_groups = -(-DEG // self.blocks)
        self.pitch = padded(self.rows, 16) + 8

    def where(self, row):
        return row // self.depth, row % self.depth


def lanes_of(shape):
    return lax.broadcasted_iota(jnp.int32, shape, len(shape) - 1)


def roll(values, shift):
    return values if isinstance(shift, int) and shift % 128 == 0 else pltpu.roll(values, shift % 128, 1)


def pack(pk, flat, pitched_ref, field_ref):
    count = flat.shape[0]
    for y in range(pk.side):
        pitched_ref[y * pk.pitch : y * pk.pitch + count, 0 : pk.side] = flat[:, y * pk.side : (y + 1) * pk.side]
    for level in range(pk.depth):
        total = None
        for block in range(pk.blocks):
            row = block * pk.depth + level
            if row < pk.rows:
                part = roll(pitched_ref[pl.ds(row, pk.side, stride=pk.pitch), :], block * pk.span)
                total = part if total is None else total + part
        field_ref[level] = total


def edge_kernel(pk, slab_ref, psi_ref, edge_ref, sem):
    first = jnp.where(slab_ref[0] == 0, pk.half - DEG, 0)
    copy = pltpu.make_async_copy(psi_ref.at[pl.ds(first, DEG)], edge_ref, sem)
    copy.start()
    copy.wait()


def start_kernel(
    pk, masks, slab_ref, dom_ref, psi_in_ref, pot_in_ref, offsets_in_ref,
    field_ref, coef_ref, code_ref, flat_ref, pitched_ref, psi_ref, pot_ref, offsets_ref, sems,
):
    psi_copy = pltpu.make_async_copy(psi_in_ref, psi_ref, sems.at[2])
    copy = pltpu.make_async_copy(pot_in_ref, pot_ref, sems.at[0])
    psi_copy.start()
    offsets_copy = pltpu.make_async_copy(offsets_in_ref, offsets_ref, sems.at[1])
    copy.start()
    offsets_copy.start()
    half, side = pk.half, pk.side
    cells = side * side
    is_lower = slab_ref[0] == 0
    flat_ref[...] = jnp.zeros(flat_ref.shape, jnp.float32)
    pitched_ref[...] = jnp.zeros(pitched_ref.shape, jnp.float32)
    psi_copy.wait()
    own = psi_ref[:, 0, :]

    @pl.when(is_lower)
    def _():
        flat_ref[0:half] = own

    @pl.when(jnp.logical_not(is_lower))
    def _():
        flat_ref[DEG : DEG + half] = own

    pack(pk, flat_ref[0 : pk.rows], pitched_ref, field_ref)
    copy.wait()

    @pl.when(is_lower)
    def _():
        flat_ref[0 : pk.rows] = pot_ref[0 : pk.rows] * (2.0 / HALF_WIDTH)

    @pl.when(jnp.logical_not(is_lower))
    def _():
        flat_ref[0 : pk.rows] = pot_ref[side - pk.rows : side] * (2.0 / HALF_WIDTH)

    pack(pk, flat_ref[0 : pk.rows], pitched_ref, coef_ref)

    offsets_copy.wait()
    dom, dom_count = dom_ref[0], len(masks)
    blocks_z = dom_count // 4
    code = jnp.int32(0)
    for idx, mask in enumerate(masks):
        other = dom ^ mask
        at_x = (offsets_ref[other, 0] != offsets_ref[dom, 0]).astype(jnp.int32)
        at_y = (offsets_ref[other, 1] != offsets_ref[dom, 1]).astype(jnp.int32)
        at_z = (offsets_ref[other, 2] - offsets_ref[dom, 2]) // CORE
        at_z = jnp.where(at_z < 0, at_z + blocks_z, at_z)
        place = (at_z * 2 + at_y) * 2 + at_x
        for where in range(dom_count):
            code = code + jnp.where(place == where, idx * dom_count**where, 0)
    code_ref[...] = jnp.full(code_ref.shape, code.astype(jnp.float32))


def filtered_field(pk, start_ref, one_ref, two_ref, coef_ref):
    lane = lanes_of((8, 128))
    is_cell = (lane % pk.span < pk.side) & (lane < pk.blocks * pk.span)
    full_weight = jnp.where(is_cell, 1.0 / HALF_WIDTH, 0.0)
    part_weight = jnp.where(is_cell & (lane < (pk.blocks - 1) * pk.span), 1.0 / HALF_WIDTH, 0.0)
    after_first = lane >= pk.span
    before_last = lane < (pk.blocks - 1) * pk.span
    previous_ref, current_ref = None, start_ref
    for order in range(DEG):
        target_ref = (one_ref, two_ref)[order % 2]
        for tile in range(pk.side // 8):
            at = 8 + 8 * tile
            values = [current_ref[level, at : at + 8, :] for level in range(pk.depth)]
            before = jnp.where(after_first, roll(values[-1], pk.span), 0.0)
            after = jnp.where(before_last, roll(values[0], -pk.span), 0.0)
            around = [before] + values + [after]
            for level in range(pk.depth):
                value = values[level]
                total = around[level] + around[level + 2]
                total = total + (
                    current_ref[level, at - 1 : at + 7, :] + current_ref[level, at + 1 : at + 9, :]
                )
                total = total + (roll(value, 1) + roll(value, -1))
                weight = full_weight if (pk.blocks - 1) * pk.depth + level < pk.rows else part_weight
                following = coef_ref[level, at - 8 : at, :] * value - weight * total
                if order == 0:
                    following = 0.5 * following
                else:
                    following = following - previous_ref[level, at : at + 8, :]
                target_ref[level, at : at + 8, :] = following
        previous_ref, current_ref = current_ref, target_ref


def clear_margins(pk, ref):
    zeros = jnp.zeros((pk.depth, 8, 128), jnp.float32)
    ref[:, 0:8, :] = zeros
    ref[:, 8 + pk.side : 16 + pk.side, :] = zeros


def first_kernel(
    pk, bands, slab_ref, start_ref, halo_ref, coef_ref, filt_ref, dens_ref, field_ref, one_ref, lines_ref
):
    side, span = pk.side, pk.span
    slab = slab_ref[0]
    is_lower = slab == 0
    clear_margins(pk, field_ref)
    clear_margins(pk, one_ref)
    clear_margins(pk, filt_ref)
    field_ref[:, 8 : 8 + side, :] = start_ref[...]
    low_block, low_level = pk.where(pk.half)
    high_block, high_level = pk.where(0)
    shift = jnp.where(is_lower, low_block * span, high_block * span)
    past = lanes_of((DEG, 128)) - shift
    is_line = (past >= 0) & (past < side)
    cells = side * side
    tiles = []
    for tile in range(-(-cells // 128)):
        width = min(128, cells - tile * 128)
        part = halo_ref[:, 0, tile * 128 : tile * 128 + width]
        tiles.append(part if width == 128 else jnp.concatenate([part, jnp.zeros((DEG, 128 - width), jnp.float32)], 1))
    for y in range(side):
        tile, start = y * side // 128, y * side % 128
        line = pltpu.roll(tiles[tile], shift + (128 - start), 1)
        if start + side > 128:
            line = jnp.where(past < 128 - start, line, pltpu.roll(tiles[tile + 1], shift + (128 - start), 1))
        lines_ref[y * DEG : (y + 1) * DEG, :] = jnp.where(is_line, line, 0.0)
    for row in range(DEG):
        level = jnp.where(is_lower, low_level, high_level) + row
        line = lines_ref[pl.ds(row, side, stride=DEG), :]
        field_ref[level, 8 : 8 + side, :] = field_ref[level, 8 : 8 + side, :] + line

    filtered_field(pk, field_ref, one_ref, filt_ref, coef_ref)
    result_ref = filt_ref

    lane = lanes_of((8, 128))
    lines = 128 // CORE
    for lower, offset in ((True, BUF), (False, DEG)):

        @pl.when(is_lower == lower)
        def _(offset=offset):
            for cell in range(CORE // 2):
                block, level = pk.where(cell + offset)
                total = None
                for line in range(lines):
                    value = result_ref[level, 8 + BUF + 8 * line : 16 + BUF + 8 * line, :]
                    value = roll(value, line * CORE - BUF - block * span)
                    total = value if total is None else jnp.where(lane >= line * CORE, value, total)
                dens_ref[cell * 8 : (cell + 1) * 8] = total * total * (1.0 / bands)


def send_kernel(pk, slab_ref, result_ref, edge_ref):
    side, span = pk.side, pk.span
    is_lower = slab_ref[0] == 0
    lane = lanes_of((side, 128))
    for group in range(pk.edge_groups):
        total = jnp.zeros((side, 128), jnp.float32)
        for slot in range(min(pk.blocks, DEG - group * pk.blocks)):
            row = group * pk.blocks + slot + jnp.where(is_lower, pk.half - DEG, DEG)
            shift = slot * span - row // pk.depth * span + 128 * pk.blocks
            line = pltpu.roll(result_ref[row % pk.depth, 8 : 8 + side, :], shift % 128, 1)
            total = jnp.where((lane >= slot * span) & (lane < slot * span + side), line, total)
        edge_ref[group * side : (group + 1) * side] = total


def take_kernel(pk, slab_ref, filt_ref, beside_ref, near_ref, field_ref, mean_ref):
    mean_ref[...] = jnp.full(mean_ref.shape, jnp.mean(near_ref[...]))
    side, span, half = pk.side, pk.span, pk.half
    is_lower = slab_ref[0] == 0
    field_ref[...] = filt_ref[...]
    lane = lanes_of((side, 128))
    base = CORE // 2 * 8
    for row in range(DEG):
        group_at, slot = row // pk.blocks, row % pk.blocks
        line = beside_ref[base + group_at * side : base + (group_at + 1) * side, :]
        for wanted, (block, level) in ((True, pk.where(half + row)), (False, pk.where(row))):
            here = (lane >= block * span) & (lane < block * span + side) & (is_lower == wanted)
            old = field_ref[level, 8 : 8 + side, :]
            field_ref[level, 8 : 8 + side, :] = jnp.where(here, roll(line, (block - slot) * span), old)


def split2(values):
    high = values.astype(jnp.bfloat16)
    return high, (values - high.astype(jnp.float32)).astype(jnp.bfloat16)


def split3(values):
    high = values.astype(jnp.bfloat16)
    rest = values - high.astype(jnp.float32)
    middle = rest.astype(jnp.bfloat16)
    return high, middle, (rest - middle.astype(jnp.float32)).astype(jnp.bfloat16)


def dot(left, right):
    return jnp.dot(left, right, preferred_element_type=jnp.float32)


def table_parts(table):
    high = table.astype(ml_dtypes.bfloat16)
    return high, (table - high.astype(np.float64)).astype(ml_dtypes.bfloat16)


def left_table(table):
    high, low = table_parts(table)
    return np.concatenate([high, low, high], -1)


def stacked(values):
    high, low = split2(values)
    return jnp.concatenate([high, high, low], 0)


@functools.lru_cache(maxsize=None)
def solver_tables(side, grid_z):
    pk = Packing(side)
    blocks_z = grid_z // CORE
    lanes = 4 * grid_z
    basis, waves = parity_basis()
    z_basis, z_waves = wave_basis(grid_z)
    lines = 128 // CORE
    into = []
    for place_z in range(blocks_z):
        along_z = z_basis[:, place_z * CORE : (place_z + 1) * CORE].T
        high, low = table_parts(np.kron(np.eye(lines), along_z))
        into += [high, high, low]
    into = np.concatenate(into, 0)
    region = np.arange(side) - BUF
    outer = basis[:, :, region % (2 * CORE)]
    small = [left_table(np.concatenate([basis[0, :, :CORE], basis[1, :, :CORE]], 0))]
    small.append(left_table(np.concatenate([outer[0].T, outer[1].T], 0)))
    for first_row in (0, side - pk.rows):
        rows = outer[:, :, first_row : first_row + pk.rows]
        rows = np.pad(rows, ((0, 0), (0, 0), (0, padded(pk.rows, 8) - pk.rows)))
        small.append(left_table(np.concatenate([rows[0].T, rows[1].T], 0)))
    small = np.concatenate(small, 0)
    back_z = []
    spread = np.zeros((blocks_z, 3, 128, 128))
    for block in range(pk.blocks):
        start = block * pk.span
        table = np.zeros((4, grid_z, 128))
        table[:, :, start : start + side] = z_basis[:, region % grid_z]
        high, low = table_parts(table.reshape(lanes, 128))
        back_z.append(np.block([[high, low], [high, np.zeros_like(low)]]))
        for cell, pos in enumerate(region % grid_z):
            spread[pos // CORE, :, block * CORE + pos % CORE, start + cell] = 1.0
    back_z = np.concatenate(back_z, 0)
    spread = spread.reshape(blocks_z * 3 * 128, 128).astype(ml_dtypes.bfloat16)
    eigen = eigenvalue(waves, 2 * CORE)
    lam = (
        eigen.T[:, None, None, :, None]
        + eigen.T[None, :, :, None, None]
        + eigenvalue(z_waves, grid_z)[None, None, None, None, :]
    )
    lam[0, 0, 0, 0, 0] = np.inf
    factor = (FOUR_PI / lam).reshape(CORE * CORE, lanes).astype(np.float32)
    pieces = [back_z, np.concatenate([into, np.pad(spread, ((0, 0), (0, lanes - 128)))], 0), small]
    height = max(len(piece) for piece in pieces)
    pieces = [np.pad(piece, ((0, height - len(piece)), (0, -piece.shape[1] % 128))) for piece in pieces]
    return np.concatenate(pieces, 1), factor


def cube_root(values):
    positive = values > 0.0
    safe = jnp.where(positive, values, 1.0)
    root = jnp.exp(jnp.log(safe) * (1.0 / 3.0))
    root = root - (root - safe / (root * root)) * (1.0 / 3.0)
    return jnp.where(positive, root, 0.0)


def second_kernel(
    pk, dom_count, slab_ref, code_ref, mean_ref, field_ref, start_coef_ref, table_ref, factor_ref, *refs
):
    gathered_refs, refs = refs[:dom_count], refs[dom_count:]
    (
        out_ref, cubes_ref, one_ref, two_ref, coef_ref, rows_ref, waves_ref, mixed_ref, flat_ref,
        near_dens_ref, own_ref,
    ) = refs
    side, half, span = pk.side, pk.half, pk.span
    is_lower = slab_ref[0] == 0
    blocks_z = dom_count // 4
    grid_z = CORE * blocks_z
    lanes = 4 * grid_z
    columns = lanes // 128
    lines = 128 // CORE
    pitch = CORE + 8
    kept = padded(pk.rows, 8)

    near_count = dom_count // 2
    early_ref, late_ref = gathered_refs[near_count : near_count + 2]
    whole, part = CORE * 8, CORE * 4
    for idx, ref in enumerate(gathered_refs):
        if idx not in (near_count, near_count + 1):
            cubes_ref[idx] = ref[...]
    cubes_ref[near_count] = early_ref[0:whole]
    own_part, other_part = early_ref[whole : whole + part], late_ref[...]
    cubes_ref[near_count + 1, 0:part] = jnp.where(is_lower, own_part, other_part)
    cubes_ref[near_count + 1, part:whole] = jnp.where(is_lower, other_part, own_part)
    mean = 4.0 * jnp.concatenate([mean_ref[...]] * CORE, 0)
    code = jnp.max(code_ref[...]).astype(jnp.int32)
    cube_at = [code // dom_count**where % dom_count for where in range(dom_count)]

    stacks = [[] for _ in range(4)]
    for at_z in range(blocks_z):
        near, at_x, at_y, at_xy = [cubes_ref[cube_at[at_z * 4 + place]] for place in range(4)]
        sums, others = near + at_x, at_y + at_xy
        diffs, other_diffs = near - at_x, at_y - at_xy
        parities = (sums + others - mean, sums - others, diffs + other_diffs, diffs - other_diffs)
        for parity, value in enumerate(parities):
            high, low = split2(value)
            stacks[parity] += [high, low, high]
    z_table = table_ref[0 : blocks_z * 3 * 128, 256 : 256 + lanes]
    product = jnp.concatenate([dot(jnp.concatenate(stack, 1), z_table) for stack in stacks], 0)
    lane = lanes_of((8, 128))
    for x in range(CORE):
        for line in range(lines):
            for col in range(columns):
                total = None
                for parity in range(4):
                    into = parity * grid_z - col * 128
                    if 0 <= into < 128:
                        at = line * grid_z
                        part = product[(parity * CORE + x) * 8 : (parity * CORE + x + 1) * 8, at // 128 * 128 : at // 128 * 128 + 128]
                        part = roll(part, into - at % 128)
                        total = part if total is None else jnp.where(lane >= into, part, total)
                rows_ref[col, x * pitch + line * 8 : x * pitch + line * 8 + 8, :] = total

    lane = lanes_of((8, 128))
    for at_z in range(blocks_z):
        for level in range(pk.depth):
            inner, low_wrap, high_wrap = [], None, None
            for block in range(pk.blocks):
                row = block * pk.depth + level
                if row >= pk.rows:
                    continue
                x = row - BUF + jnp.where(is_lower, 0, side - pk.rows)
                inside = (x >= 0) & (x < CORE)
                cell = pl.multiple_of((x + CORE) % CORE * 8, 8)

                def source(at_y):
                    place = (at_z * 2 + at_y) * 2
                    cube = jnp.where(inside, cube_at[place], cube_at[place + 1])
                    return cubes_ref[cube, pl.ds(cell, 8), :]

                def put(value, line, total):
                    value = roll(value, (block - line) * CORE)
                    return jnp.where((lane >= block * CORE) & (lane < (block + 1) * CORE), value, total)

                own, beside = source(0), source(1)
                zeros = jnp.zeros((8, 128), jnp.float32)
                inner = inner or [zeros] * lines
                inner = [put(own, line, total) for line, total in enumerate(inner)]
                low_wrap = put(beside, lines - 1, zeros if low_wrap is None else low_wrap)
                high_wrap = put(beside, 0, zeros if high_wrap is None else high_wrap)
            base = level * side
            near_dens_ref[at_z, base : base + BUF, :] = low_wrap[8 - BUF :]
            for line in range(lines):
                near_dens_ref[at_z, base + BUF + 8 * line : base + BUF + 8 * line + 8, :] = inner[line]
            near_dens_ref[at_z, base + BUF + CORE : base + side, :] = high_wrap[:BUF]

    group = max(1, 256 // lanes)
    lane_id = lanes_of((1, group * lanes)) % lanes
    even_x = lane_id < 2 * grid_z
    even_y = (lane_id // grid_z) % 2 == 0

    def side_by_side(ref, starts, stride, count):
        pieces = []
        for start in starts:
            for col in range(columns):
                if stride == 1:
                    pieces.append(ref[col, pl.ds(start, count), :])
                else:
                    pieces.append(ref[col, pl.ds(start, count, stride=stride), :])
        return jnp.concatenate(pieces, 1)

    def scatter(ref, starts, values, count):
        for idx, start in enumerate(starts):
            for col in range(columns):
                at = (idx * columns + col) * 128
                ref[col, start : start + count, :] = values[:, at : at + 128]

    def small(first, count):
        return table_ref[first : first + count, 256 + lanes : 256 + lanes + 3 * CORE]

    forward = small(0, 2 * CORE)
    back_y = small(2 * CORE, 2 * side)
    first = 2 * CORE + 2 * side
    back_x = jnp.where(is_lower, small(first, 2 * kept), small(first + 2 * kept, 2 * kept))
    for first in range(0, CORE, group):
        starts = [x * pitch for x in range(first, first + group)]
        both = dot(forward, stacked(side_by_side(rows_ref, starts, 1, CORE)))
        scatter(waves_ref, starts, jnp.where(even_y, both[:CORE], both[CORE:]), CORE)

    for first in range(0, CORE, group):
        waves_y = list(range(first, first + group))
        both = dot(forward, stacked(side_by_side(waves_ref, waves_y, pitch, CORE)))
        modes = jnp.where(even_x, both[:CORE], both[CORE:])
        scale = jnp.concatenate([factor_ref[wave * CORE : (wave + 1) * CORE] for wave in waves_y], 1)
        both = dot(back_x, stacked(modes * scale))
        scatter(mixed_ref, [wave * pitch for wave in waves_y], jnp.where(even_x, both[:kept], both[kept:]), kept)

    for level in range(pk.depth):
        rows = [block * pk.depth + level for block in range(pk.blocks)]
        rows = [row for row in rows if row < pk.rows]
        for first in range(0, len(rows), group):
            taken = rows[first : first + group]
            both = dot(back_y, stacked(side_by_side(mixed_ref, taken, pitch, CORE)))
            width = both.shape[1]
            field = jnp.where(even_y[:, :width], both[:side], both[side:])
            for idx in range(len(taken)):
                flat_ref[first + idx, level * side : (level + 1) * side, :] = field[:, idx * lanes : (idx + 1) * lanes]
        for block in range(len(rows), pk.blocks):
            flat_ref[block, level * side : (level + 1) * side, :] = jnp.zeros((side, lanes), jnp.float32)

    pieces = []
    for block in range(pk.blocks):
        pieces += split2(flat_ref[block])
    product = dot(jnp.concatenate(pieces, 1), table_ref[0 : pk.blocks * 2 * lanes, 0:256])
    hartree = product[:, 0:128] + product[:, 128:256]
    pieces = []
    for at_z in range(blocks_z):
        pieces += split3(near_dens_ref[at_z, 0 : pk.depth * side])
    density = dot(jnp.concatenate(pieces, 1), table_ref[blocks_z * 3 * 128 : blocks_z * 6 * 128, 256:384])
    added = (hartree + EXCHANGE_COEF * cube_root(density)) * (2.0 / HALF_WIDTH)
    for level in range(pk.depth):
        coef_ref[level] = start_coef_ref[level] + added[level * side : (level + 1) * side]

    clear_margins(pk, one_ref)
    clear_margins(pk, two_ref)
    filtered_field(pk, field_ref, one_ref, two_ref, coef_ref)

    for lower, offset in ((True, 0), (False, DEG)):

        @pl.when(is_lower == lower)
        def _(offset=offset):
            for row in range(half):
                block, level = pk.where(row + offset)
                own_ref[row * side : (row + 1) * side, :] = roll(two_ref[level, 8 : 8 + side, :], -block * span)

    cells = side * side
    parts = [roll(own_ref[pl.ds(y, half, stride=side), :], y * side) for y in range(side)]
    for tile in range(-(-cells // 128)):
        first, last = tile * 128 // side, min(side - 1, (tile * 128 + 127) // side)
        lane = lanes_of((half, 128)) + tile * 128
        total = None
        for y in range(first, last + 1):
            total = parts[y] if total is None else jnp.where(lane >= y * side, parts[y], total)
        width = min(128, cells - tile * 128)
        out_ref[:, 0, tile * 128 : tile * 128 + width] = total[:, :width]


SMEM = pl.BlockSpec(memory_space=pltpu.SMEM)
VMEM = pl.BlockSpec(memory_space=pltpu.VMEM)
HBM = pl.BlockSpec(memory_space=pltpu.HBM)
params = pltpu.CompilerParams(vmem_limit_bytes=32 * 1024 * 1024)


def in_vmem(*shape):
    return pltpu.VMEM(shape, jnp.float32)


def in_hbm(value):
    return pltpu.with_memory_space_constraint(value, pltpu.HBM)


def local(psi_in, v_in, offsets):
    band_count = lax.axis_size("band")
    dom_count = lax.axis_size("dom")
    dom_idx = lax.axis_index("dom")
    slab_idx = lax.axis_index("band") % 2
    is_lower = slab_idx == 0
    slab_scalar = slab_idx.astype(jnp.int32).reshape(1)
    side = v_in.shape[1]
    pk = Packing(side)
    half = side // 2
    cells = side * side
    bands = band_count // 2
    grid_z = CORE * dom_count // 4
    lanes = 4 * grid_z
    slab_rows = CORE // 2 * 8

    f32, bf16 = jnp.float32, jnp.bfloat16
    field_type = in_vmem(*pk.shape)
    padded_field = pltpu.VMEM(pk.padded_shape, f32)

    rows = psi_in.reshape(half, 1, cells)
    rows = in_hbm(rows)
    edge = pl.pallas_call(
        functools.partial(edge_kernel, pk),
        out_shape=in_vmem(DEG, 1, cells),
        in_specs=[SMEM, HBM],
        out_specs=VMEM,
        scratch_shapes=[pltpu.SemaphoreType.DMA],
        compiler_params=params,
    )(slab_scalar, rows)
    halo = swapped(edge, "band", 1)
    masks = [dom_count // 2, 0]
    bit = dom_count // 4
    while bit:
        masks = masks + [one | bit for one in masks]
        bit //= 2
    dom_scalar = dom_idx.astype(jnp.int32).reshape(1)
    start, coef, code = pl.pallas_call(
        functools.partial(start_kernel, pk, masks),
        out_shape=(field_type, field_type, in_vmem(8, 128)),
        in_specs=[SMEM, SMEM, HBM, HBM, HBM],
        out_specs=(VMEM, VMEM, VMEM),
        scratch_shapes=[
            pltpu.VMEM((padded(pk.rows, 8), cells), f32),
            pltpu.VMEM((side * pk.pitch, 128), f32),
            pltpu.VMEM((half, 1, cells), f32),
            pltpu.VMEM((side, cells), f32),
            pltpu.SMEM((dom_count, 3), jnp.int32),
            pltpu.SemaphoreType.DMA((3,)),
        ],
        compiler_params=params,
    )(slab_scalar, dom_scalar, rows, in_hbm(v_in[0]), in_hbm(offsets))

    padded_type = in_vmem(*pk.padded_shape)
    filt, dens = pl.pallas_call(
        functools.partial(first_kernel, pk, bands),
        out_shape=(padded_type, in_vmem(slab_rows, 128)),
        in_specs=[SMEM, VMEM, VMEM, VMEM],
        out_specs=(VMEM, VMEM),
        scratch_shapes=[padded_field, padded_field, pltpu.VMEM((side * DEG, 128), f32)],
        compiler_params=params,
    )(slab_scalar, start, halo, coef)
    edge = pl.pallas_call(
        functools.partial(send_kernel, pk),
        out_shape=in_vmem(pk.edge_groups * side, 128),
        in_specs=[SMEM, VMEM],
        out_specs=VMEM,
        compiler_params=params,
    )(slab_scalar, filt)

    mask = 2
    while mask < band_count:
        dens = dens + swapped(dens, "band", mask)
        mask *= 2

    far = dom_count // 2
    both = ("dom", "band")
    count = dom_count * band_count

    def crossed(value, mask):
        return lax.ppermute(value, both, [(source, source ^ mask) for source in range(count)])

    beside_all = crossed(jnp.concatenate([dens, edge], 0), 1)
    beside = beside_all[:slab_rows]
    across = crossed(dens, far * band_count)
    diagonal = crossed(dens, far * band_count + 1)

    def cube_of(own, other):
        return jnp.concatenate([jnp.where(is_lower, own, other), jnp.where(is_lower, other, own)], 0)

    cubes = [cube_of(across, diagonal), cube_of(dens, beside)]
    bit = far // 2
    while bit > 1:
        cubes = cubes + [swapped(cube, "dom", bit) for cube in cubes]
        bit //= 2
    early = swapped(jnp.concatenate([cubes[0], dens], 0), "dom", 1)
    late = swapped(beside, "dom", 1)
    cubes_across = [early, late] + [swapped(cube, "dom", 1) for cube in cubes[2:]]

    field, mean = pl.pallas_call(
        functools.partial(take_kernel, pk),
        out_shape=(padded_type, in_vmem(8, 128)),
        in_specs=[SMEM, VMEM, VMEM, VMEM],
        out_specs=(VMEM, VMEM),
        compiler_params=params,
    )(slab_scalar, filt, beside_all, cubes[1])
    table, factor = solver_tables(side, grid_z)
    pitch = CORE + 8
    result = pl.pallas_call(
        functools.partial(second_kernel, pk, dom_count),
        out_shape=jax.ShapeDtypeStruct((half, 1, cells), f32),
        in_specs=[SMEM] + [VMEM] * (6 + dom_count),
        out_specs=VMEM,
        scratch_shapes=[
            pltpu.VMEM((dom_count, CORE * 8, 128), f32),
            padded_field,
            padded_field,
            pltpu.VMEM(pk.shape, f32),
            pltpu.VMEM((lanes // 128, CORE * pitch, 128), f32),
            pltpu.VMEM((lanes // 128, CORE * pitch, 128), f32),
            pltpu.VMEM((lanes // 128, CORE * pitch, 128), f32),
            pltpu.VMEM((pk.blocks, pk.depth * side, lanes), f32),
            pltpu.VMEM((dom_count // 4, pk.depth * side + 8, 128), f32),
            pltpu.VMEM((padded(half, 8) * side, 128), f32),
        ],
        compiler_params=params,
    )(
        slab_scalar, code, mean, field, coef, jnp.asarray(table), jnp.asarray(factor), *cubes, *cubes_across
    )
    return result.reshape(1, 1, half, cells)


def solution(mesh):
    in_specs = (P("dom", "band", None, None), P("dom", None, None), P())
    out_specs = P("dom", "band", None, None)
    return jax.shard_map(local, mesh=mesh, in_specs=in_specs, out_specs=out_specs, check_vma=False)
```

```python
import functools
import math

import jax
import jax.numpy as jnp
import ml_dtypes
import numpy as np
from jax import lax
from jax.experimental import pallas as pl
from jax.experimental.pallas import tpu as pltpu
from jax.sharding import PartitionSpec as P

CORE = 32
BUF = 4
DEG = 8

HALF_WIDTH = 4.5
FOUR_PI = 4.0 * math.pi
EXCHANGE_COEF = -((3.0 / math.pi) ** (1.0 / 3.0))


def swapped(value, axis, mask):
    pairs = [(source, source ^ mask) for source in range(lax.axis_size(axis))]
    return lax.ppermute(value, axis, pairs)


def wave_basis(length):
    cells = np.arange(length)
    rows, waves = [], []
    for wave in range(length // 2 + 1):
        angle = 2.0 * np.pi * ((wave * cells) % length) / length
        if wave in (0, length // 2):
            rows.append(np.cos(angle) / np.sqrt(length))
            waves.append(wave)
        else:
            rows.append(np.cos(angle) * np.sqrt(2.0 / length))
            rows.append(np.sin(angle) * np.sqrt(2.0 / length))
            waves += [wave, wave]
    return np.array(rows), np.array(waves)


def parity_basis():
    rows, waves = wave_basis(2 * CORE)
    return np.stack([rows[waves % 2 == 0], rows[waves % 2 == 1]]), np.stack(
        [waves[waves % 2 == 0], waves[waves % 2 == 1]]
    )


def eigenvalue(waves, length):
    return 2.0 - 2.0 * np.cos(2.0 * np.pi * waves / length)


def padded(length, unit):
    return -(-length // unit) * unit


class Packing:
    def __init__(self, side):
        self.side = side
        self.half = side // 2
        self.rows = self.half + DEG
        self.blocks = 128 // (side + 1)
        self.span = 128 // self.blocks
        self.depth = -(-self.rows // self.blocks)
        self.shape = (self.depth, side, 128)
        self.padded_shape = (self.depth, side + 16, 128)
        self.edge_groups = -(-DEG // self.blocks)
        self.pitch = padded(self.rows, 16) + 8

    def where(self, row):
        return row // self.depth, row % self.depth


def lanes_of(shape):
    return lax.broadcasted_iota(jnp.int32, shape, len(shape) - 1)


def roll(values, shift):
    return values if isinstance(shift, int) and shift % 128 == 0 else pltpu.roll(values, shift % 128, 1)


def pack(pk, flat, pitched_ref, field_ref):
    count = flat.shape[0]
    for y in range(pk.side):
        pitched_ref[y * pk.pitch : y * pk.pitch + count, 0 : pk.side] = flat[:, y * pk.side : (y + 1) * pk.side]
    for level in range(pk.depth):
        total = None
        for block in range(pk.blocks):
            row = block * pk.depth + level
            if row < pk.rows:
                part = roll(pitched_ref[pl.ds(row, pk.side, stride=pk.pitch), :], block * pk.span)
                total = part if total is None else total + part
        field_ref[level] = total


def edge_kernel(pk, slab_ref, psi_ref, edge_ref, sem):
    first = jnp.where(slab_ref[0] == 0, pk.half - DEG, 0)
    copy = pltpu.make_async_copy(psi_ref.at[pl.ds(first, DEG)], edge_ref, sem)
    copy.start()
    copy.wait()


def start_kernel(
    pk, masks, slab_ref, dom_ref, psi_in_ref, pot_in_ref, offsets_in_ref,
    field_ref, coef_ref, code_ref, flat_ref, pitched_ref, psi_ref, pot_ref, offsets_ref, sems,
):
    psi_copy = pltpu.make_async_copy(psi_in_ref, psi_ref, sems.at[2])
    copy = pltpu.make_async_copy(pot_in_ref, pot_ref, sems.at[0])
    psi_copy.start()
    offsets_copy = pltpu.make_async_copy(offsets_in_ref, offsets_ref, sems.at[1])
    copy.start()
    offsets_copy.start()
    half, side = pk.half, pk.side
    cells = side * side
    is_lower = slab_ref[0] == 0
    flat_ref[...] = jnp.zeros(flat_ref.shape, jnp.float32)
    pitched_ref[...] = jnp.zeros(pitched_ref.shape, jnp.float32)
    psi_copy.wait()
    own = psi_ref[:, 0, :]

    @pl.when(is_lower)
    def _():
        flat_ref[0:half] = own

    @pl.when(jnp.logical_not(is_lower))
    def _():
        flat_ref[DEG : DEG + half] = own

    pack(pk, flat_ref[0 : pk.rows], pitched_ref, field_ref)
    copy.wait()

    @pl.when(is_lower)
    def _():
        flat_ref[0 : pk.rows] = pot_ref[0 : pk.rows] * (2.0 / HALF_WIDTH)

    @pl.when(jnp.logical_not(is_lower))
    def _():
        flat_ref[0 : pk.rows] = pot_ref[side - pk.rows : side] * (2.0 / HALF_WIDTH)

    pack(pk, flat_ref[0 : pk.rows], pitched_ref, coef_ref)

    offsets_copy.wait()
    dom, dom_count = dom_ref[0], len(masks)
    blocks_z = dom_count // 4
    code = jnp.int32(0)
    for idx, mask in enumerate(masks):
        other = dom ^ mask
        at_x = (offsets_ref[other, 0] != offsets_ref[dom, 0]).astype(jnp.int32)
        at_y = (offsets_ref[other, 1] != offsets_ref[dom, 1]).astype(jnp.int32)
        at_z = (offsets_ref[other, 2] - offsets_ref[dom, 2]) // CORE
        at_z = jnp.where(at_z < 0, at_z + blocks_z, at_z)
        place = (at_z * 2 + at_y) * 2 + at_x
        for where in range(dom_count):
            code = code + jnp.where(place == where, idx * dom_count**where, 0)
    code_ref[...] = jnp.full(code_ref.shape, code.astype(jnp.float32))


def filtered_field(pk, start_ref, one_ref, two_ref, coef_ref):
    lane = lanes_of((8, 128))
    is_cell = (lane % pk.span < pk.side) & (lane < pk.blocks * pk.span)
    full_weight = jnp.where(is_cell, 1.0 / HALF_WIDTH, 0.0)
    part_weight = jnp.where(is_cell & (lane < (pk.blocks - 1) * pk.span), 1.0 / HALF_WIDTH, 0.0)
    after_first = lane >= pk.span
    before_last = lane < (pk.blocks - 1) * pk.span
    previous_ref, current_ref = None, start_ref
    for order in range(DEG):
        target_ref = (one_ref, two_ref)[order % 2]
        for tile in range(pk.side // 8):
            at = 8 + 8 * tile
            values = [current_ref[level, at : at + 8, :] for level in range(pk.depth)]
            before = jnp.where(after_first, roll(values[-1], pk.span), 0.0)
            after = jnp.where(before_last, roll(values[0], -pk.span), 0.0)
            around = [before] + values + [after]
            for level in range(pk.depth):
                value = values[level]
                total = around[level] + around[level + 2]
                total = total + (
                    current_ref[level, at - 1 : at + 7, :] + current_ref[level, at + 1 : at + 9, :]
                )
                total = total + (roll(value, 1) + roll(value, -1))
                weight = full_weight if (pk.blocks - 1) * pk.depth + level < pk.rows else part_weight
                following = coef_ref[level, at - 8 : at, :] * value - weight * total
                if order == 0:
                    following = 0.5 * following
                else:
                    following = following - previous_ref[level, at : at + 8, :]
                target_ref[level, at : at + 8, :] = following
        previous_ref, current_ref = current_ref, target_ref


def clear_margins(pk, ref):
    zeros = jnp.zeros((pk.depth, 8, 128), jnp.float32)
    ref[:, 0:8, :] = zeros
    ref[:, 8 + pk.side : 16 + pk.side, :] = zeros


def first_kernel(
    pk, bands, slab_ref, start_ref, halo_ref, coef_ref, filt_ref, dens_ref, field_ref, one_ref, lines_ref
):
    side, span = pk.side, pk.span
    slab = slab_ref[0]
    is_lower = slab == 0
    clear_margins(pk, field_ref)
    clear_margins(pk, one_ref)
    clear_margins(pk, filt_ref)
    field_ref[:, 8 : 8 + side, :] = start_ref[...]
    low_block, low_level = pk.where(pk.half)
    high_block, high_level = pk.where(0)
    shift = jnp.where(is_lower, low_block * span, high_block * span)
    past = lanes_of((DEG, 128)) - shift
    is_line = (past >= 0) & (past < side)
    cells = side * side
    tiles = []
    for tile in range(-(-cells // 128)):
        width = min(128, cells - tile * 128)
        part = halo_ref[:, 0, tile * 128 : tile * 128 + width]
        tiles.append(part if width == 128 else jnp.concatenate([part, jnp.zeros((DEG, 128 - width), jnp.float32)], 1))
    for y in range(side):
        tile, start = y * side // 128, y * side % 128
        line = pltpu.roll(tiles[tile], shift + (128 - start), 1)
        if start + side > 128:
            line = jnp.where(past < 128 - start, line, pltpu.roll(tiles[tile + 1], shift + (128 - start), 1))
        lines_ref[y * DEG : (y + 1) * DEG, :] = jnp.where(is_line, line, 0.0)
    for row in range(DEG):
        level = jnp.where(is_lower, low_level, high_level) + row
        line = lines_ref[pl.ds(row, side, stride=DEG), :]
        field_ref[level, 8 : 8 + side, :] = field_ref[level, 8 : 8 + side, :] + line

    filtered_field(pk, field_ref, one_ref, filt_ref, coef_ref)
    result_ref = filt_ref

    lane = lanes_of((8, 128))
    lines = 128 // CORE
    for lower, offset in ((True, BUF), (False, DEG)):

        @pl.when(is_lower == lower)
        def _(offset=offset):
            for cell in range(CORE // 2):
                block, level = pk.where(cell + offset)
                total = None
                for line in range(lines):
                    value = result_ref[level, 8 + BUF + 8 * line : 16 + BUF + 8 * line, :]
                    value = roll(value, line * CORE - BUF - block * span)
                    total = value if total is None else jnp.where(lane >= line * CORE, value, total)
                dens_ref[cell * 8 : (cell + 1) * 8] = total * total * (1.0 / bands)


def send_kernel(pk, slab_ref, result_ref, edge_ref):
    side, span = pk.side, pk.span
    is_lower = slab_ref[0] == 0
    lane = lanes_of((side, 128))
    for group in range(pk.edge_groups):
        total = jnp.zeros((side, 128), jnp.float32)
        for slot in range(min(pk.blocks, DEG - group * pk.blocks)):
            row = group * pk.blocks + slot + jnp.where(is_lower, pk.half - DEG, DEG)
            shift = slot * span - row // pk.depth * span + 128 * pk.blocks
            line = pltpu.roll(result_ref[row % pk.depth, 8 : 8 + side, :], shift % 128, 1)
            total = jnp.where((lane >= slot * span) & (lane < slot * span + side), line, total)
        edge_ref[group * side : (group + 1) * side] = total


def take_kernel(pk, slab_ref, filt_ref, beside_ref, near_ref, field_ref, mean_ref):
    mean_ref[...] = jnp.full(mean_ref.shape, jnp.mean(near_ref[...]))
    side, span, half = pk.side, pk.span, pk.half
    is_lower = slab_ref[0] == 0
    field_ref[...] = filt_ref[...]
    lane = lanes_of((side, 128))
    base = CORE // 2 * 8
    for row in range(DEG):
        group_at, slot = row // pk.blocks, row % pk.blocks
        line = beside_ref[base + group_at * side : base + (group_at + 1) * side, :]
        for wanted, (block, level) in ((True, pk.where(half + row)), (False, pk.where(row))):
            here = (lane >= block * span) & (lane < block * span + side) & (is_lower == wanted)
            old = field_ref[level, 8 : 8 + side, :]
            field_ref[level, 8 : 8 + side, :] = jnp.where(here, roll(line, (block - slot) * span), old)


def split2(values):
    high = values.astype(jnp.bfloat16)
    return high, (values - high.astype(jnp.float32)).astype(jnp.bfloat16)


def split3(values):
    high = values.astype(jnp.bfloat16)
    rest = values - high.astype(jnp.float32)
    middle = rest.astype(jnp.bfloat16)
    return high, middle, (rest - middle.astype(jnp.float32)).astype(jnp.bfloat16)


def dot(left, right):
    return jnp.dot(left, right, preferred_element_type=jnp.float32)


def table_parts(table):
    high = table.astype(ml_dtypes.bfloat16)
    return high, (table - high.astype(np.float64)).astype(ml_dtypes.bfloat16)


def left_table(table):
    high, low = table_parts(table)
    return np.concatenate([high, low, high], -1)


def stacked(values):
    high, low = split2(values)
    return jnp.concatenate([high, high, low], 0)


@functools.lru_cache(maxsize=None)
def solver_tables(side, grid_z):
    pk = Packing(side)
    blocks_z = grid_z // CORE
    lanes = 4 * grid_z
    basis, waves = parity_basis()
    z_basis, z_waves = wave_basis(grid_z)
    lines = 128 // CORE
    into = []
    for place_z in range(blocks_z):
        along_z = z_basis[:, place_z * CORE : (place_z + 1) * CORE].T
        high, low = table_parts(np.kron(np.eye(lines), along_z))
        into += [high, high, low]
    into = np.concatenate(into, 0)
    region = np.arange(side) - BUF
    outer = basis[:, :, region % (2 * CORE)]
    small = [left_table(np.concatenate([basis[0, :, :CORE], basis[1, :, :CORE]], 0))]
    small.append(left_table(np.concatenate([outer[0].T, outer[1].T], 0)))
    for first_row in (0, side - pk.rows):
        rows = outer[:, :, first_row : first_row + pk.rows]
        rows = np.pad(rows, ((0, 0), (0, 0), (0, padded(pk.rows, 8) - pk.rows)))
        small.append(left_table(np.concatenate([rows[0].T, rows[1].T], 0)))
    small = np.concatenate(small, 0)
    back_z = []
    spread = np.zeros((blocks_z, 3, 128, 128))
    for block in range(pk.blocks):
        start = block * pk.span
        table = np.zeros((4, grid_z, 128))
        table[:, :, start : start + side] = z_basis[:, region % grid_z]
        high, low = table_parts(table.reshape(lanes, 128))
        back_z.append(np.block([[high, low], [high, np.zeros_like(low)]]))
        for cell, pos in enumerate(region % grid_z):
            spread[pos // CORE, :, block * CORE + pos % CORE, start + cell] = 1.0
    back_z = np.concatenate(back_z, 0)
    spread = spread.reshape(blocks_z * 3 * 128, 128).astype(ml_dtypes.bfloat16)
    eigen = eigenvalue(waves, 2 * CORE)
    lam = (
        eigen.T[:, None, None, :, None]
        + eigen.T[None, :, :, None, None]
        + eigenvalue(z_waves, grid_z)[None, None, None, None, :]
    )
    lam[0, 0, 0, 0, 0] = np.inf
    factor = (FOUR_PI / lam).reshape(CORE * CORE, lanes).astype(np.float32)
    pieces = [back_z, np.concatenate([into, np.pad(spread, ((0, 0), (0, lanes - 128)))], 0), small]
    height = max(len(piece) for piece in pieces)
    pieces = [np.pad(piece, ((0, height - len(piece)), (0, -piece.shape[1] % 128))) for piece in pieces]
    return np.concatenate(pieces, 1), factor


def cube_root(values):
    positive = values >= np.finfo(np.float32).tiny
    safe = jnp.where(positive, values, 1.0)
    root = jnp.exp(jnp.log(safe) * (1.0 / 3.0))
    root = root - (root - safe / (root * root)) * (1.0 / 3.0)
    return jnp.where(positive, root, 0.0)


def second_kernel(
    pk, dom_count, slab_ref, code_ref, mean_ref, field_ref, start_coef_ref, table_ref, factor_ref, *refs
):
    gathered_refs, refs = refs[:dom_count], refs[dom_count:]
    (
        out_ref, cubes_ref, one_ref, two_ref, coef_ref, rows_ref, waves_ref, mixed_ref, flat_ref,
        near_dens_ref, own_ref,
    ) = refs
    side, half, span = pk.side, pk.half, pk.span
    is_lower = slab_ref[0] == 0
    blocks_z = dom_count // 4
    grid_z = CORE * blocks_z
    lanes = 4 * grid_z
    columns = lanes // 128
    lines = 128 // CORE
    pitch = CORE + 8
    kept = padded(pk.rows, 8)

    near_count = dom_count // 2
    early_ref, late_ref = gathered_refs[near_count : near_count + 2]
    whole, part = CORE * 8, CORE * 4
    for idx, ref in enumerate(gathered_refs):
        if idx not in (near_count, near_count + 1):
            cubes_ref[idx] = ref[...]
    cubes_ref[near_count] = early_ref[0:whole]
    own_part, other_part = early_ref[whole : whole + part], late_ref[...]
    cubes_ref[near_count + 1, 0:part] = jnp.where(is_lower, own_part, other_part)
    cubes_ref[near_count + 1, part:whole] = jnp.where(is_lower, other_part, own_part)
    mean = 4.0 * jnp.concatenate([mean_ref[...]] * CORE, 0)
    code = jnp.max(code_ref[...]).astype(jnp.int32)
    cube_at = [code // dom_count**where % dom_count for where in range(dom_count)]

    stacks = [[] for _ in range(4)]
    for at_z in range(blocks_z):
        near, at_x, at_y, at_xy = [cubes_ref[cube_at[at_z * 4 + place]] for place in range(4)]
        sums, others = near + at_x, at_y + at_xy
        diffs, other_diffs = near - at_x, at_y - at_xy
        parities = (sums + others - mean, sums - others, diffs + other_diffs, diffs - other_diffs)
        for parity, value in enumerate(parities):
            high, low = split2(value)
            stacks[parity] += [high, low, high]
    z_table = table_ref[0 : blocks_z * 3 * 128, 256 : 256 + lanes]
    product = jnp.concatenate([dot(jnp.concatenate(stack, 1), z_table) for stack in stacks], 0)
    lane = lanes_of((8, 128))
    for x in range(CORE):
        for line in range(lines):
            for col in range(columns):
                total = None
                for parity in range(4):
                    into = parity * grid_z - col * 128
                    if 0 <= into < 128:
                        at = line * grid_z
                        part = product[(parity * CORE + x) * 8 : (parity * CORE + x + 1) * 8, at // 128 * 128 : at // 128 * 128 + 128]
                        part = roll(part, into - at % 128)
                        total = part if total is None else jnp.where(lane >= into, part, total)
                rows_ref[col, x * pitch + line * 8 : x * pitch + line * 8 + 8, :] = total

    lane = lanes_of((8, 128))
    for at_z in range(blocks_z):
        for level in range(pk.depth):
            inner, low_wrap, high_wrap = [], None, None
            for block in range(pk.blocks):
                row = block * pk.depth + level
                if row >= pk.rows:
                    continue
                x = row - BUF + jnp.where(is_lower, 0, side - pk.rows)
                inside = (x >= 0) & (x < CORE)
                cell = pl.multiple_of((x + CORE) % CORE * 8, 8)

                def source(at_y):
                    place = (at_z * 2 + at_y) * 2
                    cube = jnp.where(inside, cube_at[place], cube_at[place + 1])
                    return cubes_ref[cube, pl.ds(cell, 8), :]

                def put(value, line, total):
                    value = roll(value, (block - line) * CORE)
                    return jnp.where((lane >= block * CORE) & (lane < (block + 1) * CORE), value, total)

                own, beside = source(0), source(1)
                zeros = jnp.zeros((8, 128), jnp.float32)
                inner = inner or [zeros] * lines
                inner = [put(own, line, total) for line, total in enumerate(inner)]
                low_wrap = put(beside, lines - 1, zeros if low_wrap is None else low_wrap)
                high_wrap = put(beside, 0, zeros if high_wrap is None else high_wrap)
            base = level * side
            near_dens_ref[at_z, base : base + BUF, :] = low_wrap[8 - BUF :]
            for line in range(lines):
                near_dens_ref[at_z, base + BUF + 8 * line : base + BUF + 8 * line + 8, :] = inner[line]
            near_dens_ref[at_z, base + BUF + CORE : base + side, :] = high_wrap[:BUF]

    group = max(1, 256 // lanes)
    lane_id = lanes_of((1, group * lanes)) % lanes
    even_x = lane_id < 2 * grid_z
    even_y = (lane_id // grid_z) % 2 == 0

    def side_by_side(ref, starts, stride, count):
        pieces = []
        for start in starts:
            for col in range(columns):
                if stride == 1:
                    pieces.append(ref[col, pl.ds(start, count), :])
                else:
                    pieces.append(ref[col, pl.ds(start, count, stride=stride), :])
        return jnp.concatenate(pieces, 1)

    def scatter(ref, starts, values, count):
        for idx, start in enumerate(starts):
            for col in range(columns):
                at = (idx * columns + col) * 128
                ref[col, start : start + count, :] = values[:, at : at + 128]

    def small(first, count):
        return table_ref[first : first + count, 256 + lanes : 256 + lanes + 3 * CORE]

    forward = small(0, 2 * CORE)
    back_y = small(2 * CORE, 2 * side)
    first = 2 * CORE + 2 * side
    back_x = jnp.where(is_lower, small(first, 2 * kept), small(first + 2 * kept, 2 * kept))
    for first in range(0, CORE, group):
        starts = [x * pitch for x in range(first, first + group)]
        both = dot(forward, stacked(side_by_side(rows_ref, starts, 1, CORE)))
        scatter(waves_ref, starts, jnp.where(even_y, both[:CORE], both[CORE:]), CORE)

    for first in range(0, CORE, group):
        waves_y = list(range(first, first + group))
        both = dot(forward, stacked(side_by_side(waves_ref, waves_y, pitch, CORE)))
        modes = jnp.where(even_x, both[:CORE], both[CORE:])
        scale = jnp.concatenate([factor_ref[wave * CORE : (wave + 1) * CORE] for wave in waves_y], 1)
        both = dot(back_x, stacked(modes * scale))
        scatter(mixed_ref, [wave * pitch for wave in waves_y], jnp.where(even_x, both[:kept], both[kept:]), kept)

    for level in range(pk.depth):
        rows = [block * pk.depth + level for block in range(pk.blocks)]
        rows = [row for row in rows if row < pk.rows]
        for first in range(0, len(rows), group):
            taken = rows[first : first + group]
            both = dot(back_y, stacked(side_by_side(mixed_ref, taken, pitch, CORE)))
            width = both.shape[1]
            field = jnp.where(even_y[:, :width], both[:side], both[side:])
            for idx in range(len(taken)):
                flat_ref[first + idx, level * side : (level + 1) * side, :] = field[:, idx * lanes : (idx + 1) * lanes]
        for block in range(len(rows), pk.blocks):
            flat_ref[block, level * side : (level + 1) * side, :] = jnp.zeros((side, lanes), jnp.float32)

    pieces = []
    for block in range(pk.blocks):
        pieces += split2(flat_ref[block])
    product = dot(jnp.concatenate(pieces, 1), table_ref[0 : pk.blocks * 2 * lanes, 0:256])
    hartree = product[:, 0:128] + product[:, 128:256]
    pieces = []
    for at_z in range(blocks_z):
        pieces += split3(near_dens_ref[at_z, 0 : pk.depth * side])
    density = dot(jnp.concatenate(pieces, 1), table_ref[blocks_z * 3 * 128 : blocks_z * 6 * 128, 256:384])
    added = (hartree + EXCHANGE_COEF * cube_root(density)) * (2.0 / HALF_WIDTH)
    for level in range(pk.depth):
        coef_ref[level] = start_coef_ref[level] + added[level * side : (level + 1) * side]

    clear_margins(pk, one_ref)
    clear_margins(pk, two_ref)
    filtered_field(pk, field_ref, one_ref, two_ref, coef_ref)

    for lower, offset in ((True, 0), (False, DEG)):

        @pl.when(is_lower == lower)
        def _(offset=offset):
            for row in range(half):
                block, level = pk.where(row + offset)
                own_ref[row * side : (row + 1) * side, :] = roll(two_ref[level, 8 : 8 + side, :], -block * span)

    cells = side * side
    parts = [roll(own_ref[pl.ds(y, half, stride=side), :], y * side) for y in range(side)]
    for tile in range(-(-cells // 128)):
        first, last = tile * 128 // side, min(side - 1, (tile * 128 + 127) // side)
        lane = lanes_of((half, 128)) + tile * 128
        total = None
        for y in range(first, last + 1):
            total = parts[y] if total is None else jnp.where(lane >= y * side, parts[y], total)
        width = min(128, cells - tile * 128)
        out_ref[:, 0, tile * 128 : tile * 128 + width] = total[:, :width]


SMEM = pl.BlockSpec(memory_space=pltpu.SMEM)
VMEM = pl.BlockSpec(memory_space=pltpu.VMEM)
HBM = pl.BlockSpec(memory_space=pltpu.HBM)
params = pltpu.CompilerParams(vmem_limit_bytes=32 * 1024 * 1024)


def in_vmem(*shape):
    return pltpu.VMEM(shape, jnp.float32)


def in_hbm(value):
    return pltpu.with_memory_space_constraint(value, pltpu.HBM)


def local(psi_in, v_in, offsets):
    band_count = lax.axis_size("band")
    dom_count = lax.axis_size("dom")
    dom_idx = lax.axis_index("dom")
    slab_idx = lax.axis_index("band") % 2
    is_lower = slab_idx == 0
    slab_scalar = slab_idx.astype(jnp.int32).reshape(1)
    side = v_in.shape[1]
    pk = Packing(side)
    half = side // 2
    cells = side * side
    bands = band_count // 2
    grid_z = CORE * dom_count // 4
    lanes = 4 * grid_z
    slab_rows = CORE // 2 * 8

    f32, bf16 = jnp.float32, jnp.bfloat16
    field_type = in_vmem(*pk.shape)
    padded_field = pltpu.VMEM(pk.padded_shape, f32)

    rows = psi_in.reshape(half, 1, cells)
    rows = in_hbm(rows)
    edge = pl.pallas_call(
        functools.partial(edge_kernel, pk),
        out_shape=in_vmem(DEG, 1, cells),
        in_specs=[SMEM, HBM],
        out_specs=VMEM,
        scratch_shapes=[pltpu.SemaphoreType.DMA],
        compiler_params=params,
    )(slab_scalar, rows)
    halo = swapped(edge, "band", 1)
    masks = [dom_count // 2, 0]
    bit = dom_count // 4
    while bit:
        masks = masks + [one | bit for one in masks]
        bit //= 2
    dom_scalar = dom_idx.astype(jnp.int32).reshape(1)
    start, coef, code = pl.pallas_call(
        functools.partial(start_kernel, pk, masks),
        out_shape=(field_type, field_type, in_vmem(8, 128)),
        in_specs=[SMEM, SMEM, HBM, HBM, HBM],
        out_specs=(VMEM, VMEM, VMEM),
        scratch_shapes=[
            pltpu.VMEM((padded(pk.rows, 8), cells), f32),
            pltpu.VMEM((side * pk.pitch, 128), f32),
            pltpu.VMEM((half, 1, cells), f32),
            pltpu.VMEM((side, cells), f32),
            pltpu.SMEM((dom_count, 3), jnp.int32),
            pltpu.SemaphoreType.DMA((3,)),
        ],
        compiler_params=params,
    )(slab_scalar, dom_scalar, rows, in_hbm(v_in[0]), in_hbm(offsets))

    padded_type = in_vmem(*pk.padded_shape)
    filt, dens = pl.pallas_call(
        functools.partial(first_kernel, pk, bands),
        out_shape=(padded_type, in_vmem(slab_rows, 128)),
        in_specs=[SMEM, VMEM, VMEM, VMEM],
        out_specs=(VMEM, VMEM),
        scratch_shapes=[padded_field, padded_field, pltpu.VMEM((side * DEG, 128), f32)],
        compiler_params=params,
    )(slab_scalar, start, halo, coef)
    edge = pl.pallas_call(
        functools.partial(send_kernel, pk),
        out_shape=in_vmem(pk.edge_groups * side, 128),
        in_specs=[SMEM, VMEM],
        out_specs=VMEM,
        compiler_params=params,
    )(slab_scalar, filt)

    mask = 2
    while mask < band_count:
        dens = dens + swapped(dens, "band", mask)
        mask *= 2

    far = dom_count // 2
    both = ("dom", "band")
    count = dom_count * band_count

    def crossed(value, mask):
        return lax.ppermute(value, both, [(source, source ^ mask) for source in range(count)])

    beside_all = crossed(jnp.concatenate([dens, edge], 0), 1)
    beside = beside_all[:slab_rows]
    across = crossed(dens, far * band_count)
    diagonal = crossed(dens, far * band_count + 1)

    def cube_of(own, other):
        return jnp.concatenate([jnp.where(is_lower, own, other), jnp.where(is_lower, other, own)], 0)

    cubes = [cube_of(across, diagonal), cube_of(dens, beside)]
    bit = far // 2
    while bit > 1:
        cubes = cubes + [swapped(cube, "dom", bit) for cube in cubes]
        bit //= 2
    early = swapped(jnp.concatenate([cubes[0], dens], 0), "dom", 1)
    late = swapped(beside, "dom", 1)
    cubes_across = [early, late] + [swapped(cube, "dom", 1) for cube in cubes[2:]]

    field, mean = pl.pallas_call(
        functools.partial(take_kernel, pk),
        out_shape=(padded_type, in_vmem(8, 128)),
        in_specs=[SMEM, VMEM, VMEM, VMEM],
        out_specs=(VMEM, VMEM),
        compiler_params=params,
    )(slab_scalar, filt, beside_all, cubes[1])
    table, factor = solver_tables(side, grid_z)
    pitch = CORE + 8
    result = pl.pallas_call(
        functools.partial(second_kernel, pk, dom_count),
        out_shape=jax.ShapeDtypeStruct((half, 1, cells), f32),
        in_specs=[SMEM] + [VMEM] * (6 + dom_count),
        out_specs=VMEM,
        scratch_shapes=[
            pltpu.VMEM((dom_count, CORE * 8, 128), f32),
            padded_field,
            padded_field,
            pltpu.VMEM(pk.shape, f32),
            pltpu.VMEM((lanes // 128, CORE * pitch, 128), f32),
            pltpu.VMEM((lanes // 128, CORE * pitch, 128), f32),
            pltpu.VMEM((lanes // 128, CORE * pitch, 128), f32),
            pltpu.VMEM((pk.blocks, pk.depth * side, lanes), f32),
            pltpu.VMEM((dom_count // 4, pk.depth * side + 8, 128), f32),
            pltpu.VMEM((padded(half, 8) * side, 128), f32),
        ],
        compiler_params=params,
    )(
        slab_scalar, code, mean, field, coef, jnp.asarray(table), jnp.asarray(factor), *cubes, *cubes_across
    )
    return result.reshape(1, 1, half, cells)


def solution(mesh):
    in_specs = (P("dom", "band", None, None), P("dom", None, None), P())
    out_specs = P("dom", "band", None, None)
    return jax.shard_map(local, mesh=mesh, in_specs=in_specs, out_specs=out_specs, check_vma=False)
```
